32 devices in a mesh: dp: 16 (over z, y, core), tp: 2 (over x).
Axes of the slice: x: 2, y: 2, z: 4, core: 2. Of those that a mesh axis runs over, the one named last changes fastest.
Arguments:
- images: bfloat16 [256, 196, 768], P('dp'), may hold values from -6 to 6
- cotangent: bfloat16 [256, 196, 768], P('dp'), may hold values from -6 to 6
- image_counts: int32 [16], P('dp'), may hold values from 1 to 16, as said below
- skip_mask: int32 [256], P('dp'), may hold values 0 or 1
- first_gain: float32 [768], replicated, may hold values from 0.1 to 1.9
- first_bias: float32 [768], replicated, may hold values from -3 to 3
- token_in: bfloat16 [196, 384], replicated, may hold values from -0.4375 to 0.4375
- token_in_bias: float32 [384], replicated, may hold values from -3 to 3
- token_out: bfloat16 [384, 196], replicated, may hold values from -0.3125 to 0.3125
- token_out_bias: float32 [196], replicated, may hold values from -3 to 3
- second_gain: float32 [768], replicated, may hold values from 0.1 to 1.9
- second_bias: float32 [768], replicated, may hold values from -3 to 3
- channel_in: bfloat16 [768, 3072], P(None, 'tp'), may hold values from -0.21875 to 0.21875
- channel_in_bias: float32 [3072], P('tp'), may hold values from -3 to 3
- channel_out: bfloat16 [3072, 768], P('tp'), may hold values from -0.109375 to 0.109375
- channel_out_bias: float32 [768], replicated, may hold values from -3 to 3
Outputs:
- activations: float32 [256, 196, 768], P('dp')
- input_grad: float32 [256, 196, 768], P('dp')
- first_gain_grad: float32 [768], replicated
- first_bias_grad: float32 [768], replicated
- token_in_grad: float32 [196, 384], replicated
- token_in_bias_grad: float32 [384], replicated
- token_out_grad: float32 [384, 196], replicated
- token_out_bias_grad: float32 [196], replicated
- second_gain_grad: float32 [768], replicated
- second_bias_grad: float32 [768], replicated
- channel_in_grad: float32 [768, 3072], P(None, 'tp')
- channel_in_bias_grad: float32 [3072], P('tp')
- channel_out_grad: float32 [3072, 768], P('tp')
- channel_out_bias_grad: float32 [768], replicated
The draws below stay inside these ranges and needn't reach their ends.
Inputs may be any that keep to these rules, and one draw needn't show every extreme that they name: `image_counts`: some index of dp has all 16 slots live and some other has exactly one.
All inputs are finite; a program needn't handle non-finite values. No bound on the sum of `skip_mask` on one device may be relied on, other than what follows from the above.
Results may differ from the reference program's by a relative error of at most 0.0065.
Values may be sent and summed in bfloat16 or wider, within the bound.
A program may use at most 256 MiB of HBM per device.

```python
import jax
import jax.numpy as jnp
from jax import lax

D = 768
PATCHES = 196
TOKEN_HIDDEN = 384
FF = 3072
IMG_DEV = 16
IMAGES = 256
N_DP = 16


def draw_image_counts(key, part):
    key = jax.random.fold_in(key, 11)
    counts = jax.random.randint(key, (N_DP,), 1, IMG_DEV + 1)
    order = jax.random.permutation(jax.random.fold_in(key, 1), N_DP)
    counts = counts.at[order[0]].set(IMG_DEV)
    counts = counts.at[order[1]].set(1)
    return counts.astype(jnp.int32)


def set_ends(array, key, low, top_value):
    place = [jax.random.randint(jax.random.fold_in(key, axis), (), 0, length) for axis, length in enumerate(array.shape)]
    widest = array.shape.index(max(array.shape))
    neighbour = place[:widest] + [(place[widest] + 1) % array.shape[widest]] + place[widest + 1:]
    return array.at[tuple(place)].set(low).at[tuple(neighbour)].set(top_value)


def steps_of(key, shape, split, least, top_value):
    def one(axis_at, blocks):
        heights = jax.random.uniform(jax.random.fold_in(jax.random.fold_in(key, 6), axis_at), (blocks,), jnp.float32, least / len(split), top_value / len(split))
        return jnp.repeat(jnp.exp(heights), shape[axis_at] // blocks).reshape((-1,) + (1,) * (len(shape) - axis_at - 1))

    loudness = one(*split[0])
    for cut in split[1:]:
        loudness = loudness * one(*cut)
    return loudness


def normal_values(own_key, dims, deviation, limit, cuts=(), held_as=jnp.bfloat16):
    array = jax.random.normal(own_key, dims, jnp.float32) * deviation
    if len(cuts) > 0:
        array = steps_of(own_key, dims, cuts, -0.22, 0.18) * array
    return jnp.clip(array, min=-limit, max=limit).astype(held_as)


def setup_inputs(seed: int = 0) -> dict:
    key_list = jax.random.split(jax.random.key(seed), 17)
    images = normal_values(key_list[0], (IMAGES, PATCHES, D), 1.0, 6.0, ((0, 16),))
    cotangent = normal_values(key_list[1], (IMAGES, PATCHES, D), 1.0, 6.0, ((0, 16),))
    image_counts = draw_image_counts(jax.random.fold_in(key_list[16], 71), 0)
    skip_mask = set_ends((jax.random.randint(key_list[3], (IMAGES,), 0, 4) < 3).astype(jnp.int32), jax.random.fold_in(key_list[3], 1), 0, 1)
    first_gain = jnp.clip(1.0 + 0.18 * jax.random.normal(key_list[4], (D,), jnp.float32), 0.1, 1.9)
    first_bias = normal_values(key_list[5], (D,), 0.5, 3.0, (), jnp.float32)
    token_in = normal_values(key_list[6], (PATCHES, TOKEN_HIDDEN), PATCHES ** -0.5, 0.4375)
    token_in_bias = normal_values(key_list[7], (TOKEN_HIDDEN,), 0.5, 3.0, (), jnp.float32)
    token_out = normal_values(key_list[8], (TOKEN_HIDDEN, PATCHES), TOKEN_HIDDEN ** -0.5, 0.3125)
    token_out_bias = normal_values(key_list[9], (PATCHES,), 0.5, 3.0, (), jnp.float32)
    second_gain = jnp.clip(1.0 + 0.18 * jax.random.normal(key_list[10], (D,), jnp.float32), 0.1, 1.9)
    second_bias = normal_values(key_list[11], (D,), 0.5, 3.0, (), jnp.float32)
    channel_in = normal_values(key_list[12], (D, FF), D ** -0.5, 0.21875, ((1, 2),))
    channel_in_bias = normal_values(key_list[13], (FF,), 0.5, 3.0, ((0, 2),), jnp.float32)
    channel_out = normal_values(key_list[14], (FF, D), FF ** -0.5, 0.109375, ((0, 2),))
    channel_out_bias = normal_values(key_list[15], (D,), 0.5, 3.0, (), jnp.float32)
    return dict(images=images, cotangent=cotangent, image_counts=image_counts, skip_mask=skip_mask, first_gain=first_gain, first_bias=first_bias, token_in=token_in, token_in_bias=token_in_bias, token_out=token_out, token_out_bias=token_out_bias, second_gain=second_gain, second_bias=second_bias, channel_in=channel_in, channel_in_bias=channel_in_bias, channel_out=channel_out, channel_out_bias=channel_out_bias)


EPSILON = 1e-06

@jax.custom_vjp
def low(v):
    return lax.optimization_barrier(v.astype(jnp.bfloat16)).astype(jnp.float32)

@jax.custom_vjp
def low_back(v):
    return v

def low_keep(v):
    return (low(v), None)

def low_pass(kept, grad):
    return (grad,)

def back_keep(v):
    return (v, None)

def back_low(kept, grad):
    return (low(grad),)
low.defvjp(low_keep, low_pass)
low_back.defvjp(back_keep, back_low)

def matmul(form, left, right):
    return jnp.einsum(form, left, right, precision=lax.Precision.HIGHEST)

def layer_norm(values, gain, shift):
    center = lax.optimization_barrier(jnp.mean(values, axis=-1, keepdims=True))
    spread = lax.optimization_barrier(jnp.mean((values - center) ** 2, axis=-1, keepdims=True))
    return (values - center) * lax.rsqrt(spread + EPSILON) * gain + shift

def reference(images, cotangent, image_counts, skip_mask, first_gain, first_bias, token_in, token_in_bias, token_out, token_out_bias, second_gain, second_bias, channel_in, channel_in_bias, channel_out, channel_out_bias):
    slots = jnp.arange(IMG_DEV, dtype=jnp.int32)
    valid = (slots[None, :] < image_counts[:, None]).astype(jnp.float32).reshape(IMAGES)[:, None, None]
    keep = skip_mask.astype(jnp.float32)[:, None, None]

    def forward(source, gain_one, shift_one, tok_first, tok_first_bias, tok_second, tok_second_bias, gain_two, shift_two, chan_first, chan_first_bias, chan_second, chan_second_bias):
        normed = low(layer_norm(source, gain_one, shift_one))
        token_pre = low_back(matmul('bpd,pt->bdt', normed, tok_first) + tok_first_bias)
        token_act = low(jax.nn.gelu(token_pre, approximate=False))
        token_branch = low_back(matmul('bdt,tp->bpd', token_act, tok_second) + tok_second_bias[:, None])
        middle = source + keep * token_branch
        second = low(layer_norm(middle, gain_two, shift_two))
        channel_pre = low_back(matmul('bpd,df->bpf', second, chan_first) + chan_first_bias)
        channel_act = low(jax.nn.gelu(channel_pre, approximate=False))
        channel_branch = low_back(matmul('bpf,fd->bpd', channel_act, chan_second) + chan_second_bias)
        return valid * (middle + keep * channel_branch)
    primals = (images.astype(jnp.float32), first_gain, first_bias, token_in.astype(jnp.float32), token_in_bias, token_out.astype(jnp.float32), token_out_bias, second_gain, second_bias, channel_in.astype(jnp.float32), channel_in_bias, channel_out.astype(jnp.float32), channel_out_bias)
    result, pullback = jax.vjp(forward, *primals)
    grads = pullback(cotangent.astype(jnp.float32))
    return (result, grads[0], grads[1], grads[2], grads[3], grads[4], grads[5], grads[6], grads[7], grads[8], grads[9], grads[10], grads[11], grads[12])
```

```python
import functools

import jax
import jax.numpy as jnp
from jax import lax
from jax.experimental import pallas as pl
from jax.experimental.pallas import tpu as pltpu
from jax.sharding import PartitionSpec as P

EPSILON = 1e-06
ROOT_HALF = 0.7071067811865476
INV_ROOT_TAU = 0.3989422804014327
F32, BF16 = jnp.float32, jnp.bfloat16
VMEM_LIMIT = 60 * 1024 * 1024

N_LIVE, N_PAIRS, CORE, LIST, VALID = 0, 1, 2, 8, 24


def dot(left, right, left_dim, right_dim):
    return lax.dot_general(
        left, right, (((left_dim,), (right_dim,)), ((), ())), preferred_element_type=F32
    )


def gelu_parts(values):
    half = 0.5 * (1.0 + lax.erf(values * ROOT_HALF))
    slope = half + values * (INV_ROOT_TAU * jnp.exp(-0.5 * values * values))
    return (values * half).astype(BF16), slope


def gelu_only(values):
    return (values * (0.5 * (1.0 + lax.erf(values * ROOT_HALF)))).astype(BF16)


def standardize(values):
    width = values.shape[-1]
    center = jnp.sum(values, axis=-1, keepdims=True) * (1.0 / width)
    deviation = values - center
    scale = lax.rsqrt(
        jnp.sum(deviation * deviation, axis=-1, keepdims=True) * (1.0 / width) + EPSILON
    )
    return deviation * scale, scale


def norm_back(grad_hat, hat, scale):
    width = hat.shape[-1]
    first = jnp.sum(grad_hat, axis=-1, keepdims=True) * (1.0 / width)
    second = jnp.sum(grad_hat * hat, axis=-1, keepdims=True) * (1.0 / width)
    return scale * (grad_hat - first - hat * second)


def pad_rows(values, rows):
    return jnp.concatenate(
        [values, jnp.zeros((rows - values.shape[0], values.shape[1]), values.dtype)], axis=0
    )


def row_sums(values):
    rows, width = values.shape
    return jnp.sum(values.reshape(rows // 8, 8, width), axis=0)


def lane_sums(values):
    total = values[:, :128]
    for at in range(128, values.shape[1], 128):
        total = total + values[:, at : at + 128]
    return total


def token_forward_kernel(
    meta, x0, x1, c0, c1, gain1, shift1, tin_t, tin_bias, tout_t, tout_bias, gain2, shift2,
    second, out_grad, middle, grad_sum,
):
    step = pl.program_id(0)

    @pl.when(step == 0)
    def _():
        grad_sum[...] = jnp.zeros_like(grad_sum)

    @pl.when(step < meta[N_PAIRS])
    def _():
        rows, patches = second.shape[1], x0.shape[1]
        for place, (x, c) in enumerate(((x0, c0), (x1, c1))):
            keep = jnp.where(2 * step + place < meta[N_LIVE], 1.0, 0.0).astype(F32)
            source = x[0].astype(F32)
            hat, _ = standardize(source)
            normed = pad_rows(hat * gain1[...] + shift1[...], rows).astype(BF16)
            pre = dot(tin_t[...], normed, 1, 0) + tin_bias[...]
            act = gelu_only(pre)
            branch = dot(tout_t[...], act, 1, 0)[:patches] + tout_bias[...]
            mid = source + keep * branch
            middle[place] = mid
            hat2, _ = standardize(mid)
            second[place] = pad_rows(hat2 * gain2[...] + shift2[...], rows).astype(BF16)
            grad = pad_rows(keep * c[0].astype(F32), rows)
            grad_sum[...] += row_sums(grad)
            out_grad[place] = grad.astype(BF16)


def hidden_kernel(
    sub, meta, second, out_grad, win, win_bias, wout,
    act_out, pre_grad_out, sent, kept, bias_grad, wout_grad, win_grad,
):
    step, steps = pl.program_id(0), pl.num_programs(0)

    @pl.when(step == 0)
    def _():
        wout_grad[...] = jnp.zeros_like(wout_grad)
        win_grad[...] = jnp.zeros_like(win_grad)
        bias_grad[...] = jnp.zeros_like(bias_grad)

    @pl.when(step < meta[N_PAIRS])
    def _():
        pair, rows, width = second.shape
        s = second[...].reshape(pair * rows, width)
        g = out_grad[...].reshape(pair * rows, width)

        def head(at):
            cut = slice(at, at + sub)
            return dot(s, win[:, cut], 1, 0) + win_bias[:, cut], dot(g, wout[cut, :], 1, 1)

        units = win.shape[1]
        ahead = head(0)
        for at in range(0, units, sub):
            pre, act_grad = ahead
            if at + sub < units:
                ahead = head(at + sub)
            act, slope = gelu_parts(pre)
            grad = act_grad * slope
            pre_grad = grad.astype(BF16)
            cut = slice(at, at + sub)
            act_out[:, :, cut] = act.reshape(pair, rows, sub)
            pre_grad_out[:, :, cut] = pre_grad.reshape(pair, rows, sub)
            bias_grad[:, cut] += row_sums(pre_grad.astype(F32))
            wout_grad[cut, :] += dot(act, g, 0, 0)
            win_grad[:, cut] += dot(s, pre_grad, 0, 0)

    @pl.when(step == steps - 1)
    def _():
        half = kept.shape[1]
        mine = pl.ds(pl.multiple_of(meta[CORE] * half, half), half)
        other = pl.ds(pl.multiple_of((1 - meta[CORE]) * half, half), half)
        kept[0] = wout_grad[mine, :].astype(BF16)
        kept[1] = win_grad[mine, :].astype(BF16)
        sent[0] = wout_grad[other, :].astype(BF16)
        sent[1] = win_grad[other, :].astype(BF16)


def mixed_kernel(
    sub, meta, second, out_grad, act0, grad0, act1, grad1, win_own, wout_own, win, win_bias, wout,
    out_part, grad_part,
):
    step = pl.program_id(0)

    @pl.when(step < meta[N_PAIRS])
    def _():
        pair, rows, width = second.shape
        flat = (pair * rows, width)
        s, g = second[...].reshape(flat), out_grad[...].reshape(flat)
        units = win.shape[1]

        def head(at):
            cut = slice(at, at + sub)
            return dot(s, win[:, cut], 1, 0) + win_bias[:, cut], dot(g, wout[cut, :], 1, 1)

        out = grad_out = None
        ahead = head(0)
        for at in range(0, units, sub):
            pre, act_grad = ahead
            if at + sub < units:
                ahead = head(at + sub)
            act, slope = gelu_parts(pre)
            pre_grad = (act_grad * slope).astype(BF16)
            cut = slice(at, at + sub)
            more, more_grad = dot(act, wout[cut, :], 1, 0), dot(pre_grad, win[:, cut], 1, 1)
            out = more if out is None else out + more
            grad_out = more_grad if grad_out is None else grad_out + more_grad
        for index, (act, pre_grad) in enumerate(((act0, grad0), (act1, grad1))):
            cut = slice(index * units, (index + 1) * units)
            out = out + dot(act[...].reshape(flat), wout_own[cut, :], 1, 0)
            grad_out = grad_out + dot(pre_grad[...].reshape(flat), win_own[:, cut], 1, 1)
        out_part[...] = out.reshape(pair, rows, width)
        grad_part[...] = grad_out.reshape(pair, rows, width)


def last_units_kernel(
    sub, meta, second, out_grad, out_part, grad_part, win, win_bias, wout, out_bias, middle, image,
    activations, second_grad, held,
):
    step = pl.program_id(0)
    live = (step // 2) < meta[N_PAIRS]
    patches = activations.shape[1]
    valid = meta[VALID + step].astype(F32)

    @pl.when(live & (step % 2 == 0))
    def _():
        pair, rows, width = second.shape
        flat = (pair * rows, width)
        s, g = second[...].reshape(flat), out_grad[...].reshape(flat)
        units = win.shape[1]

        def head(at):
            cut = slice(at, at + sub)
            return dot(s, win[:, cut], 1, 0) + win_bias[:, cut], dot(g, wout[cut, :], 1, 1)

        out = out_part[...].reshape(flat) + out_bias[...]
        grad_out = grad_part[...].reshape(flat)
        ahead = head(0)
        for at in range(0, units, sub):
            pre, act_grad = ahead
            if at + sub < units:
                ahead = head(at + sub)
            act, slope = gelu_parts(pre)
            pre_grad = (act_grad * slope).astype(BF16)
            cut = slice(at, at + sub)
            out = out + dot(act, wout[cut, :], 1, 0)
            grad_out = grad_out + dot(pre_grad, win[:, cut], 1, 1)
        second_grad[...] = grad_out.reshape(pair, rows, width)
        activations[0] = valid * (middle[0] + out[:patches])
        keep = jnp.where(step + 1 < meta[N_LIVE], 1.0, 0.0).astype(F32)
        held[...] = meta[VALID + step + 1].astype(F32) * (
            middle[1] + keep * out[rows : rows + patches]
        )

    @pl.when(live & (step % 2 == 1))
    def _():
        activations[0] = held[...]

    @pl.when(jnp.logical_not(live))
    def _():
        activations[0] = valid * image[0].astype(F32)


def token_backward_kernel(
    meta, image, cotangent, middle, second_grad, gain1, shift1, gain2, tin, tin_t, tin_bias, tout,
    input_grad, tin_grad, tin_bias_grad, tout_grad, tout_bias_grad, gains,
):
    step = pl.program_id(0)
    patches = image.shape[1]
    rows = second_grad.shape[1]
    valid = meta[VALID + step].astype(F32)

    @pl.when(step == 0)
    def _():
        for ref in (tin_grad, tin_bias_grad, tout_grad, tout_bias_grad, gains):
            ref[...] = jnp.zeros_like(ref)

    @pl.when(step < meta[N_LIVE])
    def _():
        grad2 = second_grad[0][:patches]
        hat2, scale2 = standardize(middle[0])
        gains[0] += row_sums(pad_rows(grad2 * hat2, rows))
        gains[1] += row_sums(pad_rows(grad2, rows))
        middle_grad = cotangent[0].astype(F32) + norm_back(grad2 * gain2[...], hat2, scale2)
        branch = pad_rows(middle_grad, rows)
        branch_grad = branch.astype(BF16)
        tout_bias_grad[...] += lane_sums(branch_grad.astype(F32))
        hat, scale = standardize(image[0].astype(F32))
        normed = pad_rows(hat * gain1[...] + shift1[...], rows).astype(BF16)
        pre = dot(tin_t[...], normed, 1, 0) + tin_bias[...]
        act, slope = gelu_parts(pre)
        tout_grad[...] += dot(act, branch_grad, 1, 1)
        pre_grad = (dot(tout[...], branch_grad, 1, 0) * slope).astype(BF16)
        tin_bias_grad[...] += lane_sums(pre_grad.astype(F32))
        tin_grad[...] += dot(normed, pre_grad, 1, 1)
        normed_grad = dot(tin[...], pre_grad, 1, 0)
        grad1 = normed_grad[:patches]
        gains[2] += row_sums(pad_rows(grad1 * hat, rows))
        gains[3] += row_sums(pad_rows(grad1, rows))
        input_grad[0] = middle_grad + norm_back(grad1 * gain1[...], hat, scale)

    @pl.when(step >= meta[N_LIVE])
    def _():
        input_grad[0] = valid * cotangent[0].astype(F32)


def last_pair(step, meta):
    return jnp.minimum(step, jnp.maximum(meta[N_PAIRS] - 1, 0))


def pair_spec(rows, width):
    return pl.BlockSpec((2, rows, width), lambda j, meta: (last_pair(j, meta), 0, 0))


def half_pair_spec(rows, width):
    return pl.BlockSpec((2, rows, width), lambda t, meta: (last_pair(t // 2, meta), 0, 0))


def whole_spec(array):
    zeros = (0,) * array.ndim
    return pl.BlockSpec(array.shape, lambda j, meta: zeros)


def image_spec(patches, width, place=None):
    if place is None:
        return pl.BlockSpec((1, patches, width), lambda t, meta: (meta[LIST + t], 0, 0))
    return pl.BlockSpec(
        (1, patches, width), lambda j, meta: (meta[LIST + 2 * last_pair(j, meta) + place], 0, 0)
    )


def call(body, name, grid, args, in_specs, outs, out_specs, scratch=(), flops=0, traffic=0):
    return pl.pallas_call(
        body,
        name=name,
        out_shape=outs,
        grid_spec=pltpu.PrefetchScalarGridSpec(
            num_scalar_prefetch=1,
            grid=grid,
            in_specs=in_specs,
            out_specs=out_specs,
            scratch_shapes=scratch,
        ),
        cost_estimate=pl.CostEstimate(flops=flops, bytes_accessed=traffic, transcendentals=0),
        compiler_params=pltpu.CompilerParams(
            vmem_limit_bytes=VMEM_LIMIT, dimension_semantics=("arbitrary",)
        ),
    )(*args)


def steer(image_counts, skip_mask, core):
    slots = skip_mask.shape[0]
    at = jnp.arange(slots, dtype=jnp.int32)
    valid = at < image_counts[0]
    live = valid & (skip_mask != 0)
    n_live = jnp.sum(live.astype(jnp.int32))
    earlier = (at[None, :] < at[:, None]).astype(jnp.int32)
    live_before = jnp.sum(earlier * live[None, :], axis=1)
    place = jnp.where(live, live_before, n_live + at - live_before)
    hit = (place[None, :] == at[:, None]).astype(jnp.int32)
    order = jnp.sum(hit * at[None, :], axis=1)
    order_valid = jnp.sum(hit * valid[None, :], axis=1)
    head = jnp.stack([n_live, (n_live + 1) // 2, core] + [jnp.zeros_like(core)] * (LIST - 3))
    return jnp.concatenate([head, order, order_valid]).astype(jnp.int32)


def swap(value, bit, size):
    return lax.ppermute(value, "dp", [(i, i ^ bit) for i in range(size)])


def sum_over_dp(kept, sent, size):
    me = lax.axis_index("dp")
    core, bit1, rest = me & 1, (me >> 1) & 1, me >> 2
    groups = size // 4
    total = kept.astype(F32) + swap(sent, 1, size).astype(F32)
    mine = jnp.where(bit1 == 0, total[0], total[1])
    other = jnp.where(bit1 == 0, total[1], total[0]).astype(BF16)
    total = mine + swap(other, 2, size).astype(F32)
    rows, width = total.shape
    pieces = total.astype(BF16).reshape(groups, rows // groups, width)
    if groups <= 4:
        arrived = [
            swap(lax.dynamic_index_in_dim(pieces, rest ^ k, keepdims=False), 4 * k, size)
            for k in range(1, groups)
        ]
        piece = lax.dynamic_index_in_dim(
            total.reshape(groups, rows // groups, width), rest, keepdims=False
        )
        for other in arrived:
            piece = piece + other.astype(F32)
        piece = piece.astype(BF16)
        whole = jnp.zeros((groups, rows // groups, width), BF16)
        whole = lax.dynamic_update_index_in_dim(whole, piece, rest, 0)
        for k in range(1, groups):
            whole = lax.dynamic_update_index_in_dim(whole, swap(piece, 4 * k, size), rest ^ k, 0)
    else:
        teams = [[4 * r + low for r in range(groups)] for low in range(4)]
        arrived = lax.all_to_all(pieces, "dp", 0, 0, axis_index_groups=teams)
        piece = jnp.sum(arrived.astype(F32), axis=0).astype(BF16)
        whole = lax.all_gather(piece, "dp", axis_index_groups=teams)
    part = whole.reshape(rows, width)
    far = swap(part, 2, size)
    both = jnp.where(bit1 == 0, jnp.stack([part, far]), jnp.stack([far, part]))
    far = swap(both, 1, size)
    return jnp.where(
        core == 0, jnp.concatenate([both, far], axis=1), jnp.concatenate([far, both], axis=1)
    ).astype(F32)


def shards(
    size,
    images, cotangent, image_counts, skip_mask, first_gain, first_bias, token_in, token_in_bias,
    token_out, token_out_bias, second_gain, second_bias, channel_in, channel_in_bias, channel_out,
    channel_out_bias,
):
    batch, patches, width = images.shape
    tokens = token_in.shape[1]
    own = channel_in.shape[1]
    rows = -(-patches // 16) * 16
    units = own // 2
    pairs = batch // 2
    core = lax.axis_index("dp") & 1
    meta = steer(image_counts, skip_mask, core)

    tp_swap = [(0, 1), (1, 0)]
    bias_row = channel_in_bias.reshape(1, own)
    far_bias = lax.ppermute(bias_row, "tp", tp_swap)
    far = []
    for index in range(2):
        cut = slice(index * units, (index + 1) * units)
        out_cut, in_cut = channel_out[cut, :], channel_in[:, cut]
        got = lax.ppermute(jnp.where(core == 0, out_cut, in_cut), "tp", tp_swap)
        traded = swap(got, 1, size)
        far.append((jnp.where(core == 0, traded, got), jnp.where(core == 0, got, traded)))

    pad = ((0, rows - patches), (0, 0))
    tin = jnp.pad(token_in, pad)
    tin_t, tout_t = tin.T, jnp.pad(token_out.T, pad)
    tout = tout_t.T
    tin_bias = token_in_bias.reshape(tokens, 1)
    tout_bias = token_out_bias.reshape(patches, 1)
    gain1, shift1 = first_gain.reshape(1, width), first_bias.reshape(1, width)
    gain2, shift2 = second_gain.reshape(1, width), second_bias.reshape(1, width)
    out_bias = channel_out_bias.reshape(1, width)

    shape = jax.ShapeDtypeStruct
    pair = pair_spec(rows, width)
    packed = (batch, rows, width)
    block = patches * width
    acc = pl.BlockSpec((8, width), lambda j, meta: (0, 0))

    consts = (gain1, shift1, tin_t, tin_bias, tout_t, tout_bias, gain2, shift2)
    second, out_grad, middle, out_bias_grad = call(
        token_forward_kernel, "token_forward", (pairs,),
        (meta, images, images, cotangent, cotangent, *consts),
        [image_spec(patches, width, p) for p in (0, 1, 0, 1)] + [whole_spec(c) for c in consts],
        [shape(packed, BF16), shape(packed, BF16), shape((batch, patches, width), F32), shape((8, width), F32)],
        [pair, pair, pair_spec(patches, width), acc],
        flops=4 * batch * rows * width * tokens * 4, traffic=batch * block * 12,
    )

    hidden = []
    for index in range(2):
        cut = (index,)
        hidden.append(call(
            functools.partial(hidden_kernel, 256), "hidden_own", (pairs,),
            (meta, second, out_grad, channel_in, bias_row, channel_out),
            [
                pair, pair,
                pl.BlockSpec((width, units), lambda j, meta, index=index: (0, index)),
                pl.BlockSpec((1, units), lambda j, meta, index=index: (0, index)),
                pl.BlockSpec((units, width), lambda j, meta, index=index: (index, 0)),
            ],
            [shape((batch, rows, units), BF16)] * 2 + [shape((2, width // 2, width), BF16)] * 2 + [shape((8, units), F32)],
            [pair_spec(rows, units)] * 2
            + [pl.BlockSpec((2, width // 2, width), lambda j, meta: (0, 0, 0))] * 2
            + [pl.BlockSpec((8, units), lambda j, meta: (0, 0))],
            [pltpu.VMEM((units, width), F32), pltpu.VMEM((width, units), F32)],
            flops=8 * batch * rows * width * units, traffic=batch * block * 8,
        ))
    summed = [sum_over_dp(h[3], h[2], size) for h in hidden]

    mats = (channel_in, channel_out, far[0][0], far_bias[:, :units], far[0][1])
    out_part, grad_part = call(
        functools.partial(mixed_kernel, 256), "hidden_far_0", (pairs,),
        (meta, second, out_grad, hidden[0][0], hidden[0][1], hidden[1][0], hidden[1][1], *mats),
        [pair] * 2 + [pair_spec(rows, units)] * 4 + [whole_spec(m) for m in mats],
        [shape(packed, F32)] * 2, [pair] * 2,
        flops=16 * batch * rows * width * units, traffic=batch * block * 20,
    )
    half_pair = half_pair_spec(rows, width)
    mats = (far[1][0], far_bias[:, units:], far[1][1], out_bias)
    activations, second_grad = call(
        functools.partial(last_units_kernel, 256), "hidden_far_1", (batch,),
        (meta, second, out_grad, out_part, grad_part, *mats, middle, images),
        [half_pair] * 4 + [whole_spec(m) for m in mats]
        + [half_pair_spec(patches, width), image_spec(patches, width)],
        [shape((batch, patches, width), F32), shape(packed, F32)],
        [image_spec(patches, width), half_pair],
        [pltpu.VMEM((patches, width), F32)],
        flops=8 * batch * rows * width * units, traffic=batch * block * 20,
    )

    consts = (gain1, shift1, gain2, tin, tin_t, tin_bias, tout)
    one = lambda r: pl.BlockSpec((1, r, width), lambda t, meta: (jnp.minimum(t, jnp.maximum(meta[N_LIVE] - 1, 0)), 0, 0))
    smalls = [shape((rows, tokens), F32), shape((tokens, 128), F32), shape((tokens, rows), F32), shape((rows, 128), F32), shape((4, 8, width), F32)]
    input_grad, tin_grad, tin_bias_grad, tout_grad, tout_bias_grad, gains = call(
        token_backward_kernel, "token_backward", (batch,),
        (meta, images, cotangent, middle, second_grad, *consts),
        [image_spec(patches, width)] * 2 + [one(patches), one(rows)] + [whole_spec(c) for c in consts],
        [shape((batch, patches, width), F32)] + smalls,
        [image_spec(patches, width)] + [whole_spec(s) if len(s.shape) else None for s in smalls],
        flops=10 * batch * rows * width * tokens, traffic=batch * block * 16,
    )
    gains = jnp.sum(gains, axis=1)
    small = lax.psum(
        (
            gains[2], gains[3], tin_grad[:patches], jnp.sum(tin_bias_grad, axis=1),
            tout_grad[:, :patches], jnp.sum(tout_bias_grad, axis=1)[:patches], gains[0], gains[1],
            jnp.concatenate([jnp.sum(h[4], axis=0) for h in hidden]), jnp.sum(out_bias_grad, axis=0),
        ),
        "dp",
    )
    out_grad_sum = jnp.concatenate([s[0] for s in summed], axis=0)
    in_grad_sum = jnp.concatenate([s[1] for s in summed], axis=1)
    return (activations, input_grad, *small[:8], in_grad_sum, small[8], out_grad_sum, small[9])


def solution(mesh):
    placed = (
        P("dp", None, None), P("dp", None, None), P("dp"), P("dp"), P(), P(), P(), P(), P(), P(), P(), P(),
        P(None, "tp"), P("tp"), P("tp", None), P(),
    )
    return jax.shard_map(
        functools.partial(shards, mesh.shape["dp"]),
        mesh=mesh,
        in_specs=placed,
        out_specs=(
            P("dp", None, None), P("dp", None, None), P(), P(), P(), P(), P(), P(), P(), P(),
            P(None, "tp"), P("tp"), P("tp", None), P(),
        ),
        check_vma=False,
    )
```

```python
import functools

import jax
import jax.numpy as jnp
from jax import lax
from jax.experimental import pallas as pl
from jax.experimental.pallas import tpu as pltpu
from jax.sharding import PartitionSpec as P

EPSILON = 1e-06
ROOT_HALF = 0.7071067811865476
INV_ROOT_TAU = 0.3989422804014327
F32, BF16 = jnp.float32, jnp.bfloat16
VMEM_LIMIT = 60 * 1024 * 1024
CHANNEL_VMEM = 62 * 1024 * 1024
RING, SEG, LAST_TURN = 8, 48, 9
FAST_PAIRS = (6,)

N_LIVE, N_PAIRS, CORE, LIST, VALID = 0, 1, 2, 8, 24


def dot(left, right, left_dim, right_dim):
    return lax.dot_general(
        left, right, (((left_dim,), (right_dim,)), ((), ())), preferred_element_type=F32
    )


def gelu_parts(values):
    half = 0.5 * (1.0 + lax.erf(values * ROOT_HALF))
    slope = half + values * (INV_ROOT_TAU * jnp.exp(-0.5 * values * values))
    return (values * half).astype(BF16), slope


def gelu_only(values):
    return (values * (0.5 * (1.0 + lax.erf(values * ROOT_HALF)))).astype(BF16)


def standardize(values):
    width = values.shape[-1]
    center = jnp.sum(values, axis=-1, keepdims=True) * (1.0 / width)
    deviation = values - center
    scale = lax.rsqrt(
        jnp.sum(deviation * deviation, axis=-1, keepdims=True) * (1.0 / width) + EPSILON
    )
    return deviation * scale, scale


def norm_back(grad_hat, hat, scale):
    width = hat.shape[-1]
    first = jnp.sum(grad_hat, axis=-1, keepdims=True) * (1.0 / width)
    second = jnp.sum(grad_hat * hat, axis=-1, keepdims=True) * (1.0 / width)
    return scale * (grad_hat - first - hat * second)


def pad_rows(values, rows):
    return jnp.concatenate(
        [values, jnp.zeros((rows - values.shape[0], values.shape[1]), values.dtype)], axis=0
    )


def row_sums(values):
    rows, width = values.shape
    return jnp.sum(values.reshape(rows // 8, 8, width), axis=0)


def lane_sums(values):
    total = values[:, :128]
    for at in range(128, values.shape[1], 128):
        total = total + values[:, at : at + 128]
    return total


def token_forward_kernel(
    meta, x0, x1, c0, c1, gain1, shift1, tin_t, tin_bias, tout_t, tout_bias, gain2, shift2,
    second, out_grad, middle, grad_sum,
):
    step = pl.program_id(0)

    @pl.when(step == 0)
    def _():
        grad_sum[...] = jnp.zeros_like(grad_sum)

    @pl.when(step < meta[N_PAIRS])
    def _():
        rows, patches = second.shape[1], x0.shape[1]
        for place, (x, c) in enumerate(((x0, c0), (x1, c1))):
            keep = jnp.where(2 * step + place < meta[N_LIVE], 1.0, 0.0).astype(F32)
            source = x[0].astype(F32)
            hat, _ = standardize(source)
            normed = pad_rows(hat * gain1[...] + shift1[...], rows).astype(BF16)
            pre = dot(tin_t[...], normed, 1, 0) + tin_bias[...]
            act = gelu_only(pre)
            branch = dot(tout_t[...], act, 1, 0)[:patches] + tout_bias[...]
            mid = source + keep * branch
            middle[place] = mid
            hat2, _ = standardize(mid)
            second[place] = pad_rows(hat2 * gain2[...] + shift2[...], rows).astype(BF16)
            grad = pad_rows(keep * c[0].astype(F32), rows)
            grad_sum[...] += row_sums(grad)
            out_grad[place] = grad.astype(BF16)

    @pl.when(step >= meta[N_PAIRS])
    def _():
        second[...] = jnp.zeros_like(second)
        out_grad[...] = jnp.zeros_like(out_grad)


def hidden_kernel(
    sub, meta, second, out_grad, win, win_bias, wout,
    act_out, pre_grad_out, sent, kept, bias_grad, wout_grad, win_grad,
):
    step, steps = pl.program_id(0), pl.num_programs(0)

    @pl.when(step == 0)
    def _():
        wout_grad[...] = jnp.zeros_like(wout_grad)
        win_grad[...] = jnp.zeros_like(win_grad)
        bias_grad[...] = jnp.zeros_like(bias_grad)

    @pl.when(step < meta[N_PAIRS])
    def _():
        pair, rows, width = second.shape
        s = second[...].reshape(pair * rows, width)
        g = out_grad[...].reshape(pair * rows, width)

        def head(at):
            cut = slice(at, at + sub)
            return dot(s, win[:, cut], 1, 0) + win_bias[:, cut], dot(g, wout[cut, :], 1, 1)

        units = win.shape[1]
        ahead = head(0)
        for at in range(0, units, sub):
            pre, act_grad = ahead
            if at + sub < units:
                ahead = head(at + sub)
            act, slope = gelu_parts(pre)
            grad = act_grad * slope
            pre_grad = grad.astype(BF16)
            cut = slice(at, at + sub)
            act_out[:, :, cut] = act.reshape(pair, rows, sub)
            pre_grad_out[:, :, cut] = pre_grad.reshape(pair, rows, sub)
            bias_grad[:, cut] += row_sums(pre_grad.astype(F32))
            wout_grad[cut, :] += dot(act, g, 0, 0)
            win_grad[:, cut] += dot(s, pre_grad, 0, 0)

    @pl.when(step == steps - 1)
    def _():
        half = kept.shape[1]
        mine = pl.ds(pl.multiple_of(meta[CORE] * half, half), half)
        other = pl.ds(pl.multiple_of((1 - meta[CORE]) * half, half), half)
        kept[0] = wout_grad[mine, :].astype(BF16)
        kept[1] = win_grad[mine, :].astype(BF16)
        sent[0] = wout_grad[other, :].astype(BF16)
        sent[1] = win_grad[other, :].astype(BF16)


def far_units(sub, s, g, win, win_bias, wout, out, grad_out):
    def head(at):
        cut = slice(at, at + sub)
        return dot(s, win[:, cut], 1, 0) + win_bias[:, cut], dot(g, wout[cut, :], 1, 1)

    units = win.shape[1]
    ahead = head(0)
    for at in range(0, units, sub):
        pre, act_grad = ahead
        if at + sub < units:
            ahead = head(at + sub)
        act, slope = gelu_parts(pre)
        pre_grad = (act_grad * slope).astype(BF16)
        cut = slice(at, at + sub)
        more, more_grad = dot(act, wout[cut, :], 1, 0), dot(pre_grad, win[:, cut], 1, 1)
        out = more if out is None else out + more
        grad_out = more_grad if grad_out is None else grad_out + more_grad
    return out, grad_out


def far_first_kernel(
    sub, meta, second, out_grad, act0, grad0, act1, grad1, win_own, wout_own, win, win_bias, wout,
    out_part, grad_part,
):
    step = pl.program_id(0)

    @pl.when(step < meta[N_PAIRS])
    def _():
        pair, rows, width = second.shape
        flat = (pair * rows, width)
        s, g = second[...].reshape(flat), out_grad[...].reshape(flat)
        units = win.shape[1]
        out, grad_out = far_units(sub, s, g, win, win_bias, wout, None, None)
        for index, (act, pre_grad) in enumerate(((act0, grad0), (act1, grad1))):
            cut = slice(index * units, (index + 1) * units)
            out = out + dot(act[...].reshape(flat), wout_own[cut, :], 1, 0)
            grad_out = grad_out + dot(pre_grad[...].reshape(flat), win_own[:, cut], 1, 1)
        out_part[...] = out.reshape(pair, rows, width)
        grad_part[...] = grad_out.reshape(pair, rows, width)


def far_last_kernel(
    sub, meta, second, out_grad, out_part, grad_part, win, win_bias, wout, branch, second_grad,
):
    step = pl.program_id(0)

    @pl.when(step < meta[N_PAIRS])
    def _():
        pair, rows, width = second.shape
        flat = (pair * rows, width)
        s, g = second[...].reshape(flat), out_grad[...].reshape(flat)
        out, grad_out = far_units(
            sub, s, g, win, win_bias, wout, out_part[...].reshape(flat), grad_part[...].reshape(flat)
        )
        branch[...] = out.reshape(pair, rows, width)
        second_grad[...] = grad_out.reshape(pair, rows, width)


def token_backward_kernel(
    meta, image, cotangent, middle, branch, second_grad, dw_in0, dw_in1, dw_out, out_bias, gain1, shift1,
    gain2, tin, tin_t, tin_bias, tout,
    activations, input_grad, win_grad, wout_grad, tin_grad, tin_bias_grad, tout_grad, tout_bias_grad, gains,
):
    step = pl.program_id(0)
    patches = image.shape[1]
    rows = second_grad.shape[1]
    valid = meta[VALID + step].astype(F32)

    @pl.when(step == 0)
    def _():
        for ref in (tin_grad, tin_bias_grad, tout_grad, tout_bias_grad, gains):
            ref[...] = jnp.zeros_like(ref)

    units = dw_in0.shape[-1]
    win_grad[:, :units] = dw_in0[...].reshape(win_grad.shape[0], units).astype(F32)
    win_grad[:, units:] = dw_in1[...].reshape(win_grad.shape[0], units).astype(F32)
    wout_grad[...] = dw_out[...].reshape(wout_grad.shape).astype(F32)

    @pl.when(step < meta[N_LIVE])
    def _():
        activations[0] = middle[0] + (branch[0][:patches] + out_bias[...])
        grad2 = second_grad[0][:patches]
        hat2, scale2 = standardize(middle[0])
        gains[0] += row_sums(pad_rows(grad2 * hat2, rows))
        gains[1] += row_sums(pad_rows(grad2, rows))
        middle_grad = cotangent[0].astype(F32) + norm_back(grad2 * gain2[...], hat2, scale2)
        branch_grad = pad_rows(middle_grad, rows).astype(BF16)
        tout_bias_grad[...] += lane_sums(branch_grad.astype(F32))
        hat, scale = standardize(image[0].astype(F32))
        normed = pad_rows(hat * gain1[...] + shift1[...], rows).astype(BF16)
        pre = dot(tin_t[...], normed, 1, 0) + tin_bias[...]
        act, slope = gelu_parts(pre)
        tout_grad[...] += dot(act, branch_grad, 1, 1)
        pre_grad = (dot(tout[...], branch_grad, 1, 0) * slope).astype(BF16)
        tin_bias_grad[...] += lane_sums(pre_grad.astype(F32))
        tin_grad[...] += dot(normed, pre_grad, 1, 1)
        normed_grad = dot(tin[...], pre_grad, 1, 0)
        grad1 = normed_grad[:patches]
        gains[2] += row_sums(pad_rows(grad1 * hat, rows))
        gains[3] += row_sums(pad_rows(grad1, rows))
        input_grad[0] = middle_grad + norm_back(grad1 * gain1[...], hat, scale)

    @pl.when(step >= meta[N_LIVE])
    def _():
        activations[0] = valid * image[0].astype(F32)
        input_grad[0] = valid * cotangent[0].astype(F32)


def last_pair(step, meta):
    return jnp.minimum(step, jnp.maximum(meta[N_PAIRS] - 1, 0))


def pair_spec(rows, width):
    return pl.BlockSpec((2, rows, width), lambda j, meta: (last_pair(j, meta), 0, 0))


def half_pair_spec(rows, width):
    return pl.BlockSpec((2, rows, width), lambda t, meta: (last_pair(t // 2, meta), 0, 0))


def whole_spec(array):
    zeros = (0,) * array.ndim
    return pl.BlockSpec(array.shape, lambda j, meta: zeros)


def image_spec(patches, width, place=None):
    if place is None:
        return pl.BlockSpec((1, patches, width), lambda t, meta: (meta[LIST + t], 0, 0))
    return pl.BlockSpec(
        (1, patches, width), lambda j, meta: (meta[LIST + 2 * last_pair(j, meta) + place], 0, 0)
    )


def call(body, name, grid, args, in_specs, outs, out_specs, scratch=(), flops=0, traffic=0):
    return pl.pallas_call(
        body,
        name=name,
        out_shape=outs,
        grid_spec=pltpu.PrefetchScalarGridSpec(
            num_scalar_prefetch=1,
            grid=grid,
            in_specs=in_specs,
            out_specs=out_specs,
            scratch_shapes=scratch,
        ),
        cost_estimate=pl.CostEstimate(flops=flops, bytes_accessed=traffic, transcendentals=0),
        compiler_params=pltpu.CompilerParams(
            vmem_limit_bytes=VMEM_LIMIT, dimension_semantics=("arbitrary",)
        ),
    )(*args)


def steer(image_counts, skip_mask, core):
    slots = skip_mask.shape[0]
    at = jnp.arange(slots, dtype=jnp.int32)
    valid = at < image_counts[0]
    live = valid & (skip_mask != 0)
    n_live = jnp.sum(live.astype(jnp.int32))
    earlier = (at[None, :] < at[:, None]).astype(jnp.int32)
    live_before = jnp.sum(earlier * live[None, :], axis=1)
    place = jnp.where(live, live_before, n_live + at - live_before)
    hit = (place[None, :] == at[:, None]).astype(jnp.int32)
    order = jnp.sum(hit * at[None, :], axis=1)
    order_valid = jnp.sum(hit * valid[None, :], axis=1)
    head = jnp.stack([n_live, (n_live + 1) // 2, core] + [jnp.zeros_like(core)] * (LIST - 3))
    return jnp.concatenate([head, order, order_valid]).astype(jnp.int32)


def swap(value, bit, size):
    return lax.ppermute(value, "dp", [(i, i ^ bit) for i in range(size)])


def sum_over_dp(kept, sent, size):
    me = lax.axis_index("dp")
    core, bit1, rest = me & 1, (me >> 1) & 1, me >> 2
    groups = size // 4
    total = kept.astype(F32) + swap(sent, 1, size).astype(F32)
    mine = jnp.where(bit1 == 0, total[0], total[1])
    other = jnp.where(bit1 == 0, total[1], total[0]).astype(BF16)
    total = mine + swap(other, 2, size).astype(F32)
    rows, width = total.shape
    pieces = total.astype(BF16).reshape(groups, rows // groups, width)
    if groups <= 4:
        arrived = [
            swap(lax.dynamic_index_in_dim(pieces, rest ^ k, keepdims=False), 4 * k, size)
            for k in range(1, groups)
        ]
        piece = lax.dynamic_index_in_dim(
            total.reshape(groups, rows // groups, width), rest, keepdims=False
        )
        for other in arrived:
            piece = piece + other.astype(F32)
        piece = piece.astype(BF16)
        whole = jnp.zeros((groups, rows // groups, width), BF16)
        whole = lax.dynamic_update_index_in_dim(whole, piece, rest, 0)
        for k in range(1, groups):
            whole = lax.dynamic_update_index_in_dim(whole, swap(piece, 4 * k, size), rest ^ k, 0)
    else:
        teams = [[4 * r + low for r in range(groups)] for low in range(4)]
        arrived = lax.all_to_all(pieces, "dp", 0, 0, axis_index_groups=teams)
        piece = jnp.sum(arrived.astype(F32), axis=0).astype(BF16)
        whole = lax.all_gather(piece, "dp", axis_index_groups=teams)
    part = whole.reshape(rows, width)
    far = swap(part, 2, size)
    both = jnp.where(bit1 == 0, jnp.stack([part, far]), jnp.stack([far, part]))
    far = swap(both, 1, size)
    return jnp.where(core == 0, jnp.stack([both, far]), jnp.stack([far, both]))


def channel_kernel(
    sub, second_hbm, grad_hbm, win_hbm, wout_hbm, bias,
    branch_hbm, second_grad_hbm, dw_hbm, bias_grad,
    s_all, g_all, acts, grads, w_own, w_far, bias_far, dw, traded, starts, hops, out_acc, grad_acc,
    load_sem, out_sem, bias_sem, far_sem, core_sem, result_sem, ring_send, ring_recv, free_sem,
):
    pairs, _, rows, width = s_all.shape
    units = width
    half = units // 2
    flat = (2 * rows, width)
    me = lax.axis_index("dp")
    core, y, z = lax.rem(me, 2), lax.rem(lax.div(me, 2), 2), lax.div(me, 4)
    tp = lax.axis_index("tp")
    at = y * 4 + z + y * (3 - 2 * z)

    def device_at(place):
        place = lax.rem(place + RING, RING)
        row = lax.div(place, 4)
        col = lax.rem(place, 4)
        return (col + row * (3 - 2 * col)) * 4 + row * 2 + core

    sibling = me + 1 - 2 * core
    ways = (device_at(at + 1), device_at(at - 1))

    barrier = pltpu.get_barrier_semaphore()
    for near in ({"dp": sibling}, {"dp": ways[0]}, {"dp": ways[1]}, {"tp": 1 - tp}):
        pl.semaphore_signal(barrier, inc=1, device_id=near, device_id_type=pl.DeviceIdType.MESH)
    pl.semaphore_wait(barrier, 4)

    def remote(src, dst, sems, recv, device):
        return pltpu.make_async_remote_copy(
            src_ref=src, dst_ref=dst, send_sem=sems, recv_sem=recv, device_id=device,
            device_id_type=pl.DeviceIdType.MESH,
        )

    loads = []
    for chunk in range(2):
        cut = pl.ds(chunk * units, units)
        loads.append(pltpu.make_async_copy(wout_hbm.at[cut, :], w_own.at[0, chunk], load_sem.at[chunk, 0]))
        loads.append(pltpu.make_async_copy(win_hbm.at[:, cut], w_own.at[1, chunk], load_sem.at[chunk, 1]))
    loads.append(pltpu.make_async_copy(second_hbm.at[pl.ds(0, pairs)], s_all, load_sem.at[2, 0]))
    loads.append(pltpu.make_async_copy(grad_hbm.at[pl.ds(0, pairs)], g_all, load_sem.at[2, 1]))
    for load in (loads[0], loads[1], loads[4], loads[5], loads[2], loads[3]):
        load.start()

    def far_copy(chunk):
        return remote(w_own.at[core, chunk], w_far.at[core, chunk], far_sem.at[0, chunk], far_sem.at[1, chunk], {"tp": 1 - tp})

    def pass_copy(chunk):
        return remote(w_far.at[core, chunk], w_far.at[core, chunk], far_sem.at[2, chunk], far_sem.at[3, chunk], {"dp": sibling})

    bias_copy = remote(bias, bias_far, bias_sem.at[0], bias_sem.at[1], {"tp": 1 - tp})
    bias_copy.start()
    loads[0].wait()
    loads[1].wait()
    far_copy(0).start()
    bias_grad[...] = jnp.zeros_like(bias_grad)
    loads[4].wait()
    loads[5].wait()

    def reach(matrix, way):
        return 4 if matrix == way else 3

    def segment(block, index):
        chunk, matrix = block
        index = lax.rem(index + 2 * RING, RING)
        return dw.at[chunk, core, pl.ds(pl.multiple_of(matrix * half + index * SEG, SEG), SEG)]

    def sign(way):
        return 1 - 2 * way

    def part_of(ref, block, which):
        chunk, matrix = block
        return ref.at[chunk, which, pl.ds(matrix * half, half)]

    def landing(block):
        chunk, matrix = block
        return traded.at[chunk, pl.ds(matrix * half, half)]

    def core_copy(block):
        return remote(part_of(dw, block, 1 - core), landing(block), core_sem.at[(0, *block)], core_sem.at[(1, *block)], {"dp": sibling})

    def back_copy(block):
        return remote(part_of(dw, block, core), landing(block), core_sem.at[(2, *block)], core_sem.at[(3, *block)], {"dp": sibling})

    def result_copies(block):
        return (
            pltpu.make_async_copy(part_of(dw, block, core), part_of(dw_hbm, block, core), result_sem.at[(0, *block)]),
            pltpu.make_async_copy(landing(block), part_of(dw_hbm, block, 1 - core), result_sem.at[(1, *block)]),
        )

    def hop_copy(block, way, hop, src):
        slot = way * 4 + hop - 1
        return remote(
            src, hops.at[(*block, slot)], ring_send.at[(*block, slot)], ring_recv.at[(*block, slot)], {"dp": ways[way]}
        )

    def hop_arrived(block, way, hop):
        slot = hops.at[(*block, way * 4 + hop - 1)]
        hop_copy(block, way, hop, slot).wait_recv()
        return slot

    def spread_copy(block, way, hop, index):
        slot = 8 + way * 4 + hop - 1
        place = segment(block, index)
        return remote(place, place, ring_send.at[(*block, slot)], ring_recv.at[(*block, slot)], {"dp": ways[way]})

    def service(block, turn):
        @pl.when(turn == 0)
        def _():
            core_copy(block).wait()
            mine = part_of(dw, block, core)
            mine[...] = (mine[...].astype(F32) + landing(block)[...].astype(F32)).astype(BF16)
            pl.semaphore_signal(free_sem.at[block], inc=1, device_id={"dp": sibling}, device_id_type=pl.DeviceIdType.MESH)
            for way in range(2):
                begin = starts.at[(*block, way)]
                begin[...] = segment(block, at + sign(way) * reach(block[1], way))[...]
                hop_copy(block, way, 1, begin).start()

        for hop in range(2, 5):

            @pl.when(turn == hop - 1)
            def _():
                for way in range(2):
                    if hop <= reach(block[1], way):
                        slot = hop_arrived(block, way, hop - 1)
                        own = segment(block, at + sign(way) * (reach(block[1], way) - hop + 1))
                        slot[...] = (slot[...].astype(F32) + own[...].astype(F32)).astype(BF16)
                        hop_copy(block, way, hop, slot).start()

        @pl.when(turn == 4)
        def _():
            own = segment(block, at)
            total = own[...].astype(F32)
            for way in range(2):
                total = total + hop_arrived(block, way, reach(block[1], way))[...].astype(F32)
            own[...] = total.astype(BF16)
            for way in range(2):
                spread_copy(block, way, 1, at).start()

        for hop in range(2, 5):

            @pl.when(turn == hop + 3)
            def _():
                for way in range(2):
                    if hop <= reach(block[1], way):
                        spread_copy(block, way, hop - 1, at - sign(way) * (hop - 1)).wait_recv()
                        spread_copy(block, way, hop, at - sign(way) * (hop - 1)).start()

        @pl.when(turn == 8)
        def _():
            for way in range(2):
                last = reach(block[1], way)
                spread_copy(block, way, last, at - sign(way) * last).wait_recv()
            pl.semaphore_wait(free_sem.at[block], 1)
            back_copy(block).start()

        @pl.when(turn == LAST_TURN)
        def _():
            back_copy(block).wait_recv()
            for result in result_copies(block):
                result.start()

    def service_end(block):
        back_copy(block).wait_send()
        for result in result_copies(block):
            result.wait()
        for way in range(2):
            for hop in range(1, reach(block[1], way) + 1):
                hop_copy(block, way, hop, hops.at[(*block, way * 4 + hop - 1)]).wait_send()
                spread_copy(block, way, hop, at).wait_send()

    def rows_of(ref, pair):
        return ref[pair].reshape(flat)

    def own_units(chunk, pair):
        s, g = rows_of(s_all, pair), rows_of(g_all, pair)

        def head(start):
            cut = slice(start, start + sub)
            place = slice(chunk * units + start, chunk * units + start + sub)
            return (
                dot(s, w_own[1, chunk, :, cut], 1, 0) + bias[:, place],
                dot(g, w_own[0, chunk, cut, :], 1, 1),
            )

        ahead = head(0)
        for start in range(0, units, sub):
            pre, act_grad = ahead
            if start + sub < units:
                ahead = head(start + sub)
            act, slope = gelu_parts(pre)
            pre_grad = (act_grad * slope).astype(BF16)
            cut = slice(start, start + sub)
            place = slice(chunk * units + start, chunk * units + start + sub)
            acts[chunk, pair, :, :, cut] = act.reshape(2, rows, sub)
            grads[chunk, pair, :, :, cut] = pre_grad.reshape(2, rows, sub)
            bias_grad[:, place] += row_sums(pre_grad.astype(F32))

    def weight_grads(chunk, matrix, part):
        depth = pairs * 2 * rows
        cut = slice(part * half, (part + 1) * half)
        if matrix == 0:
            left, right = acts[chunk, :, :, :, cut], g_all[...]
        else:
            left, right = s_all[:, :, :, cut], grads[chunk]
        grad = dot(left.reshape(depth, half), right.reshape(depth, width), 0, 0)
        dw[chunk, part, matrix * half : (matrix + 1) * half] = grad.astype(BF16)

    first = [(0, 0), (0, 1)]
    second = [(1, 0), (1, 1)]
    done = {block: -1 for block in first + second}

    def serve(*blocks):
        for block in blocks:
            done[block] += 1
            if done[block] <= LAST_TURN:
                service(block, done[block])

    @pl.loop(0, pairs)
    def _(pair):
        own_units(0, pair)

    for matrix in range(2):
        weight_grads(0, matrix, 0)
        weight_grads(0, matrix, 1)
        core_copy((0, matrix)).start()
    serve((0, 0))
    loads[2].wait()
    loads[3].wait()

    base = dict(done)

    @pl.loop(0, pairs)
    def _(pair):
        own_units(1, pair)

        @pl.when(lax.rem(pair, 2) == 1)
        def _():
            for block in first:
                service(block, base[block] + 1 + lax.div(pair, 2))

    for block in first:
        done[block] += pairs // 2
    weight_grads(1, 0, 0)
    weight_grads(1, 0, 1)
    core_copy((1, 0)).start()
    serve(*first)
    weight_grads(1, 1, 0)
    weight_grads(1, 1, 1)
    core_copy((1, 1)).start()
    serve((1, 0), *first)
    far_copy(0).wait_recv()
    pass_copy(0).start()
    far_copy(1).start()
    bias_copy.wait()
    pass_copy(0).wait_recv()

    def far_part(chunk, pair, out, grad_out):
        base = chunk * units
        return far_units(
            sub, rows_of(s_all, pair), rows_of(g_all, pair), w_far.at[1, chunk],
            bias_far.at[:, pl.ds(base, units)], w_far.at[0, chunk], out, grad_out,
        )

    base_far = dict(done)

    @pl.loop(0, pairs)
    def _(pair):
        out = grad_out = None
        for chunk in range(2):
            act, pre_grad = rows_of(acts.at[chunk], pair), rows_of(grads.at[chunk], pair)
            more = dot(act, w_own[0, chunk], 1, 0)
            more_grad = dot(pre_grad, w_own[1, chunk], 1, 1)
            out = more if out is None else out + more
            grad_out = more_grad if grad_out is None else grad_out + more_grad
        out_acc[pair] = out.reshape(2, rows, width)
        grad_acc[pair] = grad_out.reshape(2, rows, width)
        for block in second:
            service(block, base_far[block] + 1 + pair)
        out, grad_out = far_part(0, pair, rows_of(out_acc, pair), rows_of(grad_acc, pair))
        out_acc[pair] = out.reshape(2, rows, width)
        grad_acc[pair] = grad_out.reshape(2, rows, width)
        for block in first:
            service(block, base_far[block] + 1 + pair)

    for block in done:
        done[block] += pairs
    far_copy(1).wait_recv()
    pass_copy(1).start()
    pass_copy(1).wait_recv()

    def out_copies(pair):
        return (
            pltpu.make_async_copy(out_acc.at[pair], branch_hbm.at[pair], out_sem.at[0, pair]),
            pltpu.make_async_copy(grad_acc.at[pair], second_grad_hbm.at[pair], out_sem.at[1, pair]),
        )

    base_last = dict(done)

    @pl.loop(0, pairs)
    def _(pair):
        out, grad_out = far_part(1, pair, rows_of(out_acc, pair), rows_of(grad_acc, pair))
        out_acc[pair] = out.reshape(2, rows, width)
        grad_acc[pair] = grad_out.reshape(2, rows, width)
        for out_copy in out_copies(pair):
            out_copy.start()
        for block in first + second:
            if base_last[block] < LAST_TURN:
                service(block, base_last[block] + 1 + pair)

    for block in done:
        done[block] += pairs
    while min(done.values()) < LAST_TURN:
        serve(*[block for block in done if done[block] < LAST_TURN])

    for chunk in range(2):
        far_copy(chunk).wait_send()
        pass_copy(chunk).wait_send()
    for block in done:
        service_end(block)

    @pl.loop(0, pairs)
    def _(pair):
        for out_copy in out_copies(pair):
            out_copy.wait()


def channel_call(pairs, collective_id, second, out_grad, channel_in, bias_row, channel_out):
    batch, rows, width = second.shape
    own = channel_in.shape[1]
    units = own // 2
    half = units // 2
    shape = jax.ShapeDtypeStruct
    slots = (batch // 2, 2, rows, width)
    anywhere = pl.BlockSpec(memory_space=pl.ANY)
    vmem = pl.BlockSpec(memory_space=pltpu.VMEM)
    dma = pltpu.SemaphoreType.DMA
    held = (pairs, 2, rows, width)
    branch, second_grad, dw, bias_grad = pl.pallas_call(
        functools.partial(channel_kernel, 256),
        name=f"channel_{pairs}",
        out_shape=[
            shape(slots, F32), shape(slots, F32), shape((2, 2, 2 * half, width), BF16), shape((8, own), F32),
        ],
        in_specs=[anywhere] * 4 + [vmem],
        out_specs=[anywhere] * 3 + [vmem],
        scratch_shapes=[
            pltpu.VMEM(held, BF16), pltpu.VMEM(held, BF16),
            pltpu.VMEM((2,) + held, BF16), pltpu.VMEM((2,) + held, BF16),
            pltpu.VMEM((2, 2, units, width), BF16), pltpu.VMEM((2, 2, units, width), BF16),
            pltpu.VMEM((1, own), F32),
            pltpu.VMEM((2, 2, 2 * half, width), BF16), pltpu.VMEM((2, 2 * half, width), BF16),
            pltpu.VMEM((2, 2, 2, SEG, width), BF16), pltpu.VMEM((2, 2, 8, SEG, width), BF16),
            pltpu.VMEM(held, F32), pltpu.VMEM(held, F32),
            dma((3, 2)), dma((2, pairs)), dma((2,)), dma((4, 2)), dma((4, 2, 2)),
            dma((2, 2, 2)), dma((2, 2, 16)), dma((2, 2, 16)), pltpu.SemaphoreType.REGULAR((2, 2)),
        ],
        cost_estimate=pl.CostEstimate(
            flops=40 * pairs * rows * width * units, bytes_accessed=40 << 20, transcendentals=0
        ),
        compiler_params=pltpu.CompilerParams(
            vmem_limit_bytes=CHANNEL_VMEM, collective_id=collective_id, has_side_effects=True
        ),
    )(second.reshape(slots), out_grad.reshape(slots), channel_in, channel_out, bias_row)
    packed = (batch, rows, width)
    return branch.reshape(packed), second_grad.reshape(packed), dw.reshape(2, 2, 2, half, width), bias_grad


def channel_general(size, meta, core, second, out_grad, channel_in, bias_row, channel_out):
    batch, rows, width = second.shape
    own = channel_in.shape[1]
    units = own // 2
    pairs = batch // 2
    packed = (batch, rows, width)
    shape = jax.ShapeDtypeStruct
    pair = pair_spec(rows, width)

    tp_swap = [(0, 1), (1, 0)]
    far_bias = lax.ppermute(bias_row, "tp", tp_swap)
    far = []
    for index in range(2):
        cut = slice(index * units, (index + 1) * units)
        out_cut, in_cut = channel_out[cut, :], channel_in[:, cut]
        got = lax.ppermute(jnp.where(core == 0, out_cut, in_cut), "tp", tp_swap)
        traded = swap(got, 1, size)
        far.append((jnp.where(core == 0, traded, got), jnp.where(core == 0, got, traded)))

    hidden = []
    for index in range(2):
        hidden.append(call(
            functools.partial(hidden_kernel, 256), "hidden_own", (pairs,),
            (meta, second, out_grad, channel_in, bias_row, channel_out),
            [
                pair, pair,
                pl.BlockSpec((width, units), lambda j, meta, index=index: (0, index)),
                pl.BlockSpec((1, units), lambda j, meta, index=index: (0, index)),
                pl.BlockSpec((units, width), lambda j, meta, index=index: (index, 0)),
            ],
            [shape((batch, rows, units), BF16)] * 2 + [shape((2, width // 2, width), BF16)] * 2 + [shape((8, units), F32)],
            [pair_spec(rows, units)] * 2
            + [pl.BlockSpec((2, width // 2, width), lambda j, meta: (0, 0, 0))] * 2
            + [pl.BlockSpec((8, units), lambda j, meta: (0, 0))],
            [pltpu.VMEM((units, width), F32), pltpu.VMEM((width, units), F32)],
            flops=8 * batch * rows * width * units, traffic=8 * batch * rows * width,
        ))
    dw = jnp.stack([sum_over_dp(h[3], h[2], size) for h in hidden])
    mats = (channel_in, channel_out, far[0][0], far_bias[:, :units], far[0][1])
    parts = call(
        functools.partial(far_first_kernel, 256), "far_first", (pairs,),
        (meta, second, out_grad, hidden[0][0], hidden[0][1], hidden[1][0], hidden[1][1], *mats),
        [pair] * 2 + [pair_spec(rows, units)] * 4 + [whole_spec(m) for m in mats],
        [shape(packed, F32)] * 2, [pair] * 2,
        flops=16 * batch * rows * width * units, traffic=20 * batch * rows * width,
    )
    mats = (far[1][0], far_bias[:, units:], far[1][1])
    branch, second_grad = call(
        functools.partial(far_last_kernel, 256), "far_last", (pairs,),
        (meta, second, out_grad, *parts, *mats),
        [pair] * 4 + [whole_spec(m) for m in mats],
        [shape(packed, F32)] * 2, [pair] * 2,
        flops=8 * batch * rows * width * units, traffic=20 * batch * rows * width,
    )
    return branch, second_grad, dw, jnp.concatenate([h[4] for h in hidden], axis=1)


def shards(
    size,
    images, cotangent, image_counts, skip_mask, first_gain, first_bias, token_in, token_in_bias,
    token_out, token_out_bias, second_gain, second_bias, channel_in, channel_in_bias, channel_out,
    channel_out_bias,
):
    batch, patches, width = images.shape
    tokens = token_in.shape[1]
    own = channel_in.shape[1]
    rows = -(-patches // 16) * 16
    units = own // 2
    half = units // 2
    pairs = batch // 2
    core = lax.axis_index("dp") & 1
    meta = steer(image_counts, skip_mask, core)
    most = lax.pmax(meta[N_LIVE], "dp")

    pad = ((0, rows - patches), (0, 0))
    tin = jnp.pad(token_in, pad)
    tin_t, tout_t = tin.T, jnp.pad(token_out.T, pad)
    tout = tout_t.T
    tin_bias = token_in_bias.reshape(tokens, 1)
    tout_bias = token_out_bias.reshape(patches, 1)
    gain1, shift1 = first_gain.reshape(1, width), first_bias.reshape(1, width)
    gain2, shift2 = second_gain.reshape(1, width), second_bias.reshape(1, width)
    out_bias = channel_out_bias.reshape(1, width)
    bias_row = channel_in_bias.reshape(1, own)

    shape = jax.ShapeDtypeStruct
    pair = pair_spec(rows, width)
    packed = (batch, rows, width)
    block = patches * width

    consts = (gain1, shift1, tin_t, tin_bias, tout_t, tout_bias, gain2, shift2)
    second, out_grad, middle, out_bias_grad = call(
        token_forward_kernel, "token_forward", (pairs,),
        (meta, images, images, cotangent, cotangent, *consts),
        [image_spec(patches, width, p) for p in (0, 1, 0, 1)] + [whole_spec(c) for c in consts],
        [shape(packed, BF16), shape(packed, BF16), shape((batch, patches, width), F32), shape((8, width), F32)],
        [pl.BlockSpec((2, rows, width), lambda j, meta: (j, 0, 0))] * 2
        + [pair_spec(patches, width), pl.BlockSpec((8, width), lambda j, meta: (0, 0))],
        flops=4 * batch * rows * width * tokens * 4, traffic=batch * block * 12,
    )

    operands = (second, out_grad, channel_in, bias_row, channel_out)
    general = functools.partial(channel_general, size, meta, core)
    if size == 2 * RING:
        fast = [functools.partial(channel_call, p, i + 1) for i, p in enumerate(FAST_PAIRS)]
        branch_at = sum((most > 2 * p).astype(jnp.int32) for p in FAST_PAIRS)
        branch, second_grad, dw, in_bias_grad = lax.switch(branch_at, fast + [general], *operands)
    else:
        branch, second_grad, dw, in_bias_grad = general(*operands)

    consts = (out_bias, gain1, shift1, gain2, tin, tin_t, tin_bias, tout)
    one = lambda r: pl.BlockSpec((1, r, width), lambda t, meta: (jnp.minimum(t, jnp.maximum(meta[N_LIVE] - 1, 0)), 0, 0))
    smalls = [shape((rows, tokens), F32), shape((tokens, 128), F32), shape((tokens, rows), F32), shape((rows, 128), F32), shape((4, 8, width), F32)]
    in_rows, out_rows = width // batch, own // batch
    in_turns, out_turns = half // in_rows, half // out_rows
    outs = call(
        token_backward_kernel, "token_backward", (batch,),
        (meta, images, cotangent, middle, branch, second_grad, dw, dw, dw, *consts),
        [image_spec(patches, width)] * 2 + [one(patches), one(rows), one(rows)]
        + [
            pl.BlockSpec((1, 1, 1, in_rows, width), lambda t, meta, c=c: (c, t // in_turns, 1, t % in_turns, 0))
            for c in range(2)
        ]
        + [pl.BlockSpec(
            (1, 1, 1, out_rows, width),
            lambda t, meta: (t // (2 * out_turns), (t // out_turns) % 2, 0, t % out_turns, 0),
        )]
        + [whole_spec(c) for c in consts],
        [shape((batch, patches, width), F32)] * 2 + [shape((width, own), F32), shape((own, width), F32)] + smalls,
        [image_spec(patches, width)] * 2
        + [pl.BlockSpec((in_rows, own), lambda t, meta: (t, 0)), pl.BlockSpec((out_rows, width), lambda t, meta: (t, 0))]
        + [whole_spec(s) for s in smalls],
        flops=10 * batch * rows * width * tokens, traffic=batch * block * 24,
    )
    activations, input_grad, in_grad_sum, out_grad_sum, tin_grad, tin_bias_grad, tout_grad, tout_bias_grad, gains = outs
    gains = jnp.sum(gains, axis=1)
    small = lax.psum(
        (
            gains[2], gains[3], tin_grad[:patches], jnp.sum(tin_bias_grad, axis=1),
            tout_grad[:, :patches], jnp.sum(tout_bias_grad, axis=1)[:patches], gains[0], gains[1],
            jnp.sum(in_bias_grad, axis=0), jnp.sum(out_bias_grad, axis=0),
        ),
        "dp",
    )
    return (activations, input_grad, *small[:8], in_grad_sum, small[8], out_grad_sum, small[9])


def solution(mesh):
    placed = (
        P("dp", None, None), P("dp", None, None), P("dp"), P("dp"), P(), P(), P(), P(), P(), P(), P(), P(),
        P(None, "tp"), P("tp"), P("tp", None), P(),
    )
    return jax.shard_map(
        functools.partial(shards, mesh.shape["dp"]),
        mesh=mesh,
        in_specs=placed,
        out_specs=(
            P("dp", None, None), P("dp", None, None), P(), P(), P(), P(), P(), P(), P(), P(),
            P(None, "tp"), P("tp"), P("tp", None), P(),
        ),
        check_vma=False,
    )
```

```python
import functools

import jax
import jax.numpy as jnp
from jax import lax
from jax.experimental import pallas as pl
from jax.experimental.pallas import tpu as pltpu
from jax.sharding import PartitionSpec as P

EPSILON = 1e-06
ROOT_HALF = 0.7071067811865476
INV_ROOT_TAU = 0.3989422804014327
F32, BF16 = jnp.float32, jnp.bfloat16
VMEM_LIMIT = 60 * 1024 * 1024
CHANNEL_VMEM = 60 * 1024 * 1024
RING, SEG, LAST_TURN = 8, 48, 9
FAST_PAIRS = (5, 6, 8)
SHARE_ID, SUM_ID = 9, 10
PACKED = 256

MOVE = 4
N_LIVE, KEPT, RECEIVED, N_PAIRS, CORE, GIVEN, LIST, VALID = 0, 1, 2, 3, 4, 5, 8, 24
GAIN1, SHIFT1, GAIN2, SHIFT2, OUT_BIAS, TIN_BIAS, TOUT_BIAS = range(7)


def dot(left, right, left_dim, right_dim):
    return lax.dot_general(
        left, right, (((left_dim,), (right_dim,)), ((), ())), preferred_element_type=F32
    )


def gelu_parts(values):
    half = 0.5 * (1.0 + lax.erf(values * ROOT_HALF))
    slope = half + values * (INV_ROOT_TAU * jnp.exp(-0.5 * values * values))
    return (values * half).astype(BF16), slope


def gelu_only(values):
    return (values * (0.5 * (1.0 + lax.erf(values * ROOT_HALF)))).astype(BF16)


def standardize(values):
    width = values.shape[-1]
    center = jnp.sum(values, axis=-1, keepdims=True) * (1.0 / width)
    deviation = values - center
    scale = lax.rsqrt(
        jnp.sum(deviation * deviation, axis=-1, keepdims=True) * (1.0 / width) + EPSILON
    )
    return deviation * scale, scale


def norm_back(grad_hat, hat, scale):
    width = hat.shape[-1]
    first = jnp.sum(grad_hat, axis=-1, keepdims=True) * (1.0 / width)
    second = jnp.sum(grad_hat * hat, axis=-1, keepdims=True) * (1.0 / width)
    return scale * (grad_hat - first - hat * second)


def pad_rows(values, rows):
    return jnp.concatenate(
        [values, jnp.zeros((rows - values.shape[0], values.shape[1]), values.dtype)], axis=0
    )


def row_sums(values):
    rows, width = values.shape
    return jnp.sum(values.reshape(rows // 8, 8, width), axis=0)


def lane_sums(values):
    total = values[:, :128]
    for at in range(128, values.shape[1], 128):
        total = total + values[:, at : at + 128]
    return total


def split_lanes(source, target, pieces):
    patches, images, width = source.shape
    step = patches // pieces
    for piece in range(pieces):
        rows = source[piece * step : (piece + 1) * step].astype(F32).reshape(step * images, width)
        for group in range(width // 128):
            target[group, piece * step * images : (piece + 1) * step * images, :] = rows[:, group * 128 : (group + 1) * 128]


def one_image(split, index, images):
    patches = split.shape[1] // images
    return jnp.concatenate(
        [split[group, pl.ds(index, patches, stride=images), :] for group in range(split.shape[0])], axis=1
    )


def share_kernel(
    counts, skips, images, cotangents, meta, most, sent_images, sent_cotangents,
    x_split, c_split, mine, gathered, gathered_smem, send_sem, recv_sem, local_sem,
):
    slots = images.shape[1]
    rows = sent_images.shape[1]
    size = gathered.shape[0]
    me = lax.axis_index("dp")
    barrier = pltpu.get_barrier_semaphore()

    def peer(step):
        return {"dp": lax.rem(me + step, size)}

    for step in range(1, size):
        pl.semaphore_signal(barrier, inc=1, device_id=peer(step), device_id_type=pl.DeviceIdType.MESH)
    one, none = jnp.int32(1), jnp.int32(0)
    valid, live, rank, total = [], [], [], none
    for slot in range(slots):
        valid.append(jnp.where(slot < counts[0], one, none))
        live.append(valid[slot] * skips[slot])
        rank.append(total)
        total = total + live[slot]
    mine[...] = jnp.zeros_like(mine) + total
    gathered[me] = mine[...]
    pl.semaphore_wait(barrier, size - 1)

    def send(step):
        return pltpu.make_async_remote_copy(
            src_ref=mine, dst_ref=gathered.at[me], send_sem=send_sem.at[step], recv_sem=recv_sem.at[step],
            device_id=peer(step), device_id_type=pl.DeviceIdType.MESH,
        )

    for step in range(1, size):
        send(step).start()
    split_lanes(images, x_split, 14)
    split_lanes(cotangents, c_split, 14)
    place_of = [jnp.where(live[slot] == 1, rank[slot], total + slot - rank[slot]) for slot in range(slots)]
    for place in range(slots):
        index, ok = none, none
        for slot in range(slots):
            hit = jnp.where(place_of[slot] == place, one, none)
            index = index + hit * slot
            ok = ok + hit * valid[slot]
        meta[LIST + place] = index
        meta[VALID + place] = ok
    for place in range(MOVE):
        index = none
        for slot in range(slots):
            index = index + slot * live[slot] * jnp.where(rank[slot] == total - 1 - place, one, none)
        sent_images[place] = pad_rows(one_image(x_split, index, slots), rows).astype(BF16)
        sent_cotangents[place] = pad_rows(one_image(c_split, index, slots), rows).astype(BF16)
    for step in range(1, size):
        send(step).wait()
    local = pltpu.make_async_copy(gathered.at[:, 0, :], gathered_smem, local_sem)
    local.start()
    local.wait()

    def excess(left, right):
        return jnp.clip(lax.shift_right_arithmetic(left - right, one), 0, MOVE)

    fullest = none
    for chip in range(size // 2):
        left, right = gathered_smem[2 * chip, 0], gathered_smem[2 * chip + 1, 0]
        shift = excess(left, right) - excess(right, left)
        fullest = jnp.maximum(fullest, jnp.maximum(left - shift, right + shift))
    most[0] = fullest
    sibling = me + 1 - 2 * lax.rem(me, 2)
    there = gathered_smem[sibling, 0]
    given, received = excess(total, there), excess(there, total)
    kept = total - given
    for at, value in (
        (N_LIVE, total), (KEPT, kept), (RECEIVED, received),
        (N_PAIRS, lax.shift_right_arithmetic(kept + received + 1, one)), (CORE, lax.rem(me, 2)), (GIVEN, given),
    ):
        meta[at] = value


def column(row):
    return jnp.transpose(jnp.broadcast_to(row, (8, row.shape[1])))[:, :1]


def token_forward(sources, grads, vectors, tin_t, tin_bias, tout_t, tout_bias, rows):
    patches = sources[0].shape[0]
    normed = [
        pad_rows(standardize(x)[0] * vectors[GAIN1 : GAIN1 + 1] + vectors[SHIFT1 : SHIFT1 + 1], rows).astype(BF16)
        for x in sources
    ]
    pre = [dot(tin_t[...], n, 1, 0) + tin_bias[...] for n in normed]
    act = [gelu_only(p) for p in pre]
    branch = [dot(tout_t[...], a, 1, 0)[:patches] + tout_bias[:patches] for a in act]
    middle = [x + b for x, b in zip(sources, branch)]
    second = [
        pad_rows(standardize(m)[0] * vectors[GAIN2 : GAIN2 + 1] + vectors[SHIFT2 : SHIFT2 + 1], rows) for m in middle
    ]
    return middle, second, [pad_rows(g, rows) for g in grads]


def token_forward_kernel(
    meta, images, cotangents, vectors, tin, tout_in,
    second, out_grad, middle, source, grad_sum, tin_pad, tin_t, tout_t, tout, tin_bias, tout_bias, activations, input_grad,
    x_split, c_split, fill, fill_sem,
):
    step = pl.program_id(0)
    steps = pl.num_programs(0)
    rows = second.shape[1]
    slots = images.shape[1]

    @pl.when(step == 0)
    def _():
        grad_sum[...] = jnp.zeros_like(grad_sum)
        wide = pad_rows(tin[...].astype(F32), rows)
        tin_pad[...] = wide.astype(BF16)
        tin_t[...] = jnp.transpose(wide).astype(BF16)
        wide = pad_rows(tout_in[...].astype(F32), rows)
        tout_t[...] = wide.astype(BF16)
        tout[...] = jnp.transpose(wide).astype(BF16)
        tin_bias[...] = column(vectors[TIN_BIAS : TIN_BIAS + 1, : tin_bias.shape[0]])
        tout_bias[...] = column(vectors[TOUT_BIAS : TOUT_BIAS + 1, : tout_bias.shape[0]])
        split_lanes(images, x_split, 14)
        split_lanes(cotangents, c_split, 14)

    def run(places):
        at = [meta[LIST + 2 * step + place] for place in places]
        sources = [one_image(x_split, index, slots) for index in at]
        grads = [one_image(c_split, index, slots) for index in at]
        mid, sec, gra = token_forward(sources, grads, vectors, tin_t, tin_bias, tout_t, tout_bias, rows)
        for place, m, s, g, x in zip(places, mid, sec, gra, sources):
            middle[place] = m
            second[place] = s.astype(BF16)
            out_grad[place] = g.astype(BF16)
            source[place] = pad_rows(x, rows).astype(BF16)
            grad_sum[...] += row_sums(g)

    @pl.when(2 * step + 1 < meta[KEPT])
    def _():
        run((0, 1))

    @pl.when(2 * step + 1 == meta[KEPT])
    def _():
        run((0,))
        second[1] = jnp.zeros_like(second[1])
        out_grad[1] = jnp.zeros_like(out_grad[1])

    @pl.when(2 * step >= meta[KEPT])
    def _():
        second[...] = jnp.zeros_like(second)
        out_grad[...] = jnp.zeros_like(out_grad)

    def copies(at_step, place):
        slot = lax.rem(at_step, 2)
        index = meta[LIST + 2 * at_step + place]
        return (
            pltpu.make_async_copy(fill.at[slot, place, 0], activations.at[:, index, :], fill_sem.at[slot, place, 0]),
            pltpu.make_async_copy(fill.at[slot, place, 1], input_grad.at[:, index, :], fill_sem.at[slot, place, 1]),
        )

    for place in range(2):

        @pl.when((step >= 2) & (2 * (step - 2) + place >= meta[N_LIVE]))
        def _():
            for copy in copies(step - 2, place):
                copy.wait()

        @pl.when(2 * step + place >= meta[N_LIVE])
        def _():
            index = meta[LIST + 2 * step + place]
            valid = meta[VALID + 2 * step + place].astype(F32)
            slot = lax.rem(step, 2)
            fill[slot, place, 0] = valid * one_image(x_split, index, slots)
            fill[slot, place, 1] = valid * one_image(c_split, index, slots)
            for copy in copies(step, place):
                copy.start()

        @pl.when((step == steps - 1) & (2 * (step - 1) + place >= meta[N_LIVE]))
        def _():
            for copy in copies(step - 1, place):
                copy.wait()

        @pl.when((step == steps - 1) & (2 * step + place >= meta[N_LIVE]))
        def _():
            for copy in copies(step, place):
                copy.wait()


def token_received_kernel(
    meta, images, cotangents, vectors, tin_t, tin_bias, tout_t, tout_bias, grad_sum_in,
    second_in, out_grad_in, middle_in, source_in,
    second, out_grad, middle, source, grad_sum,
    second_one, grad_one, middle_one, sem,
):
    grad_sum[...] = grad_sum_in[...]
    rows = second_one.shape[0]
    patches = middle_one.shape[0]

    @pl.loop(0, meta[RECEIVED])
    def _(place):
        x = images[place, :patches].astype(F32)
        mid, sec, gra = token_forward(
            [x], [cotangents[place, :patches].astype(F32)], vectors, tin_t, tin_bias, tout_t, tout_bias, rows
        )
        second_one[...] = sec[0].astype(BF16)
        grad_one[...] = gra[0].astype(BF16)
        middle_one[...] = mid[0]
        grad_sum[...] += row_sums(gra[0])
        index = meta[KEPT] + place
        copies = [
            pltpu.make_async_copy(src, dst.at[index], sem.at[number])
            for number, (src, dst) in enumerate((
                (second_one, second), (grad_one, out_grad), (middle_one, middle), (images.at[place], source),
            ))
        ]
        for copy in copies:
            copy.start()
        for copy in copies:
            copy.wait()


def hidden_kernel(
    sub, meta, second, out_grad, win, win_bias, wout,
    act_out, pre_grad_out, sent, kept, bias_grad, wout_grad, win_grad,
):
    step, steps = pl.program_id(0), pl.num_programs(0)

    @pl.when(step == 0)
    def _():
        wout_grad[...] = jnp.zeros_like(wout_grad)
        win_grad[...] = jnp.zeros_like(win_grad)
        bias_grad[...] = jnp.zeros_like(bias_grad)

    @pl.when(step < meta[N_PAIRS])
    def _():
        pair, rows, width = second.shape
        s = second[...].reshape(pair * rows, width)
        g = out_grad[...].reshape(pair * rows, width)

        def head(at):
            cut = slice(at, at + sub)
            return dot(s, win[:, cut], 1, 0) + win_bias[:, cut], dot(g, wout[cut, :], 1, 1)

        units = win.shape[1]
        ahead = head(0)
        for at in range(0, units, sub):
            pre, act_grad = ahead
            if at + sub < units:
                ahead = head(at + sub)
            act, slope = gelu_parts(pre)
            grad = act_grad * slope
            pre_grad = grad.astype(BF16)
            cut = slice(at, at + sub)
            act_out[:, :, cut] = act.reshape(pair, rows, sub)
            pre_grad_out[:, :, cut] = pre_grad.reshape(pair, rows, sub)
            bias_grad[:, cut] += row_sums(pre_grad.astype(F32))
            wout_grad[cut, :] += dot(act, g, 0, 0)
            win_grad[:, cut] += dot(s, pre_grad, 0, 0)

    @pl.when(step == steps - 1)
    def _():
        half = kept.shape[1]
        mine = pl.ds(pl.multiple_of(meta[CORE] * half, half), half)
        other = pl.ds(pl.multiple_of((1 - meta[CORE]) * half, half), half)
        kept[0] = wout_grad[mine, :].astype(BF16)
        kept[1] = win_grad[mine, :].astype(BF16)
        sent[0] = wout_grad[other, :].astype(BF16)
        sent[1] = win_grad[other, :].astype(BF16)


def far_units(sub, s, g, win, win_bias, wout, out, grad_out):
    def head(at):
        cut = slice(at, at + sub)
        return dot(s, win[:, cut], 1, 0) + win_bias[:, cut], dot(g, wout[cut, :], 1, 1)

    units = win.shape[1]
    ahead = head(0)
    for at in range(0, units, sub):
        pre, act_grad = ahead
        if at + sub < units:
            ahead = head(at + sub)
        act, slope = gelu_parts(pre)
        pre_grad = (act_grad * slope).astype(BF16)
        cut = slice(at, at + sub)
        more, more_grad = dot(act, wout[cut, :], 1, 0), dot(pre_grad, win[:, cut], 1, 1)
        out = more if out is None else out + more
        grad_out = more_grad if grad_out is None else grad_out + more_grad
    return out, grad_out


def far_first_kernel(
    sub, meta, second, out_grad, act0, grad0, act1, grad1, win_own, wout_own, win, win_bias, wout,
    out_part, grad_part,
):
    step = pl.program_id(0)

    @pl.when(step < meta[N_PAIRS])
    def _():
        pair, rows, width = second.shape
        flat = (pair * rows, width)
        s, g = second[...].reshape(flat), out_grad[...].reshape(flat)
        units = win.shape[1]
        out, grad_out = far_units(sub, s, g, win, win_bias, wout, None, None)
        for index, (act, pre_grad) in enumerate(((act0, grad0), (act1, grad1))):
            cut = slice(index * units, (index + 1) * units)
            out = out + dot(act[...].reshape(flat), wout_own[cut, :], 1, 0)
            grad_out = grad_out + dot(pre_grad[...].reshape(flat), win_own[:, cut], 1, 1)
        out_part[...] = out.reshape(pair, rows, width)
        grad_part[...] = grad_out.reshape(pair, rows, width)


def far_last_kernel(
    sub, meta, second, out_grad, out_part, grad_part, win, win_bias, wout, branch, second_grad,
):
    step = pl.program_id(0)

    @pl.when(step < meta[N_PAIRS])
    def _():
        pair, rows, width = second.shape
        flat = (pair * rows, width)
        s, g = second[...].reshape(flat), out_grad[...].reshape(flat)
        out, grad_out = far_units(
            sub, s, g, win, win_bias, wout, out_part[...].reshape(flat), grad_part[...].reshape(flat)
        )
        branch[...] = out.reshape(pair, rows, width).astype(BF16)
        second_grad[...] = grad_out.reshape(pair, rows, width).astype(BF16)


def token_backward_kernel(
    own, meta, *refs,
):
    items = [refs[2 * number : 2 * number + 2] for number in range(5)]
    images, grads, middles, branches, second_grads = items
    vectors, tin, tin_t, tin_bias, tout = refs[10:15]
    refs = refs[15:]
    if own:
        sums_in, refs = refs[:5], refs[5:]
        dw_in0, dw_in1, dw_out = refs[:3]
        refs = refs[5:]
    activations, input_grad = refs[:2]
    sums = refs[2:7]
    refs = refs[7:]
    if own:
        win_grad, wout_grad = refs[:2]
        refs = refs[2:]
    stage, stage_sem = refs
    tin_grad, tin_bias_grad, tout_grad, tout_bias_grad, gains = sums
    step, steps = pl.program_id(0), pl.num_programs(0)
    patches, rows = middles[0].shape[1], images[0].shape[1]
    count = meta[KEPT] if own else meta[RECEIVED]

    @pl.when(step == 0)
    def _():
        for number, ref in enumerate(sums):
            ref[...] = sums_in[number][...] if own else jnp.zeros_like(ref)

    if own:
        units = dw_in0.shape[-1]
        win_grad[:, :units] = dw_in0[...].reshape(win_grad.shape[0], units).astype(F32)
        win_grad[:, units:] = dw_in1[...].reshape(win_grad.shape[0], units).astype(F32)
        wout_grad[...] = dw_out[...].reshape(wout_grad.shape).astype(F32)

    def copies(at_step, place):
        slot = lax.rem(at_step, 2)
        item = 2 * at_step + place
        if own:
            index = meta[LIST + item]
            targets = (activations.at[:, index, :], input_grad.at[:, index, :])
        else:
            targets = (activations.at[:, item, :], input_grad.at[:, item, :])
        return [
            pltpu.make_async_copy(stage.at[slot, place, number], target, stage_sem.at[slot, place, number])
            for number, target in enumerate(targets)
        ]

    def vector(row):
        return vectors[row : row + 1]

    def run(places):
        slot = lax.rem(step, 2)
        middle = [middles[p][0] for p in places]
        norm2 = [standardize(m) for m in middle]
        grad2 = [second_grads[p][0].astype(F32)[:patches] for p in places]
        middle_grad = [
            grads[p][0].astype(F32)[:patches] + norm_back(g * vector(GAIN2), hat, scale)
            for p, g, (hat, scale) in zip(places, grad2, norm2)
        ]
        branch_grad = [pad_rows(m, rows).astype(BF16) for m in middle_grad]
        norm1 = [standardize(images[p][0].astype(F32)[:patches]) for p in places]
        normed = [pad_rows(hat * vector(GAIN1) + vector(SHIFT1), rows).astype(BF16) for hat, _ in norm1]
        pre = [dot(tin_t[...], n, 1, 0) + tin_bias[...] for n in normed]
        act_grad = [dot(tout[...], b, 1, 0) for b in branch_grad]
        parts = [gelu_parts(p) for p in pre]
        pre_grad = [(a * slope).astype(BF16) for a, (_, slope) in zip(act_grad, parts)]
        normed_grad = [dot(tin[...], p, 1, 0)[:patches] for p in pre_grad]
        for p, m in zip(places, middle):
            stage[slot, p, 0] = m + (branches[p][0].astype(F32)[:patches] + vector(OUT_BIAS))
        for p, m, n, (hat, scale) in zip(places, middle_grad, normed_grad, norm1):
            stage[slot, p, 1] = m + norm_back(n * vector(GAIN1), hat, scale)
        for p in places:
            for copy in copies(step, p):
                copy.start()
        tout_grad[...] += sum(dot(act, b, 1, 1) for (act, _), b in zip(parts, branch_grad))
        tin_grad[...] += sum(dot(n, p, 1, 1) for n, p in zip(normed, pre_grad))
        tin_bias_grad[...] += sum(lane_sums(p.astype(F32)) for p in pre_grad)
        tout_bias_grad[...] += sum(lane_sums(b.astype(F32)) for b in branch_grad)
        gains[0] += sum(row_sums(pad_rows(g * hat, rows)) for g, (hat, _) in zip(grad2, norm2))
        gains[1] += sum(row_sums(pad_rows(g, rows)) for g in grad2)
        gains[2] += sum(row_sums(pad_rows(n * hat, rows)) for n, (hat, _) in zip(normed_grad, norm1))
        gains[3] += sum(row_sums(pad_rows(n, rows)) for n in normed_grad)

    for place in range(2):

        @pl.when((step >= 2) & (2 * (step - 2) + place < count))
        def _():
            for copy in copies(step - 2, place):
                copy.wait()

    @pl.when(2 * step + 1 < count)
    def _():
        run((0, 1))

    @pl.when(2 * step + 1 == count)
    def _():
        run((0,))

    for place in range(2):
        for back in (1, 0):

            @pl.when((step == steps - 1) & (step >= back) & (2 * (step - back) + place < count))
            def _():
                for copy in copies(step - back, place):
                    copy.wait()


def place_kernel(meta, images, grads, activations_in, input_grad_in, activations, input_grad, held, sem):
    def loads(place):
        return [
            pltpu.make_async_copy(back.at[:, place, :], held.at[number, place], sem.at[0, number, place])
            for number, back in enumerate((images, grads))
        ]

    def stores(place):
        index = meta[LIST + meta[N_LIVE] - 1 - place]
        return [
            pltpu.make_async_copy(held.at[number, place], out.at[:, index, :], sem.at[1, number, place])
            for number, out in enumerate((activations, input_grad))
        ]

    @pl.loop(0, meta[GIVEN])
    def _(place):
        for copy in loads(place):
            copy.start()

    @pl.loop(0, meta[GIVEN])
    def _(place):
        for load, store in zip(loads(place), stores(place)):
            load.wait()
            store.start()

    @pl.loop(0, meta[GIVEN])
    def _(place):
        for copy in stores(place):
            copy.wait()


def small_sum_kernel(
    tin_grad, tout_grad, tin_bias_grad, tout_bias_grad, gains, in_bias_grad, out_bias_grad,
    tin_out, tout_out, tin_bias_out, tout_bias_out, gain1_out, shift1_out, gain2_out, shift2_out, in_bias_out, out_bias_out,
    packed, landed, reduced, gathered, other, pieces, core_sem, sum_send, sum_recv, gather_send, gather_recv,
):
    width = packed.shape[-1]
    rows, tokens = tin_grad.shape
    patches = tin_out.shape[0]
    me = lax.axis_index("dp")
    core, chip = lax.rem(me, 2), lax.div(me, 2)
    sibling = me + 1 - 2 * core

    def chip_at(step):
        return lax.rem(chip + step, RING)

    def peer(step):
        return {"dp": 2 * chip_at(step) + core}

    barrier = pltpu.get_barrier_semaphore()
    for near in [{"dp": sibling}] + [peer(step) for step in range(1, RING)]:
        pl.semaphore_signal(barrier, inc=1, device_id=near, device_id_type=pl.DeviceIdType.MESH)

    def remote(src, dst, send, recv, device):
        return pltpu.make_async_remote_copy(
            src_ref=src, dst_ref=dst, send_sem=send, recv_sem=recv, device_id=device,
            device_id_type=pl.DeviceIdType.MESH,
        )

    half_rows, third = rows // 2, tokens // 3
    wide_tout = jnp.concatenate([tout_grad[...], jnp.zeros((tokens, 256 - rows), F32)], axis=1)
    line = lambda v: jnp.sum(v, axis=0, keepdims=True)
    flat = lambda v: jnp.concatenate([v, jnp.zeros((1, width - v.shape[1]), F32)], axis=1)
    vectors = [line(gains[number]) for number in range(4)]
    in_bias = line(in_bias_grad[...])
    vectors += [in_bias[:, :width], in_bias[:, width:], line(out_bias_grad[...])]
    vectors += [flat(line(jnp.transpose(tin_bias_grad[...]))), flat(line(jnp.transpose(tout_bias_grad[...])))]
    everything = jnp.concatenate([
        jnp.concatenate([tin_grad[:half_rows], tin_grad[half_rows:]], axis=1),
        jnp.concatenate([wide_tout[number * third : (number + 1) * third] for number in range(3)], axis=1),
        jnp.concatenate(vectors + [jnp.zeros((PACKED - half_rows - third - len(vectors), width), F32)], axis=0),
    ], axis=0)
    packed[0] = everything[: PACKED // 2]
    packed[1] = everything[PACKED // 2 :]
    pl.semaphore_wait(barrier, RING)

    swap_copy = remote(packed.at[1 - core], landed, core_sem.at[0], core_sem.at[1], {"dp": sibling})
    swap_copy.start()
    swap_copy.wait()
    packed[core] = packed[core] + landed[...]
    reduced[...] = packed[core].astype(BF16)
    piece = PACKED // 2 // RING

    def segment(ref, index):
        return ref.at[pl.ds(pl.multiple_of(index * piece, piece), piece)]

    def sum_copy(step):
        return remote(segment(reduced, chip_at(step)), pieces.at[step], sum_send.at[step], sum_recv.at[step], peer(step))

    for step in range(1, RING):
        sum_copy(step).start()
    total = segment(packed.at[core], chip)[...]
    for step in range(1, RING):
        sum_copy(step).wait()
        total = total + pieces[step].astype(F32)
    pieces[0] = total.astype(BF16)

    def gather_copy(step):
        return remote(
            pieces.at[0], segment(gathered, chip), gather_send.at[step], gather_recv.at[step], peer(step)
        )

    for step in range(1, RING):
        gather_copy(step).start()
    segment(gathered, chip)[...] = pieces[0]
    for step in range(1, RING):
        gather_copy(step).wait()
    back_copy = remote(gathered, other, core_sem.at[2], core_sem.at[3], {"dp": sibling})
    back_copy.start()
    back_copy.wait()
    low = jnp.where(core == 0, gathered[...].astype(F32), other[...].astype(F32))
    high = jnp.where(core == 0, other[...].astype(F32), gathered[...].astype(F32))
    summed = jnp.concatenate([low, high], axis=0)
    tin_all = jnp.concatenate([summed[:half_rows, :tokens], summed[:half_rows, tokens:]], axis=0)
    tin_out[...] = tin_all[:patches]
    tout_all = jnp.concatenate(
        [summed[half_rows : half_rows + third, number * 256 : (number + 1) * 256] for number in range(3)], axis=0
    )
    tout_out[...] = tout_all[:, :patches]
    vector = lambda number: summed[half_rows + third + number : half_rows + third + number + 1]
    gain2_out[...], shift2_out[...], gain1_out[...], shift1_out[...] = (vector(number) for number in range(4))
    in_bias_out[...] = jnp.concatenate([vector(4), vector(5)], axis=1)
    out_bias_out[...] = vector(6)
    tin_bias_out[...] = vector(7)[:, :tokens]
    tout_bias_out[...] = vector(8)[:, :patches]


def last_pair(step, meta):
    return jnp.minimum(step, jnp.maximum(meta[N_PAIRS] - 1, 0))


def pair_spec(rows, width):
    return pl.BlockSpec((2, rows, width), lambda j, meta: (last_pair(j, meta), 0, 0))


def whole_spec(array):
    zeros = (0,) * array.ndim
    return pl.BlockSpec(array.shape, lambda j, meta: zeros)


def call(body, name, grid, args, in_specs, outs, out_specs, scratch=(), flops=0, traffic=0, aliases={}):
    return pl.pallas_call(
        body,
        name=name,
        out_shape=outs,
        grid_spec=pltpu.PrefetchScalarGridSpec(
            num_scalar_prefetch=1,
            grid=grid,
            in_specs=in_specs,
            out_specs=out_specs,
            scratch_shapes=scratch,
        ),
        input_output_aliases=aliases,
        cost_estimate=pl.CostEstimate(flops=flops, bytes_accessed=traffic, transcendentals=0),
        compiler_params=pltpu.CompilerParams(
            vmem_limit_bytes=VMEM_LIMIT, dimension_semantics=("arbitrary",)
        ),
    )(*args)


def swap(value, bit, size):
    return lax.ppermute(value, "dp", [(i, i ^ bit) for i in range(size)])


def sum_over_dp(kept, sent, size):
    me = lax.axis_index("dp")
    core, bit1, rest = me & 1, (me >> 1) & 1, me >> 2
    groups = size // 4
    total = kept.astype(F32) + swap(sent, 1, size).astype(F32)
    mine = jnp.where(bit1 == 0, total[0], total[1])
    other = jnp.where(bit1 == 0, total[1], total[0]).astype(BF16)
    total = mine + swap(other, 2, size).astype(F32)
    rows, width = total.shape
    pieces = total.astype(BF16).reshape(groups, rows // groups, width)
    if groups <= 4:
        arrived = [
            swap(lax.dynamic_index_in_dim(pieces, rest ^ k, keepdims=False), 4 * k, size)
            for k in range(1, groups)
        ]
        piece = lax.dynamic_index_in_dim(
            total.reshape(groups, rows // groups, width), rest, keepdims=False
        )
        for other in arrived:
            piece = piece + other.astype(F32)
        piece = piece.astype(BF16)
        whole = jnp.zeros((groups, rows // groups, width), BF16)
        whole = lax.dynamic_update_index_in_dim(whole, piece, rest, 0)
        for k in range(1, groups):
            whole = lax.dynamic_update_index_in_dim(whole, swap(piece, 4 * k, size), rest ^ k, 0)
    else:
        teams = [[4 * r + low for r in range(groups)] for low in range(4)]
        arrived = lax.all_to_all(pieces, "dp", 0, 0, axis_index_groups=teams)
        piece = jnp.sum(arrived.astype(F32), axis=0).astype(BF16)
        whole = lax.all_gather(piece, "dp", axis_index_groups=teams)
    part = whole.reshape(rows, width)
    far = swap(part, 2, size)
    both = jnp.where(bit1 == 0, jnp.stack([part, far]), jnp.stack([far, part]))
    far = swap(both, 1, size)
    return jnp.where(core == 0, jnp.stack([both, far]), jnp.stack([far, both]))


def channel_kernel(
    sub, second_hbm, grad_hbm, win_hbm, wout_hbm, bias,
    branch_hbm, second_grad_hbm, dw_hbm, bias_grad,
    s_all, g_all, acts, grads, w_own, w_far, bias_far, dw, traded, starts, hops, out_acc, grad_acc, out_stage,
    load_sem, out_sem, bias_sem, far_sem, core_sem, result_sem, ring_send, ring_recv, free_sem,
):
    pairs, _, rows, width = s_all.shape
    units = width
    direct = out_acc.dtype == BF16
    if direct:
        out_acc, grad_acc = acts.at[0], grads.at[0]
    half = units // 2
    flat = (2 * rows, width)
    me = lax.axis_index("dp")
    core, y, z = lax.rem(me, 2), lax.rem(lax.div(me, 2), 2), lax.div(me, 4)
    tp = lax.axis_index("tp")
    at = y * 4 + z + y * (3 - 2 * z)

    def device_at(place):
        place = lax.rem(place + RING, RING)
        row = lax.div(place, 4)
        col = lax.rem(place, 4)
        return (col + row * (3 - 2 * col)) * 4 + row * 2 + core

    sibling = me + 1 - 2 * core
    ways = (device_at(at + 1), device_at(at - 1))

    barrier = pltpu.get_barrier_semaphore()
    for near in ({"dp": sibling}, {"dp": ways[0]}, {"dp": ways[1]}, {"tp": 1 - tp}):
        pl.semaphore_signal(barrier, inc=1, device_id=near, device_id_type=pl.DeviceIdType.MESH)
    pl.semaphore_wait(barrier, 4)

    def remote(src, dst, sems, recv, device):
        return pltpu.make_async_remote_copy(
            src_ref=src, dst_ref=dst, send_sem=sems, recv_sem=recv, device_id=device,
            device_id_type=pl.DeviceIdType.MESH,
        )

    loads = []
    for chunk in range(2):
        cut = pl.ds(chunk * units, units)
        loads.append(pltpu.make_async_copy(wout_hbm.at[cut, :], w_own.at[0, chunk], load_sem.at[chunk, 0]))
        loads.append(pltpu.make_async_copy(win_hbm.at[:, cut], w_own.at[1, chunk], load_sem.at[chunk, 1]))
    loads.append(pltpu.make_async_copy(second_hbm.at[pl.ds(0, pairs)], s_all, load_sem.at[2, 0]))
    loads.append(pltpu.make_async_copy(grad_hbm.at[pl.ds(0, pairs)], g_all, load_sem.at[2, 1]))
    for load in (loads[0], loads[1], loads[4], loads[5], loads[2], loads[3]):
        load.start()

    def far_copy(chunk):
        return remote(w_own.at[core, chunk], w_far.at[core, chunk], far_sem.at[0, chunk], far_sem.at[1, chunk], {"tp": 1 - tp})

    def pass_copy(chunk):
        return remote(w_far.at[core, chunk], w_far.at[core, chunk], far_sem.at[2, chunk], far_sem.at[3, chunk], {"dp": sibling})

    bias_copy = remote(bias, bias_far, bias_sem.at[0], bias_sem.at[1], {"tp": 1 - tp})
    bias_copy.start()
    loads[0].wait()
    loads[1].wait()
    far_copy(0).start()
    bias_grad[...] = jnp.zeros_like(bias_grad)
    loads[4].wait()
    loads[5].wait()

    def reach(matrix, way):
        return 4 if matrix == way else 3

    def segment(block, index):
        chunk, matrix = block
        index = lax.rem(index + 2 * RING, RING)
        return dw.at[chunk, core, pl.ds(pl.multiple_of(matrix * half + index * SEG, SEG), SEG)]

    def sign(way):
        return 1 - 2 * way

    def part_of(ref, block, which):
        chunk, matrix = block
        return ref.at[chunk, which, pl.ds(matrix * half, half)]

    def landing(block):
        chunk, matrix = block
        return traded.at[chunk, pl.ds(matrix * half, half)]

    def core_copy(block):
        return remote(part_of(dw, block, 1 - core), landing(block), core_sem.at[(0, *block)], core_sem.at[(1, *block)], {"dp": sibling})

    def back_copy(block):
        return remote(part_of(dw, block, core), landing(block), core_sem.at[(2, *block)], core_sem.at[(3, *block)], {"dp": sibling})

    def result_copies(block):
        return (
            pltpu.make_async_copy(part_of(dw, block, core), part_of(dw_hbm, block, core), result_sem.at[(0, *block)]),
            pltpu.make_async_copy(landing(block), part_of(dw_hbm, block, 1 - core), result_sem.at[(1, *block)]),
        )

    def hop_copy(block, way, hop, src):
        slot = way * 4 + hop - 1
        return remote(
            src, hops.at[(*block, slot)], ring_send.at[(*block, slot)], ring_recv.at[(*block, slot)], {"dp": ways[way]}
        )

    def hop_arrived(block, way, hop):
        slot = hops.at[(*block, way * 4 + hop - 1)]
        hop_copy(block, way, hop, slot).wait_recv()
        return slot

    def spread_copy(block, way, hop, index):
        slot = 8 + way * 4 + hop - 1
        place = segment(block, index)
        return remote(place, place, ring_send.at[(*block, slot)], ring_recv.at[(*block, slot)], {"dp": ways[way]})

    def service(block, turn):
        @pl.when(turn == 0)
        def _():
            core_copy(block).wait()
            mine = part_of(dw, block, core)
            mine[...] = (mine[...].astype(F32) + landing(block)[...].astype(F32)).astype(BF16)
            pl.semaphore_signal(free_sem.at[block], inc=1, device_id={"dp": sibling}, device_id_type=pl.DeviceIdType.MESH)
            for way in range(2):
                begin = starts.at[(*block, way)]
                begin[...] = segment(block, at + sign(way) * reach(block[1], way))[...]
                hop_copy(block, way, 1, begin).start()

        for hop in range(2, 5):

            @pl.when(turn == hop - 1)
            def _():
                for way in range(2):
                    if hop <= reach(block[1], way):
                        slot = hop_arrived(block, way, hop - 1)
                        own = segment(block, at + sign(way) * (reach(block[1], way) - hop + 1))
                        slot[...] = (slot[...].astype(F32) + own[...].astype(F32)).astype(BF16)
                        hop_copy(block, way, hop, slot).start()

        @pl.when(turn == 4)
        def _():
            own = segment(block, at)
            total = own[...].astype(F32)
            for way in range(2):
                total = total + hop_arrived(block, way, reach(block[1], way))[...].astype(F32)
            own[...] = total.astype(BF16)
            for way in range(2):
                spread_copy(block, way, 1, at).start()

        for hop in range(2, 5):

            @pl.when(turn == hop + 3)
            def _():
                for way in range(2):
                    if hop <= reach(block[1], way):
                        spread_copy(block, way, hop - 1, at - sign(way) * (hop - 1)).wait_recv()
                        spread_copy(block, way, hop, at - sign(way) * (hop - 1)).start()

        @pl.when(turn == 8)
        def _():
            for way in range(2):
                last = reach(block[1], way)
                spread_copy(block, way, last, at - sign(way) * last).wait_recv()
            pl.semaphore_wait(free_sem.at[block], 1)
            back_copy(block).start()

        @pl.when(turn == LAST_TURN)
        def _():
            back_copy(block).wait_recv()
            for result in result_copies(block):
                result.start()

    def service_end(block):
        back_copy(block).wait_send()
        for result in result_copies(block):
            result.wait()
        for way in range(2):
            for hop in range(1, reach(block[1], way) + 1):
                hop_copy(block, way, hop, hops.at[(*block, way * 4 + hop - 1)]).wait_send()
                spread_copy(block, way, hop, at).wait_send()

    def rows_of(ref, pair):
        return ref[pair].reshape(flat)

    def own_units(chunk, pair):
        s, g = rows_of(s_all, pair), rows_of(g_all, pair)

        def head(start):
            cut = slice(start, start + sub)
            place = slice(chunk * units + start, chunk * units + start + sub)
            return (
                dot(s, w_own[1, chunk, :, cut], 1, 0) + bias[:, place],
                dot(g, w_own[0, chunk, cut, :], 1, 1),
            )

        ahead = head(0)
        for start in range(0, units, sub):
            pre, act_grad = ahead
            if start + sub < units:
                ahead = head(start + sub)
            act, slope = gelu_parts(pre)
            pre_grad = (act_grad * slope).astype(BF16)
            cut = slice(start, start + sub)
            place = slice(chunk * units + start, chunk * units + start + sub)
            acts[chunk, pair, :, :, cut] = act.reshape(2, rows, sub)
            grads[chunk, pair, :, :, cut] = pre_grad.reshape(2, rows, sub)
            bias_grad[:, place] += row_sums(pre_grad.astype(F32))

    def weight_grads(chunk, matrix, part):
        depth = pairs * 2 * rows
        cut = slice(part * half, (part + 1) * half)
        if matrix == 0:
            left, right = acts[chunk, :, :, :, cut], g_all[...]
        else:
            left, right = s_all[:, :, :, cut], grads[chunk]
        grad = dot(left.reshape(depth, half), right.reshape(depth, width), 0, 0)
        dw[chunk, part, matrix * half : (matrix + 1) * half] = grad.astype(BF16)

    first = [(0, 0), (0, 1)]
    second = [(1, 0), (1, 1)]
    done = {block: -1 for block in first + second}

    def serve(*blocks):
        for block in blocks:
            done[block] += 1
            if done[block] <= LAST_TURN:
                service(block, done[block])

    @pl.loop(0, pairs)
    def _(pair):
        own_units(0, pair)

    for matrix in range(2):
        weight_grads(0, matrix, 0)
        weight_grads(0, matrix, 1)
        core_copy((0, matrix)).start()
    serve((0, 0))
    loads[2].wait()
    loads[3].wait()

    base = dict(done)

    @pl.loop(0, pairs)
    def _(pair):
        own_units(1, pair)

        @pl.when(lax.rem(pair, 2) == 1)
        def _():
            for block in first:
                service(block, base[block] + 1 + lax.div(pair, 2))

    for block in first:
        done[block] += pairs // 2
    weight_grads(1, 0, 0)
    weight_grads(1, 0, 1)
    core_copy((1, 0)).start()
    serve(*first)
    weight_grads(1, 1, 0)
    weight_grads(1, 1, 1)
    core_copy((1, 1)).start()
    serve((1, 0), *first)
    far_copy(0).wait_recv()
    pass_copy(0).start()
    far_copy(1).start()
    bias_copy.wait()
    pass_copy(0).wait_recv()

    def far_part(chunk, pair, out, grad_out):
        base = chunk * units
        return far_units(
            sub, rows_of(s_all, pair), rows_of(g_all, pair), w_far.at[1, chunk],
            bias_far.at[:, pl.ds(base, units)], w_far.at[0, chunk], out, grad_out,
        )

    base_far = dict(done)

    @pl.loop(0, pairs)
    def _(pair):
        out = grad_out = None
        for chunk in range(2):
            act, pre_grad = rows_of(acts.at[chunk], pair), rows_of(grads.at[chunk], pair)
            more = dot(act, w_own[0, chunk], 1, 0)
            more_grad = dot(pre_grad, w_own[1, chunk], 1, 1)
            out = more if out is None else out + more
            grad_out = more_grad if grad_out is None else grad_out + more_grad
        out_acc[pair] = out.reshape(2, rows, width).astype(out_acc.dtype)
        grad_acc[pair] = grad_out.reshape(2, rows, width).astype(out_acc.dtype)
        for block in second:
            service(block, base_far[block] + 1 + pair)
        out, grad_out = far_part(0, pair, rows_of(out_acc, pair).astype(F32), rows_of(grad_acc, pair).astype(F32))
        out_acc[pair] = out.reshape(2, rows, width).astype(out_acc.dtype)
        grad_acc[pair] = grad_out.reshape(2, rows, width).astype(out_acc.dtype)
        for block in first:
            service(block, base_far[block] + 1 + pair)

    for block in done:
        done[block] += pairs
    far_copy(1).wait_recv()
    pass_copy(1).start()
    pass_copy(1).wait_recv()

    slots = pairs if direct else 2

    def out_places(pair):
        slot = lax.rem(pair, slots)
        if direct:
            return out_acc.at[slot], grad_acc.at[slot]
        return out_stage.at[slot, 0], out_stage.at[slot, 1]

    def out_copies(pair):
        slot = lax.rem(pair, slots)
        out_place, grad_place = out_places(pair)
        return (
            pltpu.make_async_copy(out_place, branch_hbm.at[pair], out_sem.at[0, slot]),
            pltpu.make_async_copy(grad_place, second_grad_hbm.at[pair], out_sem.at[1, slot]),
        )

    base_last = dict(done)

    @pl.loop(0, pairs)
    def _(pair):
        out, grad_out = far_part(1, pair, rows_of(out_acc, pair).astype(F32), rows_of(grad_acc, pair).astype(F32))

        @pl.when(pair >= slots)
        def _():
            for out_copy in out_copies(pair - slots):
                out_copy.wait()

        out_place, grad_place = out_places(pair)
        out_place[...] = out.reshape(2, rows, width).astype(BF16)
        grad_place[...] = grad_out.reshape(2, rows, width).astype(BF16)
        for out_copy in out_copies(pair):
            out_copy.start()
        for block in first + second:
            if base_last[block] < LAST_TURN:
                service(block, base_last[block] + 1 + pair)

    for block in done:
        done[block] += pairs
    while min(done.values()) < LAST_TURN:
        serve(*[block for block in done if done[block] < LAST_TURN])

    for chunk in range(2):
        far_copy(chunk).wait_send()
        pass_copy(chunk).wait_send()
    for block in done:
        service_end(block)

    for pair in range(pairs - slots, pairs):
        for out_copy in out_copies(pair):
            out_copy.wait()


def channel_call(pairs, collective_id, second, out_grad, channel_in, bias_row, channel_out):
    batch, rows, width = second.shape
    own = channel_in.shape[1]
    units = own // 2
    half = units // 2
    shape = jax.ShapeDtypeStruct
    slots = (batch // 2, 2, rows, width)
    anywhere = pl.BlockSpec(memory_space=pl.ANY)
    vmem = pl.BlockSpec(memory_space=pltpu.VMEM)
    dma = pltpu.SemaphoreType.DMA
    held = (pairs, 2, rows, width)
    acc_type = F32 if pairs <= 5 else BF16
    branch, second_grad, dw, bias_grad = pl.pallas_call(
        functools.partial(channel_kernel, 256),
        name=f"channel_{pairs}",
        out_shape=[
            shape(slots, BF16), shape(slots, BF16), shape((2, 2, 2 * half, width), BF16), shape((8, own), F32),
        ],
        in_specs=[anywhere] * 4 + [vmem],
        out_specs=[anywhere] * 3 + [vmem],
        scratch_shapes=[
            pltpu.VMEM(held, BF16), pltpu.VMEM(held, BF16),
            pltpu.VMEM((2,) + held, BF16), pltpu.VMEM((2,) + held, BF16),
            pltpu.VMEM((2, 2, units, width), BF16), pltpu.VMEM((2, 2, units, width), BF16),
            pltpu.VMEM((1, own), F32),
            pltpu.VMEM((2, 2, 2 * half, width), BF16), pltpu.VMEM((2, 2 * half, width), BF16),
            pltpu.VMEM((2, 2, 2, SEG, width), BF16), pltpu.VMEM((2, 2, 8, SEG, width), BF16),
            pltpu.VMEM(held if acc_type == F32 else (16, 128), acc_type),
            pltpu.VMEM(held if acc_type == F32 else (16, 128), acc_type),
            pltpu.VMEM((2, 2, 2, rows, width) if acc_type == F32 else (1, 1, 1, 16, 128), BF16),
            dma((3, 2)), dma((2, pairs)), dma((2,)), dma((4, 2)), dma((4, 2, 2)),
            dma((2, 2, 2)), dma((2, 2, 16)), dma((2, 2, 16)), pltpu.SemaphoreType.REGULAR((2, 2)),
        ],
        cost_estimate=pl.CostEstimate(
            flops=40 * pairs * rows * width * units, bytes_accessed=40 << 20, transcendentals=0
        ),
        compiler_params=pltpu.CompilerParams(
            vmem_limit_bytes=CHANNEL_VMEM, collective_id=collective_id, has_side_effects=True
        ),
    )(second.reshape(slots), out_grad.reshape(slots), channel_in, channel_out, bias_row)
    packed = (batch, rows, width)
    return branch.reshape(packed), second_grad.reshape(packed), dw.reshape(2, 2, 2, half, width), bias_grad


def channel_general(size, meta, core, second, out_grad, channel_in, bias_row, channel_out):
    batch, rows, width = second.shape
    own = channel_in.shape[1]
    units = own // 2
    pairs = batch // 2
    packed = (batch, rows, width)
    shape = jax.ShapeDtypeStruct
    pair = pair_spec(rows, width)

    tp_swap = [(0, 1), (1, 0)]
    far_bias = lax.ppermute(bias_row, "tp", tp_swap)
    far = []
    for index in range(2):
        cut = slice(index * units, (index + 1) * units)
        out_cut, in_cut = channel_out[cut, :], channel_in[:, cut]
        got = lax.ppermute(jnp.where(core == 0, out_cut, in_cut), "tp", tp_swap)
        traded = swap(got, 1, size)
        far.append((jnp.where(core == 0, traded, got), jnp.where(core == 0, got, traded)))

    hidden = []
    for index in range(2):
        hidden.append(call(
            functools.partial(hidden_kernel, 256), "hidden_own", (pairs,),
            (meta, second, out_grad, channel_in, bias_row, channel_out),
            [
                pair, pair,
                pl.BlockSpec((width, units), lambda j, meta, index=index: (0, index)),
                pl.BlockSpec((1, units), lambda j, meta, index=index: (0, index)),
                pl.BlockSpec((units, width), lambda j, meta, index=index: (index, 0)),
            ],
            [shape((batch, rows, units), BF16)] * 2 + [shape((2, width // 2, width), BF16)] * 2 + [shape((8, units), F32)],
            [pair_spec(rows, units)] * 2
            + [pl.BlockSpec((2, width // 2, width), lambda j, meta: (0, 0, 0))] * 2
            + [pl.BlockSpec((8, units), lambda j, meta: (0, 0))],
            [pltpu.VMEM((units, width), F32), pltpu.VMEM((width, units), F32)],
            flops=8 * batch * rows * width * units, traffic=8 * batch * rows * width,
        ))
    dw = jnp.stack([sum_over_dp(h[3], h[2], size) for h in hidden])
    mats = (channel_in, channel_out, far[0][0], far_bias[:, :units], far[0][1])
    parts = call(
        functools.partial(far_first_kernel, 256), "far_first", (pairs,),
        (meta, second, out_grad, hidden[0][0], hidden[0][1], hidden[1][0], hidden[1][1], *mats),
        [pair] * 2 + [pair_spec(rows, units)] * 4 + [whole_spec(m) for m in mats],
        [shape(packed, F32)] * 2, [pair] * 2,
        flops=16 * batch * rows * width * units, traffic=20 * batch * rows * width,
    )
    mats = (far[1][0], far_bias[:, units:], far[1][1])
    branch, second_grad = call(
        functools.partial(far_last_kernel, 256), "far_last", (pairs,),
        (meta, second, out_grad, *parts, *mats),
        [pair] * 4 + [whole_spec(m) for m in mats],
        [shape(packed, BF16)] * 2, [pair] * 2,
        flops=8 * batch * rows * width * units, traffic=20 * batch * rows * width,
    )
    return branch, second_grad, dw, jnp.concatenate([h[4] for h in hidden], axis=1)


def shards(
    size,
    images, cotangent, image_counts, skip_mask, first_gain, first_bias, token_in, token_in_bias,
    token_out, token_out_bias, second_gain, second_bias, channel_in, channel_in_bias, channel_out,
    channel_out_bias,
):
    batch, patches, width = images.shape
    tokens = token_in.shape[1]
    own = channel_in.shape[1]
    rows = -(-patches // 16) * 16
    units = own // 2
    half = units // 2
    pairs = batch // 2
    core = lax.axis_index("dp") & 1
    shape = jax.ShapeDtypeStruct
    packed = (batch, rows, width)
    block = patches * width
    anywhere = pl.BlockSpec(memory_space=pl.ANY)
    vmem = pl.BlockSpec(memory_space=pltpu.VMEM)
    smem = pl.BlockSpec(memory_space=pltpu.SMEM)
    dma = pltpu.SemaphoreType.DMA
    images_t, cotangent_t = jnp.transpose(images, (1, 0, 2)), jnp.transpose(cotangent, (1, 0, 2))
    split = pltpu.VMEM((width // 128, patches * batch, 128), F32)

    def row(vector):
        return jnp.pad(vector, (0, width - vector.shape[0]))

    vectors = jnp.stack([
        row(v) for v in (first_gain, first_bias, second_gain, second_bias, channel_out_bias, token_in_bias, token_out_bias)
    ])
    bias_row = channel_in_bias.reshape(1, own)

    moved = (MOVE, rows, width)
    meta, most, sent_images, sent_cotangents = pl.pallas_call(
        share_kernel,
        name="share",
        out_shape=[
            shape((VALID + batch,), jnp.int32), shape((1,), jnp.int32), shape(moved, BF16), shape(moved, BF16),
        ],
        in_specs=[smem, smem, vmem, vmem],
        out_specs=[smem, smem, vmem, vmem],
        scratch_shapes=[
            split, split, pltpu.VMEM((8, 128), jnp.int32), pltpu.VMEM((size, 8, 128), jnp.int32),
            pltpu.SMEM((size, 128), jnp.int32), dma((size,)), dma((size,)), dma,
        ],
        compiler_params=pltpu.CompilerParams(
            vmem_limit_bytes=VMEM_LIMIT, collective_id=SHARE_ID, has_side_effects=True
        ),
    )(image_counts, skip_mask, images_t, cotangent_t)
    got_images, got_cotangents = swap(sent_images, 1, size), swap(sent_cotangents, 1, size)

    whole_one = lambda array: pl.BlockSpec(array.shape, lambda j, meta: (0,) * array.ndim, pipeline_mode=pl.Buffered(1))
    any_pair = pl.BlockSpec((2, rows, width), lambda j, meta: (j, 0, 0))
    last_kept = lambda j, meta: jnp.minimum(j, jnp.maximum((meta[KEPT] + 1) // 2 - 1, 0))
    kept_pair = lambda r: pl.BlockSpec((2, r, width), lambda j, meta: (last_kept(j, meta), 0, 0))
    native = shape((patches, batch, width), F32)
    smalls = [
        shape((8, width), F32), shape((rows, tokens), BF16), shape((tokens, rows), BF16), shape((rows, tokens), BF16),
        shape((tokens, rows), BF16), shape((tokens, 1), F32), shape((rows, 1), F32),
    ]
    token_out_t = token_out.T
    (
        second, out_grad, middle, source, out_bias_grad, tin, tin_t, tout_t, tout, tin_bias, tout_bias, activations, input_grad,
    ) = call(
        token_forward_kernel, "token_forward", (pairs,),
        (meta, images_t, cotangent_t, vectors, token_in, token_out_t),
        [whole_one(v) for v in (images_t, cotangent_t, vectors, token_in, token_out_t)],
        [shape(packed, BF16), shape(packed, BF16), shape((batch, patches, width), F32), shape(packed, BF16)] + smalls + [native] * 2,
        [any_pair, any_pair, kept_pair(patches), kept_pair(rows)] + [whole_one(v) for v in smalls] + [anywhere] * 2,
        [split, split, pltpu.VMEM((2, 2, 2, patches, width), F32), dma((2, 2, 2))],
        flops=4 * batch * rows * width * tokens * 4, traffic=batch * block * 12,
    )
    second, out_grad, middle, source, out_bias_grad = pl.pallas_call(
        token_received_kernel,
        name="token_received",
        out_shape=[shape(packed, BF16), shape(packed, BF16), shape((batch, patches, width), F32), shape(packed, BF16), shape((8, width), F32)],
        in_specs=[smem] + [vmem] * 8 + [anywhere] * 4,
        out_specs=[anywhere] * 4 + [vmem],
        scratch_shapes=[
            pltpu.VMEM((rows, width), BF16), pltpu.VMEM((rows, width), BF16), pltpu.VMEM((patches, width), F32), dma((4,)),
        ],
        input_output_aliases={9: 0, 10: 1, 11: 2, 12: 3},
        compiler_params=pltpu.CompilerParams(vmem_limit_bytes=VMEM_LIMIT),
    )(
        meta, got_images, got_cotangents, vectors, tin_t, tin_bias, tout_t, tout_bias, out_bias_grad,
        second, out_grad, middle, source,
    )

    operands = (second, out_grad, channel_in, bias_row, channel_out)
    general = functools.partial(channel_general, size, meta, core)
    if size == 2 * RING:
        fast = [functools.partial(channel_call, p, i + 1) for i, p in enumerate(FAST_PAIRS)]
        branch_at = sum((most[0] > 2 * p).astype(jnp.int32) for p in FAST_PAIRS[:-1])
        branch, second_grad, dw, in_bias_grad = lax.switch(branch_at, fast, *operands)
    else:
        branch, second_grad, dw, in_bias_grad = general(*operands)

    def item_specs(own_items):
        def index(place):
            def at(j, meta):
                if own_items:
                    return jnp.minimum(2 * j + place, jnp.maximum(meta[KEPT] - 1, 0)), 0, 0
                return jnp.minimum(meta[KEPT] + jnp.minimum(2 * j + place, jnp.maximum(meta[RECEIVED] - 1, 0)), batch - 1), 0, 0
            return at
        return [pl.BlockSpec((1, r, width), index(place)) for r in (rows, rows, patches, rows, rows) for place in range(2)]

    items = [a for a in (source, out_grad, middle, branch, second_grad) for _ in range(2)]
    consts = (vectors, tin, tin_t, tin_bias, tout)
    sums = [
        shape((rows, tokens), F32), shape((tokens, 128), F32), shape((tokens, rows), F32), shape((rows, 128), F32),
        shape((4, 8, width), F32),
    ]
    stage = [pltpu.VMEM((2, 2, 2, patches, width), F32), dma((2, 2, 2))]
    returned = shape((patches, MOVE, width), F32)
    back_images, back_grads, *partial = call(
        functools.partial(token_backward_kernel, False), "token_backward_received", (MOVE // 2,),
        (meta, *items, *consts),
        item_specs(False) + [whole_one(c) for c in consts],
        [returned] * 2 + sums, [anywhere] * 2 + [whole_one(v) for v in sums],
        stage, flops=10 * MOVE * rows * width * tokens, traffic=MOVE * block * 24,
    )
    back_images, back_grads = swap(back_images, 1, size), swap(back_grads, 1, size)
    in_rows, out_rows = width // pairs, own // pairs
    in_turns, out_turns = half // in_rows, half // out_rows
    first_alias = 1 + len(items) + len(consts) + len(sums) + 3
    activations, input_grad, *partial, in_grad_sum, out_grad_sum = call(
        functools.partial(token_backward_kernel, True), "token_backward", (pairs,),
        (meta, *items, *consts, *partial, dw, dw, dw, activations, input_grad),
        item_specs(True) + [whole_one(c) for c in consts] + [whole_one(v) for v in sums]
        + [
            pl.BlockSpec((1, 1, 1, in_rows, width), lambda t, meta, c=c: (c, t // in_turns, 1, t % in_turns, 0))
            for c in range(2)
        ]
        + [pl.BlockSpec(
            (1, 1, 1, out_rows, width),
            lambda t, meta: (t // (2 * out_turns), (t // out_turns) % 2, 0, t % out_turns, 0),
        )]
        + [anywhere] * 2,
        [native] * 2 + sums + [shape((width, own), F32), shape((own, width), F32)],
        [anywhere] * 2 + [whole_one(v) for v in sums]
        + [pl.BlockSpec((in_rows, own), lambda t, meta: (t, 0)), pl.BlockSpec((out_rows, width), lambda t, meta: (t, 0))],
        stage, flops=10 * batch * rows * width * tokens, traffic=batch * block * 24,
        aliases={first_alias: 0, first_alias + 1: 1},
    )
    activations, input_grad = pl.pallas_call(
        place_kernel,
        name="place",
        out_shape=[native] * 2,
        in_specs=[smem] + [anywhere] * 4,
        out_specs=[anywhere] * 2,
        scratch_shapes=[pltpu.VMEM((2, MOVE, patches, width), F32), dma((2, 2, MOVE))],
        input_output_aliases={3: 0, 4: 1},
        compiler_params=pltpu.CompilerParams(vmem_limit_bytes=VMEM_LIMIT),
    )(meta, back_images, back_grads, activations, input_grad)
    activations, input_grad = jnp.transpose(activations, (1, 0, 2)), jnp.transpose(input_grad, (1, 0, 2))

    tin_grad, tin_bias_grad, tout_grad, tout_bias_grad, gains = partial
    if size == 2 * RING:
        lines = [tokens, patches, width, width, width, width, own, width]
        sums = pl.pallas_call(
            small_sum_kernel,
            name="small_sum",
            out_shape=[shape((patches, tokens), F32), shape((tokens, patches), F32)] + [shape((1, n), F32) for n in lines],
            in_specs=[vmem] * 7,
            out_specs=[vmem] * 10,
            scratch_shapes=[
                pltpu.VMEM((2, PACKED // 2, width), F32), pltpu.VMEM((PACKED // 2, width), F32),
                pltpu.VMEM((PACKED // 2, width), BF16), pltpu.VMEM((PACKED // 2, width), BF16),
                pltpu.VMEM((PACKED // 2, width), BF16), pltpu.VMEM((RING, PACKED // 2 // RING, width), BF16),
                dma((4,)), dma((RING,)), dma((RING,)), dma((RING,)), dma((RING,)),
            ],
            compiler_params=pltpu.CompilerParams(
                vmem_limit_bytes=VMEM_LIMIT, collective_id=SUM_ID, has_side_effects=True
            ),
        )(tin_grad, tout_grad, tin_bias_grad, tout_bias_grad, gains, in_bias_grad, out_bias_grad)
        tin_sum, tout_sum, tin_b, tout_b, gain1, shift1, gain2, shift2, in_b, out_b = [
            v.reshape(-1) if v.shape[0] == 1 else v for v in sums
        ]
        small = (gain1, shift1, tin_sum, tin_b, tout_sum, tout_b, gain2, shift2, in_b, out_b)
    else:
        gains = jnp.sum(gains, axis=1)
        small = lax.psum(
            (
                gains[2], gains[3], tin_grad[:patches], jnp.sum(tin_bias_grad, axis=1),
                tout_grad[:, :patches], jnp.sum(tout_bias_grad, axis=1)[:patches], gains[0], gains[1],
                jnp.sum(in_bias_grad, axis=0), jnp.sum(out_bias_grad, axis=0),
            ),
            "dp",
        )
    return (activations, input_grad, *small[:8], in_grad_sum, small[8], out_grad_sum, small[9])


def solution(mesh):
    placed = (
        P("dp", None, None), P("dp", None, None), P("dp"), P("dp"), P(), P(), P(), P(), P(), P(), P(), P(),
        P(None, "tp"), P("tp"), P("tp", None), P(),
    )
    return jax.shard_map(
        functools.partial(shards, mesh.shape["dp"]),
        mesh=mesh,
        in_specs=placed,
        out_specs=(
            P("dp", None, None), P("dp", None, None), P(), P(), P(), P(), P(), P(), P(), P(),
            P(None, "tp"), P("tp"), P("tp", None), P(),
        ),
        check_vma=False,
    )
```

```python
import functools

import jax
import jax.numpy as jnp
from jax import lax
from jax.experimental import pallas as pl
from jax.experimental.pallas import tpu as pltpu
from jax.sharding import PartitionSpec as P

EPSILON = 1e-06
ROOT_HALF = 0.7071067811865476
INV_ROOT_TAU = 0.3989422804014327
F32, BF16 = jnp.float32, jnp.bfloat16
VMEM_LIMIT = 60 * 1024 * 1024
CHANNEL_VMEM = 60 * 1024 * 1024
RING, SEG, LAST_TURN = 8, 48, 9
FAST_PAIRS = (5, 6, 8)
SHARE_ID, SUM_ID = 9, 10
PACKED = 256

MOVE = 4
N_LIVE, KEPT, RECEIVED, N_PAIRS, CORE, GIVEN, LIST, VALID = 0, 1, 2, 3, 4, 5, 8, 24
GAIN1, SHIFT1, GAIN2, SHIFT2, OUT_BIAS, TIN_BIAS, TOUT_BIAS = range(7)


def dot(left, right, left_dim, right_dim):
    return lax.dot_general(
        left, right, (((left_dim,), (right_dim,)), ((), ())), preferred_element_type=F32
    )


def gelu_parts(values):
    half = 0.5 * (1.0 + lax.erf(values * ROOT_HALF))
    slope = half + values * (INV_ROOT_TAU * jnp.exp(-0.5 * values * values))
    return (values * half).astype(BF16), slope


def gelu_only(values):
    return (values * (0.5 * (1.0 + lax.erf(values * ROOT_HALF)))).astype(BF16)


def standardize(values):
    width = values.shape[-1]
    center = jnp.sum(values, axis=-1, keepdims=True) * (1.0 / width)
    deviation = values - center
    scale = lax.rsqrt(
        jnp.sum(deviation * deviation, axis=-1, keepdims=True) * (1.0 / width) + EPSILON
    )
    return deviation * scale, scale


def norm_back(grad_hat, hat, scale):
    width = hat.shape[-1]
    first = jnp.sum(grad_hat, axis=-1, keepdims=True) * (1.0 / width)
    second = jnp.sum(grad_hat * hat, axis=-1, keepdims=True) * (1.0 / width)
    return scale * (grad_hat - first - hat * second)


def pad_rows(values, rows):
    return jnp.concatenate(
        [values, jnp.zeros((rows - values.shape[0], values.shape[1]), values.dtype)], axis=0
    )


def row_sums(values):
    rows, width = values.shape
    return jnp.sum(values.reshape(rows // 8, 8, width), axis=0)


def lane_sums(values):
    total = values[:, :128]
    for at in range(128, values.shape[1], 128):
        total = total + values[:, at : at + 128]
    return total


def split_lanes(source, target, pieces):
    patches, images, width = source.shape
    step = patches // pieces
    for piece in range(pieces):
        rows = source[piece * step : (piece + 1) * step].astype(F32).reshape(step * images, width)
        for group in range(width // 128):
            target[group, piece * step * images : (piece + 1) * step * images, :] = rows[:, group * 128 : (group + 1) * 128]


def one_image(split, index, images):
    patches = split.shape[1] // images
    return jnp.concatenate(
        [split[group, pl.ds(index, patches, stride=images), :] for group in range(split.shape[0])], axis=1
    )


def share_kernel(
    counts, skips, images, cotangents, meta, most, sent_images, sent_cotangents,
    x_split, c_split, mine, gathered, gathered_smem, send_sem, recv_sem, local_sem,
):
    slots = images.shape[1]
    rows = sent_images.shape[1]
    size = gathered.shape[0]
    me = lax.axis_index("dp")
    barrier = pltpu.get_barrier_semaphore()

    def peer(step):
        return {"dp": lax.rem(me + step, size)}

    for step in range(1, size):
        pl.semaphore_signal(barrier, inc=1, device_id=peer(step), device_id_type=pl.DeviceIdType.MESH)
    one, none = jnp.int32(1), jnp.int32(0)
    valid, live, rank, total = [], [], [], none
    for slot in range(slots):
        valid.append(jnp.where(slot < counts[0], one, none))
        live.append(valid[slot] * skips[slot])
        rank.append(total)
        total = total + live[slot]
    mine[...] = jnp.zeros_like(mine) + total
    gathered[me] = mine[...]
    pl.semaphore_wait(barrier, size - 1)

    def send(step):
        return pltpu.make_async_remote_copy(
            src_ref=mine, dst_ref=gathered.at[me], send_sem=send_sem.at[step], recv_sem=recv_sem.at[step],
            device_id=peer(step), device_id_type=pl.DeviceIdType.MESH,
        )

    for step in range(1, size):
        send(step).start()
    split_lanes(images, x_split, 14)
    split_lanes(cotangents, c_split, 14)
    place_of = [jnp.where(live[slot] == 1, rank[slot], total + slot - rank[slot]) for slot in range(slots)]
    for place in range(slots):
        index, ok = none, none
        for slot in range(slots):
            hit = jnp.where(place_of[slot] == place, one, none)
            index = index + hit * slot
            ok = ok + hit * valid[slot]
        meta[LIST + place] = index
        meta[VALID + place] = ok
    for place in range(MOVE):
        index = none
        for slot in range(slots):
            index = index + slot * live[slot] * jnp.where(rank[slot] == total - 1 - place, one, none)
        sent_images[place] = pad_rows(one_image(x_split, index, slots), rows).astype(BF16)
        sent_cotangents[place] = pad_rows(one_image(c_split, index, slots), rows).astype(BF16)
    for step in range(1, size):
        send(step).wait()
    local = pltpu.make_async_copy(gathered.at[:, 0, :], gathered_smem, local_sem)
    local.start()
    local.wait()

    def excess(left, right):
        return jnp.clip(lax.shift_right_arithmetic(left - right, one), 0, MOVE)

    fullest = none
    for chip in range(size // 2):
        left, right = gathered_smem[2 * chip, 0], gathered_smem[2 * chip + 1, 0]
        shift = excess(left, right) - excess(right, left)
        fullest = jnp.maximum(fullest, jnp.maximum(left - shift, right + shift))
    most[0] = fullest
    sibling = me + 1 - 2 * lax.rem(me, 2)
    there = gathered_smem[sibling, 0]
    given, received = excess(total, there), excess(there, total)
    kept = total - given
    for at, value in (
        (N_LIVE, total), (KEPT, kept), (RECEIVED, received),
        (N_PAIRS, lax.shift_right_arithmetic(kept + received + 1, one)), (CORE, lax.rem(me, 2)), (GIVEN, given),
    ):
        meta[at] = value


def column(row):
    return jnp.transpose(jnp.broadcast_to(row, (8, row.shape[1])))[:, :1]


def token_forward(sources, grads, vectors, tin_t, tin_bias, tout_t, tout_bias, rows):
    patches = sources[0].shape[0]
    normed = [
        pad_rows(standardize(x)[0] * vectors[GAIN1 : GAIN1 + 1] + vectors[SHIFT1 : SHIFT1 + 1], rows).astype(BF16)
        for x in sources
    ]
    pre = [dot(tin_t[...], n, 1, 0) + tin_bias[...] for n in normed]
    act = [gelu_only(p) for p in pre]
    branch = [dot(tout_t[...], a, 1, 0)[:patches] + tout_bias[:patches] for a in act]
    middle = [x + b for x, b in zip(sources, branch)]
    second = [
        pad_rows(standardize(m)[0] * vectors[GAIN2 : GAIN2 + 1] + vectors[SHIFT2 : SHIFT2 + 1], rows) for m in middle
    ]
    return middle, second, [pad_rows(g, rows) for g in grads]


def token_forward_kernel(
    meta, images, cotangents, vectors, tin, tout_in,
    second, out_grad, middle, source, grad_sum, tin_pad, tin_t, tout_t, tout, tin_bias, tout_bias, activations, input_grad,
    x_split, c_split, fill, fill_sem,
):
    step = pl.program_id(0)
    steps = pl.num_programs(0)
    rows = second.shape[1]
    slots = images.shape[1]

    @pl.when(step == 0)
    def _():
        grad_sum[...] = jnp.zeros_like(grad_sum)
        wide = pad_rows(tin[...].astype(F32), rows)
        tin_pad[...] = wide.astype(BF16)
        tin_t[...] = jnp.transpose(wide).astype(BF16)
        wide = pad_rows(tout_in[...].astype(F32), rows)
        tout_t[...] = wide.astype(BF16)
        tout[...] = jnp.transpose(wide).astype(BF16)
        tin_bias[...] = column(vectors[TIN_BIAS : TIN_BIAS + 1, : tin_bias.shape[0]])
        tout_bias[...] = column(vectors[TOUT_BIAS : TOUT_BIAS + 1, : tout_bias.shape[0]])
        split_lanes(images, x_split, 14)
        split_lanes(cotangents, c_split, 14)

    def run(places):
        at = [meta[LIST + 2 * step + place] for place in places]
        sources = [one_image(x_split, index, slots) for index in at]
        grads = [one_image(c_split, index, slots) for index in at]
        mid, sec, gra = token_forward(sources, grads, vectors, tin_t, tin_bias, tout_t, tout_bias, rows)
        for place, m, s, g, x in zip(places, mid, sec, gra, sources):
            middle[place] = m
            second[place] = s.astype(BF16)
            out_grad[place] = g.astype(BF16)
            source[place] = pad_rows(x, rows).astype(BF16)
            grad_sum[...] += row_sums(g)

    @pl.when(2 * step + 1 < meta[KEPT])
    def _():
        run((0, 1))

    @pl.when(2 * step + 1 == meta[KEPT])
    def _():
        run((0,))
        second[1] = jnp.zeros_like(second[1])
        out_grad[1] = jnp.zeros_like(out_grad[1])

    @pl.when(2 * step >= meta[KEPT])
    def _():
        second[...] = jnp.zeros_like(second)
        out_grad[...] = jnp.zeros_like(out_grad)

    def copies(at_step, place):
        slot = lax.rem(at_step, 2)
        index = meta[LIST + 2 * at_step + place]
        return (
            pltpu.make_async_copy(fill.at[slot, place, 0], activations.at[:, index, :], fill_sem.at[slot, place, 0]),
            pltpu.make_async_copy(fill.at[slot, place, 1], input_grad.at[:, index, :], fill_sem.at[slot, place, 1]),
        )

    for place in range(2):

        @pl.when((step >= 2) & (2 * (step - 2) + place >= meta[N_LIVE]))
        def _():
            for copy in copies(step - 2, place):
                copy.wait()

        @pl.when(2 * step + place >= meta[N_LIVE])
        def _():
            index = meta[LIST + 2 * step + place]
            valid = meta[VALID + 2 * step + place].astype(F32)
            slot = lax.rem(step, 2)
            fill[slot, place, 0] = valid * one_image(x_split, index, slots)
            fill[slot, place, 1] = valid * one_image(c_split, index, slots)
            for copy in copies(step, place):
                copy.start()

        @pl.when((step == steps - 1) & (2 * (step - 1) + place >= meta[N_LIVE]))
        def _():
            for copy in copies(step - 1, place):
                copy.wait()

        @pl.when((step == steps - 1) & (2 * step + place >= meta[N_LIVE]))
        def _():
            for copy in copies(step, place):
                copy.wait()


def token_received_kernel(
    meta, images, cotangents, vectors, tin_t, tin_bias, tout_t, tout_bias, grad_sum_in,
    second_in, out_grad_in, middle_in, source_in,
    second, out_grad, middle, source, grad_sum,
    second_one, grad_one, middle_one, sem,
):
    grad_sum[...] = grad_sum_in[...]
    rows = second_one.shape[0]
    patches = middle_one.shape[0]

    @pl.loop(0, meta[RECEIVED])
    def _(place):
        x = images[place, :patches].astype(F32)
        mid, sec, gra = token_forward(
            [x], [cotangents[place, :patches].astype(F32)], vectors, tin_t, tin_bias, tout_t, tout_bias, rows
        )
        second_one[...] = sec[0].astype(BF16)
        grad_one[...] = gra[0].astype(BF16)
        middle_one[...] = mid[0]
        grad_sum[...] += row_sums(gra[0])
        index = meta[KEPT] + place
        copies = [
            pltpu.make_async_copy(src, dst.at[index], sem.at[number])
            for number, (src, dst) in enumerate((
                (second_one, second), (grad_one, out_grad), (middle_one, middle), (images.at[place], source),
            ))
        ]
        for copy in copies:
            copy.start()
        for copy in copies:
            copy.wait()


def hidden_kernel(
    sub, meta, second, out_grad, win, win_bias, wout,
    act_out, pre_grad_out, sent, kept, bias_grad, wout_grad, win_grad,
):
    step, steps = pl.program_id(0), pl.num_programs(0)

    @pl.when(step == 0)
    def _():
        wout_grad[...] = jnp.zeros_like(wout_grad)
        win_grad[...] = jnp.zeros_like(win_grad)
        bias_grad[...] = jnp.zeros_like(bias_grad)

    @pl.when(step < meta[N_PAIRS])
    def _():
        pair, rows, width = second.shape
        s = second[...].reshape(pair * rows, width)
        g = out_grad[...].reshape(pair * rows, width)

        def head(at):
            cut = slice(at, at + sub)
            return dot(s, win[:, cut], 1, 0) + win_bias[:, cut], dot(g, wout[cut, :], 1, 1)

        units = win.shape[1]
        ahead = head(0)
        for at in range(0, units, sub):
            pre, act_grad = ahead
            if at + sub < units:
                ahead = head(at + sub)
            act, slope = gelu_parts(pre)
            grad = act_grad * slope
            pre_grad = grad.astype(BF16)
            cut = slice(at, at + sub)
            act_out[:, :, cut] = act.reshape(pair, rows, sub)
            pre_grad_out[:, :, cut] = pre_grad.reshape(pair, rows, sub)
            bias_grad[:, cut] += row_sums(pre_grad.astype(F32))
            wout_grad[cut, :] += dot(act, g, 0, 0)
            win_grad[:, cut] += dot(s, pre_grad, 0, 0)

    @pl.when(step == steps - 1)
    def _():
        half = kept.shape[1]
        mine = pl.ds(pl.multiple_of(meta[CORE] * half, half), half)
        other = pl.ds(pl.multiple_of((1 - meta[CORE]) * half, half), half)
        kept[0] = wout_grad[mine, :].astype(BF16)
        kept[1] = win_grad[mine, :].astype(BF16)
        sent[0] = wout_grad[other, :].astype(BF16)
        sent[1] = win_grad[other, :].astype(BF16)


def far_units(sub, s, g, win, win_bias, wout, out, grad_out):
    def head(at):
        cut = slice(at, at + sub)
        return dot(s, win[:, cut], 1, 0) + win_bias[:, cut], dot(g, wout[cut, :], 1, 1)

    units = win.shape[1]
    ahead = head(0)
    for at in range(0, units, sub):
        pre, act_grad = ahead
        if at + sub < units:
            ahead = head(at + sub)
        act, slope = gelu_parts(pre)
        pre_grad = (act_grad * slope).astype(BF16)
        cut = slice(at, at + sub)
        more, more_grad = dot(act, wout[cut, :], 1, 0), dot(pre_grad, win[:, cut], 1, 1)
        out = more if out is None else out + more
        grad_out = more_grad if grad_out is None else grad_out + more_grad
    return out, grad_out


def far_first_kernel(
    sub, meta, second, out_grad, act0, grad0, act1, grad1, win_own, wout_own, win, win_bias, wout,
    out_part, grad_part,
):
    step = pl.program_id(0)

    @pl.when(step < meta[N_PAIRS])
    def _():
        pair, rows, width = second.shape
        flat = (pair * rows, width)
        s, g = second[...].reshape(flat), out_grad[...].reshape(flat)
        units = win.shape[1]
        out, grad_out = far_units(sub, s, g, win, win_bias, wout, None, None)
        for index, (act, pre_grad) in enumerate(((act0, grad0), (act1, grad1))):
            cut = slice(index * units, (index + 1) * units)
            out = out + dot(act[...].reshape(flat), wout_own[cut, :], 1, 0)
            grad_out = grad_out + dot(pre_grad[...].reshape(flat), win_own[:, cut], 1, 1)
        out_part[...] = out.reshape(pair, rows, width)
        grad_part[...] = grad_out.reshape(pair, rows, width)


def far_last_kernel(
    sub, meta, second, out_grad, out_part, grad_part, win, win_bias, wout, branch, second_grad,
):
    step = pl.program_id(0)

    @pl.when(step < meta[N_PAIRS])
    def _():
        pair, rows, width = second.shape
        flat = (pair * rows, width)
        s, g = second[...].reshape(flat), out_grad[...].reshape(flat)
        out, grad_out = far_units(
            sub, s, g, win, win_bias, wout, out_part[...].reshape(flat), grad_part[...].reshape(flat)
        )
        branch[...] = out.reshape(pair, rows, width).astype(BF16)
        second_grad[...] = grad_out.reshape(pair, rows, width).astype(BF16)


def token_backward_kernel(
    own, meta, *refs,
):
    items = [refs[2 * number : 2 * number + 2] for number in range(5)]
    images, grads, middles, branches, second_grads = items
    vectors, tin, tin_t, tin_bias, tout = refs[10:15]
    refs = refs[15:]
    if own:
        sums_in, refs = refs[:5], refs[5:]
        dw_in0, dw_in1, dw_out = refs[:3]
        refs = refs[5:]
    activations, input_grad = refs[:2]
    sums = refs[2:7]
    refs = refs[7:]
    if own:
        win_grad, wout_grad = refs[:2]
        refs = refs[2:]
    stage, stage_sem = refs
    tin_grad, tin_bias_grad, tout_grad, tout_bias_grad, gains = sums
    step, steps = pl.program_id(0), pl.num_programs(0)
    patches, rows = middles[0].shape[1], images[0].shape[1]
    count = meta[KEPT] if own else meta[RECEIVED]

    @pl.when(step == 0)
    def _():
        for number, ref in enumerate(sums):
            ref[...] = sums_in[number][...] if own else jnp.zeros_like(ref)

    if own:
        units = dw_in0.shape[-1]
        win_grad[:, :units] = dw_in0[...].reshape(win_grad.shape[0], units).astype(F32)
        win_grad[:, units:] = dw_in1[...].reshape(win_grad.shape[0], units).astype(F32)
        wout_grad[...] = dw_out[...].reshape(wout_grad.shape).astype(F32)

    def copies(at_step, place):
        slot = lax.rem(at_step, 2)
        item = 2 * at_step + place
        if own:
            index = meta[LIST + item]
            targets = (activations.at[:, index, :], input_grad.at[:, index, :])
        else:
            targets = (activations.at[:, item, :], input_grad.at[:, item, :])
        return [
            pltpu.make_async_copy(stage.at[slot, place, number], target, stage_sem.at[slot, place, number])
            for number, target in enumerate(targets)
        ]

    def vector(row):
        return vectors[row : row + 1]

    def run(places):
        slot = lax.rem(step, 2)
        middle = [middles[p][0] for p in places]
        norm2 = [standardize(m) for m in middle]
        grad2 = [second_grads[p][0].astype(F32)[:patches] for p in places]
        middle_grad = [
            grads[p][0].astype(F32)[:patches] + norm_back(g * vector(GAIN2), hat, scale)
            for p, g, (hat, scale) in zip(places, grad2, norm2)
        ]
        branch_grad = [pad_rows(m, rows).astype(BF16) for m in middle_grad]
        norm1 = [standardize(images[p][0].astype(F32)[:patches]) for p in places]
        normed = [pad_rows(hat * vector(GAIN1) + vector(SHIFT1), rows).astype(BF16) for hat, _ in norm1]
        pre = [dot(tin_t[...], n, 1, 0) + tin_bias[...] for n in normed]
        act_grad = [dot(tout[...], b, 1, 0) for b in branch_grad]
        parts = [gelu_parts(p) for p in pre]
        pre_grad = [(a * slope).astype(BF16) for a, (_, slope) in zip(act_grad, parts)]
        normed_grad = [dot(tin[...], p, 1, 0)[:patches] for p in pre_grad]
        for p, m in zip(places, middle):
            stage[slot, p, 0] = m + (branches[p][0].astype(F32)[:patches] + vector(OUT_BIAS))
        for p, m, n, (hat, scale) in zip(places, middle_grad, normed_grad, norm1):
            stage[slot, p, 1] = m + norm_back(n * vector(GAIN1), hat, scale)
        for p in places:
            for copy in copies(step, p):
                copy.start()
        tout_grad[...] += sum(dot(b, act, 1, 1) for (act, _), b in zip(parts, branch_grad))
        tin_grad[...] += sum(dot(n, p, 1, 1) for n, p in zip(normed, pre_grad))
        tin_bias_grad[...] += sum(lane_sums(p.astype(F32)) for p in pre_grad)
        tout_bias_grad[...] += sum(lane_sums(b.astype(F32)) for b in branch_grad)
        gains[0] += sum(row_sums(pad_rows(g * hat, rows)) for g, (hat, _) in zip(grad2, norm2))
        gains[1] += sum(row_sums(pad_rows(g, rows)) for g in grad2)
        gains[2] += sum(row_sums(pad_rows(n * hat, rows)) for n, (hat, _) in zip(normed_grad, norm1))
        gains[3] += sum(row_sums(pad_rows(n, rows)) for n in normed_grad)

    for place in range(2):

        @pl.when((step >= 2) & (2 * (step - 2) + place < count))
        def _():
            for copy in copies(step - 2, place):
                copy.wait()

    @pl.when(2 * step + 1 < count)
    def _():
        run((0, 1))

    @pl.when(2 * step + 1 == count)
    def _():
        run((0,))

    for place in range(2):
        for back in (1, 0):

            @pl.when((step == steps - 1) & (step >= back) & (2 * (step - back) + place < count))
            def _():
                for copy in copies(step - back, place):
                    copy.wait()


def place_kernel(
    meta, images, grads, activations_in, input_grad_in, summed,
    activations, input_grad,
    tin_out, tout_out, tin_bias_out, tout_bias_out, gain1_out, shift1_out, gain2_out, shift2_out, in_bias_out, out_bias_out,
    held, sem,
):
    def loads(place):
        return [
            pltpu.make_async_copy(back.at[:, place, :], held.at[number, place], sem.at[0, number, place])
            for number, back in enumerate((images, grads))
        ]

    def stores(place):
        index = meta[LIST + meta[N_LIVE] - 1 - place]
        return [
            pltpu.make_async_copy(held.at[number, place], out.at[:, index, :], sem.at[1, number, place])
            for number, out in enumerate((activations, input_grad))
        ]

    @pl.loop(0, meta[GIVEN])
    def _(place):
        for copy in loads(place):
            copy.start()

    patches, tokens = tin_out.shape
    rows = -(-patches // 16) * 16
    width = summed.shape[1]
    unfold = lambda v: jnp.concatenate([v[:, :tokens], v[:, tokens:]], axis=0)[:patches]
    tin_out[...] = unfold(summed[: rows // 2])
    tout_out[...] = unfold(summed[rows // 2 : rows])

    def vector(number, length=width):
        row = summed[rows + number : rows + number + 1]
        return jnp.concatenate([row[:, at : at + 128] for at in range(0, length, 128)], axis=0)

    gain2_out[...], shift2_out[...], gain1_out[...], shift1_out[...] = (vector(number) for number in range(4))
    in_bias_out[...] = jnp.concatenate([vector(4), vector(5)], axis=0)
    out_bias_out[...] = vector(6)
    tin_bias_out[...] = vector(7, tokens)
    tout_bias_out[...] = vector(8, patches)

    @pl.loop(0, meta[GIVEN])
    def _(place):
        for load, store in zip(loads(place), stores(place)):
            load.wait()
            store.start()

    @pl.loop(0, meta[GIVEN])
    def _(place):
        for copy in stores(place):
            copy.wait()


def pack_small(tin_grad, tout_grad, tin_bias_grad, tout_bias_grad, gains, in_bias_grad, out_bias_grad):
    rows, width = tin_grad.shape[0], out_bias_grad.shape[1]
    line = lambda v: jnp.sum(v, axis=0, keepdims=True)
    flat = lambda v: jnp.concatenate([v, jnp.zeros((1, width - v.shape[1]), F32)], axis=1)
    fold = lambda v: jnp.concatenate([v[: rows // 2], v[rows // 2 :]], axis=1)
    vectors = [line(gains[number]) for number in range(4)]
    in_bias = line(in_bias_grad)
    vectors += [in_bias[:, :width], in_bias[:, width:], line(out_bias_grad)]
    vectors += [flat(line(jnp.transpose(tin_bias_grad))), flat(line(jnp.transpose(tout_bias_grad)))]
    return jnp.concatenate(
        [fold(tin_grad), fold(tout_grad)] + vectors + [jnp.zeros((PACKED - rows - len(vectors), width), F32)], axis=0
    )


def small_sum_kernel(
    tin_grad, tout_grad, tin_bias_grad, tout_bias_grad, gains, in_bias_grad, out_bias_grad,
    summed,
    packed, landed, reduced, gathered, other, pieces, core_sem, sum_send, sum_recv, gather_send, gather_recv,
):
    width = packed.shape[-1]
    rows = tin_grad.shape[0]
    me = lax.axis_index("dp")
    core, chip = lax.rem(me, 2), lax.div(me, 2)
    sibling = me + 1 - 2 * core

    def chip_at(step):
        return lax.rem(chip + step, RING)

    def peer(step):
        return {"dp": 2 * chip_at(step) + core}

    barrier = pltpu.get_barrier_semaphore()
    for near in [{"dp": sibling}] + [peer(step) for step in range(1, RING)]:
        pl.semaphore_signal(barrier, inc=1, device_id=near, device_id_type=pl.DeviceIdType.MESH)

    def remote(src, dst, send, recv, device):
        return pltpu.make_async_remote_copy(
            src_ref=src, dst_ref=dst, send_sem=send, recv_sem=recv, device_id=device,
            device_id_type=pl.DeviceIdType.MESH,
        )

    everything = pack_small(
        tin_grad[...], tout_grad[...], tin_bias_grad[...], tout_bias_grad[...], gains[...], in_bias_grad[...], out_bias_grad[...]
    )
    packed[0] = everything[: PACKED // 2]
    packed[1] = everything[PACKED // 2 :]
    pl.semaphore_wait(barrier, RING)

    swap_copy = remote(packed.at[1 - core], landed, core_sem.at[0], core_sem.at[1], {"dp": sibling})
    swap_copy.start()
    swap_copy.wait()
    packed[core] = packed[core] + landed[...]
    reduced[...] = packed[core].astype(BF16)
    piece = PACKED // 2 // RING

    def segment(ref, index):
        return ref.at[pl.ds(pl.multiple_of(index * piece, piece), piece)]

    def sum_copy(step):
        return remote(segment(reduced, chip_at(step)), pieces.at[step], sum_send.at[step], sum_recv.at[step], peer(step))

    for step in range(1, RING):
        sum_copy(step).start()
    total = segment(packed.at[core], chip)[...]
    for step in range(1, RING):
        sum_copy(step).wait()
        total = total + pieces[step].astype(F32)
    pieces[0] = total.astype(BF16)

    def gather_copy(step):
        return remote(
            pieces.at[0], segment(gathered, chip), gather_send.at[step], gather_recv.at[step], peer(step)
        )

    for step in range(1, RING):
        gather_copy(step).start()
    segment(gathered, chip)[...] = pieces[0]
    for step in range(1, RING):
        gather_copy(step).wait()
    back_copy = remote(gathered, other, core_sem.at[2], core_sem.at[3], {"dp": sibling})
    back_copy.start()
    back_copy.wait()
    summed[: PACKED // 2] = jnp.where(core == 0, gathered[...], other[...]).astype(F32)
    summed[PACKED // 2 :] = jnp.where(core == 0, other[...], gathered[...]).astype(F32)


def last_pair(step, meta):
    return jnp.minimum(step, jnp.maximum(meta[N_PAIRS] - 1, 0))


def pair_spec(rows, width):
    return pl.BlockSpec((2, rows, width), lambda j, meta: (last_pair(j, meta), 0, 0))


def whole_spec(array):
    zeros = (0,) * array.ndim
    return pl.BlockSpec(array.shape, lambda j, meta: zeros)


def call(body, name, grid, args, in_specs, outs, out_specs, scratch=(), flops=0, traffic=0, aliases={}):
    return pl.pallas_call(
        body,
        name=name,
        out_shape=outs,
        grid_spec=pltpu.PrefetchScalarGridSpec(
            num_scalar_prefetch=1,
            grid=grid,
            in_specs=in_specs,
            out_specs=out_specs,
            scratch_shapes=scratch,
        ),
        input_output_aliases=aliases,
        cost_estimate=pl.CostEstimate(flops=flops, bytes_accessed=traffic, transcendentals=0),
        compiler_params=pltpu.CompilerParams(
            vmem_limit_bytes=VMEM_LIMIT, dimension_semantics=("arbitrary",)
        ),
    )(*args)


def swap(value, bit, size):
    return lax.ppermute(value, "dp", [(i, i ^ bit) for i in range(size)])


def sum_over_dp(kept, sent, size):
    me = lax.axis_index("dp")
    core, bit1, rest = me & 1, (me >> 1) & 1, me >> 2
    groups = size // 4
    total = kept.astype(F32) + swap(sent, 1, size).astype(F32)
    mine = jnp.where(bit1 == 0, total[0], total[1])
    other = jnp.where(bit1 == 0, total[1], total[0]).astype(BF16)
    total = mine + swap(other, 2, size).astype(F32)
    rows, width = total.shape
    pieces = total.astype(BF16).reshape(groups, rows // groups, width)
    if groups <= 4:
        arrived = [
            swap(lax.dynamic_index_in_dim(pieces, rest ^ k, keepdims=False), 4 * k, size)
            for k in range(1, groups)
        ]
        piece = lax.dynamic_index_in_dim(
            total.reshape(groups, rows // groups, width), rest, keepdims=False
        )
        for other in arrived:
            piece = piece + other.astype(F32)
        piece = piece.astype(BF16)
        whole = jnp.zeros((groups, rows // groups, width), BF16)
        whole = lax.dynamic_update_index_in_dim(whole, piece, rest, 0)
        for k in range(1, groups):
            whole = lax.dynamic_update_index_in_dim(whole, swap(piece, 4 * k, size), rest ^ k, 0)
    else:
        teams = [[4 * r + low for r in range(groups)] for low in range(4)]
        arrived = lax.all_to_all(pieces, "dp", 0, 0, axis_index_groups=teams)
        piece = jnp.sum(arrived.astype(F32), axis=0).astype(BF16)
        whole = lax.all_gather(piece, "dp", axis_index_groups=teams)
    part = whole.reshape(rows, width)
    far = swap(part, 2, size)
    both = jnp.where(bit1 == 0, jnp.stack([part, far]), jnp.stack([far, part]))
    far = swap(both, 1, size)
    return jnp.where(core == 0, jnp.stack([both, far]), jnp.stack([far, both]))


def channel_kernel(
    sub, second_hbm, grad_hbm, win_hbm, wout_hbm, bias,
    branch_hbm, second_grad_hbm, dw_hbm, bias_grad,
    s_all, g_all, acts, grads, w_own, w_far, bias_far, dw, traded, starts, hops,
    load_sem, out_sem, bias_sem, far_sem, core_sem, result_sem, ring_send, ring_recv, free_sem,
):
    pairs, _, rows, width = s_all.shape
    units = width
    half = units // 2
    flat = (2 * rows, width)
    packed = (2, rows, width)
    me = lax.axis_index("dp")
    core, y, z = lax.rem(me, 2), lax.rem(lax.div(me, 2), 2), lax.div(me, 4)
    tp = lax.axis_index("tp")
    at = y * 4 + z + y * (3 - 2 * z)

    def device_at(place):
        place = lax.rem(place + RING, RING)
        row = lax.div(place, 4)
        col = lax.rem(place, 4)
        return (col + row * (3 - 2 * col)) * 4 + row * 2 + core

    sibling = me + 1 - 2 * core
    ahead_device, behind_device = device_at(at + 1), device_at(at - 1)

    barrier = pltpu.get_barrier_semaphore()
    for near in ({"dp": sibling}, {"dp": ahead_device}, {"dp": behind_device}, {"tp": 1 - tp}):
        pl.semaphore_signal(barrier, inc=1, device_id=near, device_id_type=pl.DeviceIdType.MESH)
    pl.semaphore_wait(barrier, 4)

    def remote(src, dst, send, recv, device):
        return pltpu.make_async_remote_copy(
            src_ref=src, dst_ref=dst, send_sem=send, recv_sem=recv, device_id=device,
            device_id_type=pl.DeviceIdType.MESH,
        )

    def weight_loads(chunk):
        cut = pl.ds(chunk * units, units)
        return (
            pltpu.make_async_copy(wout_hbm.at[cut, :], w_own.at[0, chunk], load_sem.at[chunk, 0]),
            pltpu.make_async_copy(win_hbm.at[:, cut], w_own.at[1, chunk], load_sem.at[chunk, 1]),
        )

    row_loads = (
        pltpu.make_async_copy(second_hbm.at[pl.ds(0, pairs)], s_all, load_sem.at[2, 0]),
        pltpu.make_async_copy(grad_hbm.at[pl.ds(0, pairs)], g_all, load_sem.at[2, 1]),
    )
    for load in (*weight_loads(0), *row_loads, *weight_loads(1)):
        load.start()

    def far_copy(chunk):
        return remote(
            w_own.at[core, chunk], w_far.at[core, chunk], far_sem.at[0, chunk], far_sem.at[1, chunk], {"tp": 1 - tp}
        )

    def pass_copy(chunk):
        return remote(
            w_far.at[core, chunk], w_far.at[core, chunk], far_sem.at[2, chunk], far_sem.at[3, chunk], {"dp": sibling}
        )

    bias_copy = remote(bias, bias_far, bias_sem.at[0], bias_sem.at[1], {"tp": 1 - tp})
    bias_copy.start()
    for load in weight_loads(0):
        load.wait()
    far_copy(0).start()
    bias_grad[...] = jnp.zeros_like(bias_grad)
    for load in row_loads:
        load.wait()

    def reach(matrix, way):
        return 3 + jnp.where(matrix == way, 1, 0)

    def segment(chunk, matrix, index):
        index = lax.rem(index + 2 * RING, RING)
        return dw.at[chunk, core, pl.ds(pl.multiple_of(matrix * half + index * SEG, SEG), SEG)]

    def sign(way):
        return 1 - 2 * way

    def toward(way):
        return {"dp": jnp.where(way == 0, ahead_device, behind_device)}

    def part_of(ref, chunk, matrix, which):
        return ref.at[chunk, which, pl.ds(pl.multiple_of(matrix * half, half), half)]

    def landing(chunk, matrix):
        return traded.at[chunk, pl.ds(pl.multiple_of(matrix * half, half), half)]

    def core_copy(chunk, matrix):
        return remote(
            part_of(dw, chunk, matrix, 1 - core), landing(chunk, matrix),
            core_sem.at[0, chunk, matrix], core_sem.at[1, chunk, matrix], {"dp": sibling},
        )

    def back_copy(chunk, matrix):
        return remote(
            part_of(dw, chunk, matrix, core), landing(chunk, matrix),
            core_sem.at[2, chunk, matrix], core_sem.at[3, chunk, matrix], {"dp": sibling},
        )

    def result_copies(chunk, matrix):
        return (
            pltpu.make_async_copy(
                part_of(dw, chunk, matrix, core), part_of(dw_hbm, chunk, matrix, core), result_sem.at[0, chunk, matrix]
            ),
            pltpu.make_async_copy(
                landing(chunk, matrix), part_of(dw_hbm, chunk, matrix, 1 - core), result_sem.at[1, chunk, matrix]
            ),
        )

    def hop_copy(chunk, matrix, way, hop, src):
        slot = way * 4 + hop - 1
        return remote(
            src, hops.at[chunk, matrix, slot], ring_send.at[chunk, matrix, slot], ring_recv.at[chunk, matrix, slot], toward(way)
        )

    def hop_arrived(chunk, matrix, way, hop):
        slot = hops.at[chunk, matrix, way * 4 + hop - 1]
        hop_copy(chunk, matrix, way, hop, slot).wait_recv()
        return slot

    def spread_copy(chunk, matrix, way, hop, index):
        slot = 8 + way * 4 + hop - 1
        place = segment(chunk, matrix, index)
        return remote(
            place, place, ring_send.at[chunk, matrix, slot], ring_recv.at[chunk, matrix, slot], toward(way)
        )

    def service(chunk, matrix, turn):
        @pl.when(turn == 0)
        def _():
            core_copy(chunk, matrix).wait()

            @pl.loop(0, RING)
            def _(index):
                mine = segment(chunk, matrix, index)
                theirs = traded.at[chunk, pl.ds(pl.multiple_of(matrix * half + index * SEG, SEG), SEG)]
                mine[...] = (mine[...].astype(F32) + theirs[...].astype(F32)).astype(BF16)

            pl.semaphore_signal(
                free_sem.at[chunk, matrix], inc=1, device_id={"dp": sibling}, device_id_type=pl.DeviceIdType.MESH
            )

            @pl.loop(0, 2)
            def _(way):
                begin = starts.at[chunk, matrix, way]
                begin[...] = segment(chunk, matrix, at + sign(way) * reach(matrix, way))[...]
                hop_copy(chunk, matrix, way, 1, begin).start()

        @pl.when((turn >= 1) & (turn <= 3))
        def _():
            hop = turn + 1

            @pl.loop(0, 2)
            def _(way):
                @pl.when(hop <= reach(matrix, way))
                def _():
                    slot = hop_arrived(chunk, matrix, way, hop - 1)
                    own = segment(chunk, matrix, at + sign(way) * (reach(matrix, way) - hop + 1))
                    slot[...] = (slot[...].astype(F32) + own[...].astype(F32)).astype(BF16)
                    hop_copy(chunk, matrix, way, hop, slot).start()

        @pl.when(turn == 4)
        def _():
            own = segment(chunk, matrix, at)
            total = own[...].astype(F32)
            for way in range(2):
                total = total + hop_arrived(chunk, matrix, way, reach(matrix, way))[...].astype(F32)
            own[...] = total.astype(BF16)
            for way in range(2):
                spread_copy(chunk, matrix, way, 1, at).start()

        @pl.when((turn >= 5) & (turn <= 7))
        def _():
            hop = turn - 3

            @pl.loop(0, 2)
            def _(way):
                @pl.when(hop <= reach(matrix, way))
                def _():
                    index = at - sign(way) * (hop - 1)
                    spread_copy(chunk, matrix, way, hop - 1, index).wait_recv()
                    spread_copy(chunk, matrix, way, hop, index).start()

        @pl.when(turn == 8)
        def _():
            for way in range(2):
                last = reach(matrix, way)
                spread_copy(chunk, matrix, way, last, at - sign(way) * last).wait_recv()
            pl.semaphore_wait(free_sem.at[chunk, matrix], 1)
            back_copy(chunk, matrix).start()

        @pl.when(turn == LAST_TURN)
        def _():
            back_copy(chunk, matrix).wait_recv()
            for result in result_copies(chunk, matrix):
                result.start()

    def serve(*turns):
        @pl.loop(0, 4)
        def _(block):
            turn = sum(jnp.where(block == number, value, 0) for number, value in enumerate(turns))

            @pl.when((turn >= 0) & (turn <= LAST_TURN))
            def _():
                service(lax.div(block, 2), lax.rem(block, 2), turn)

    def rows_of(ref, pair):
        return ref[pair].reshape(flat)

    depth = pairs * 2 * rows
    odd_turns, even_turns = pairs // 2, (pairs - 1) // 2

    @pl.loop(0, 2)
    def _(chunk):
        @pl.when(chunk == 1)
        def _():
            for load in weight_loads(1):
                load.wait()

        @pl.loop(0, pairs)
        def _(pair):
            s, g = rows_of(s_all, pair), rows_of(g_all, pair)

            def head(start):
                cut = slice(start, start + sub)
                place = pl.ds(pl.multiple_of(chunk * units + start, 128), sub)
                return (
                    dot(s, w_own[1, chunk, :, cut], 1, 0) + bias[:, place],
                    dot(g, w_own[0, chunk, cut, :], 1, 1),
                )

            ahead = head(0)
            for start in range(0, units, sub):
                pre, act_grad = ahead
                if start + sub < units:
                    ahead = head(start + sub)
                act, slope = gelu_parts(pre)
                pre_grad = (act_grad * slope).astype(BF16)
                cut = slice(start, start + sub)
                place = pl.ds(pl.multiple_of(chunk * units + start, 128), sub)
                acts[chunk, pair, :, :, cut] = act.reshape(2, rows, sub)
                grads[chunk, pair, :, :, cut] = pre_grad.reshape(2, rows, sub)
                bias_grad[:, place] += row_sums(pre_grad.astype(F32))

            @pl.when((chunk == 1) & (pair > 0))
            def _():
                odd = lax.rem(pair, 2) == 1
                serve(jnp.where(odd, lax.div(pair + 1, 2), -1), jnp.where(odd, -1, lax.div(pair, 2) - 1), -1, -1)

        for matrix in range(2):

            @pl.loop(0, 2)
            def _(part):
                cut = pl.ds(pl.multiple_of(part * half, half), half)
                if matrix == 0:
                    left, right = acts[chunk, :, :, :, cut], g_all[...]
                else:
                    left, right = s_all[:, :, :, cut], grads[chunk]
                grad = dot(left.reshape(depth, half), right.reshape(depth, width), 0, 0)
                dw[chunk, part, matrix * half : (matrix + 1) * half] = grad.astype(BF16)

                @pl.when(chunk == 1)
                def _():
                    serve(
                        jnp.where(part == 1, odd_turns + 1 + matrix, -1), jnp.where(part == 0, even_turns + matrix, -1), -1, -1
                    )

            core_copy(chunk, matrix).start()
            if matrix == 0:

                @pl.when(chunk == 1)
                def _():
                    far_copy(0).wait_recv()
                    pass_copy(0).start()
                    far_copy(1).start()

        serve(jnp.where(chunk == 0, 0, -1), -1, jnp.where(chunk == 0, -1, 0), -1)

    bias_copy.wait()

    def out_copies(pair):
        return (
            pltpu.make_async_copy(acts.at[0, pair], branch_hbm.at[pair], out_sem.at[0, pair]),
            pltpu.make_async_copy(grads.at[0, pair], second_grad_hbm.at[pair], out_sem.at[1, pair]),
        )

    @pl.loop(0, 2)
    def _(chunk):
        pass_copy(chunk).wait_recv()

        @pl.loop(0, pairs)
        def _(pair):
            done = chunk * pairs + pair

            @pl.when(chunk == 0)
            def _():
                out = sum(dot(rows_of(acts.at[own], pair), w_own[0, own], 1, 0) for own in range(2))
                grad_out = sum(dot(rows_of(grads.at[own], pair), w_own[1, own], 1, 1) for own in range(2))
                acts[0, pair] = out.reshape(packed).astype(BF16)
                grads[0, pair] = grad_out.reshape(packed).astype(BF16)

                @pl.when(pair == pairs - 1)
                def _():
                    far_copy(1).wait_recv()
                    pass_copy(1).start()

            serve(odd_turns + 3 + done, -1, 1 + done, -1)
            out, grad_out = far_units(
                sub, rows_of(s_all, pair), rows_of(g_all, pair), w_far.at[1, chunk],
                bias_far.at[:, pl.ds(pl.multiple_of(chunk * units, units), units)], w_far.at[0, chunk],
                rows_of(acts.at[0], pair).astype(F32), rows_of(grads.at[0], pair).astype(F32),
            )
            acts[0, pair] = out.reshape(packed).astype(BF16)
            grads[0, pair] = grad_out.reshape(packed).astype(BF16)

            @pl.when(chunk == 1)
            def _():
                for copy in out_copies(pair):
                    copy.start()

            serve(-1, even_turns + 2 + done, -1, done)

    @pl.loop(0, 2)
    def _(chunk):
        far_copy(chunk).wait_send()
        pass_copy(chunk).wait_send()

        @pl.loop(0, 2)
        def _(matrix):
            back_copy(chunk, matrix).wait_send()
            for result in result_copies(chunk, matrix):
                result.wait()

            @pl.loop(0, 2)
            def _(way):
                @pl.loop(1, reach(matrix, way) + 1)
                def _(hop):
                    hop_copy(chunk, matrix, way, hop, hops.at[chunk, matrix, way * 4 + hop - 1]).wait_send()
                    spread_copy(chunk, matrix, way, hop, at).wait_send()

    @pl.loop(0, pairs)
    def _(pair):
        for copy in out_copies(pair):
            copy.wait()


def channel_call(pairs, collective_id, second, out_grad, channel_in, bias_row, channel_out):
    batch, rows, width = second.shape
    own = channel_in.shape[1]
    units = own // 2
    half = units // 2
    shape = jax.ShapeDtypeStruct
    slots = (batch // 2, 2, rows, width)
    anywhere = pl.BlockSpec(memory_space=pl.ANY)
    vmem = pl.BlockSpec(memory_space=pltpu.VMEM)
    dma = pltpu.SemaphoreType.DMA
    held = (pairs, 2, rows, width)
    branch, second_grad, dw, bias_grad = pl.pallas_call(
        functools.partial(channel_kernel, 256),
        name=f"channel_{pairs}",
        out_shape=[
            shape(slots, BF16), shape(slots, BF16), shape((2, 2, 2 * half, width), BF16), shape((8, own), F32),
        ],
        in_specs=[anywhere] * 4 + [vmem],
        out_specs=[anywhere] * 3 + [vmem],
        scratch_shapes=[
            pltpu.VMEM(held, BF16), pltpu.VMEM(held, BF16),
            pltpu.VMEM((2,) + held, BF16), pltpu.VMEM((2,) + held, BF16),
            pltpu.VMEM((2, 2, units, width), BF16), pltpu.VMEM((2, 2, units, width), BF16),
            pltpu.VMEM((1, own), F32),
            pltpu.VMEM((2, 2, 2 * half, width), BF16), pltpu.VMEM((2, 2 * half, width), BF16),
            pltpu.VMEM((2, 2, 2, SEG, width), BF16), pltpu.VMEM((2, 2, 8, SEG, width), BF16),
            dma((3, 2)), dma((2, pairs)), dma((2,)), dma((4, 2)), dma((4, 2, 2)),
            dma((2, 2, 2)), dma((2, 2, 16)), dma((2, 2, 16)), pltpu.SemaphoreType.REGULAR((2, 2)),
        ],
        cost_estimate=pl.CostEstimate(
            flops=40 * pairs * rows * width * units, bytes_accessed=40 << 20, transcendentals=0
        ),
        compiler_params=pltpu.CompilerParams(
            vmem_limit_bytes=CHANNEL_VMEM, collective_id=collective_id, has_side_effects=True
        ),
    )(second.reshape(slots), out_grad.reshape(slots), channel_in, channel_out, bias_row)
    packed = (batch, rows, width)
    return branch.reshape(packed), second_grad.reshape(packed), dw.reshape(2, 2, 2, half, width), bias_grad


def channel_general(size, meta, core, second, out_grad, channel_in, bias_row, channel_out):
    batch, rows, width = second.shape
    own = channel_in.shape[1]
    units = own // 2
    pairs = batch // 2
    packed = (batch, rows, width)
    shape = jax.ShapeDtypeStruct
    pair = pair_spec(rows, width)

    tp_swap = [(0, 1), (1, 0)]
    far_bias = lax.ppermute(bias_row, "tp", tp_swap)
    far = []
    for index in range(2):
        cut = slice(index * units, (index + 1) * units)
        out_cut, in_cut = channel_out[cut, :], channel_in[:, cut]
        got = lax.ppermute(jnp.where(core == 0, out_cut, in_cut), "tp", tp_swap)
        traded = swap(got, 1, size)
        far.append((jnp.where(core == 0, traded, got), jnp.where(core == 0, got, traded)))

    hidden = []
    for index in range(2):
        hidden.append(call(
            functools.partial(hidden_kernel, 256), "hidden_own", (pairs,),
            (meta, second, out_grad, channel_in, bias_row, channel_out),
            [
                pair, pair,
                pl.BlockSpec((width, units), lambda j, meta, index=index: (0, index)),
                pl.BlockSpec((1, units), lambda j, meta, index=index: (0, index)),
                pl.BlockSpec((units, width), lambda j, meta, index=index: (index, 0)),
            ],
            [shape((batch, rows, units), BF16)] * 2 + [shape((2, width // 2, width), BF16)] * 2 + [shape((8, units), F32)],
            [pair_spec(rows, units)] * 2
            + [pl.BlockSpec((2, width // 2, width), lambda j, meta: (0, 0, 0))] * 2
            + [pl.BlockSpec((8, units), lambda j, meta: (0, 0))],
            [pltpu.VMEM((units, width), F32), pltpu.VMEM((width, units), F32)],
            flops=8 * batch * rows * width * units, traffic=8 * batch * rows * width,
        ))
    dw = jnp.stack([sum_over_dp(h[3], h[2], size) for h in hidden])
    mats = (channel_in, channel_out, far[0][0], far_bias[:, :units], far[0][1])
    parts = call(
        functools.partial(far_first_kernel, 256), "far_first", (pairs,),
        (meta, second, out_grad, hidden[0][0], hidden[0][1], hidden[1][0], hidden[1][1], *mats),
        [pair] * 2 + [pair_spec(rows, units)] * 4 + [whole_spec(m) for m in mats],
        [shape(packed, F32)] * 2, [pair] * 2,
        flops=16 * batch * rows * width * units, traffic=20 * batch * rows * width,
    )
    mats = (far[1][0], far_bias[:, units:], far[1][1])
    branch, second_grad = call(
        functools.partial(far_last_kernel, 256), "far_last", (pairs,),
        (meta, second, out_grad, *parts, *mats),
        [pair] * 4 + [whole_spec(m) for m in mats],
        [shape(packed, BF16)] * 2, [pair] * 2,
        flops=8 * batch * rows * width * units, traffic=20 * batch * rows * width,
    )
    return branch, second_grad, dw, jnp.concatenate([h[4] for h in hidden], axis=1)


def shards(
    size,
    images, cotangent, image_counts, skip_mask, first_gain, first_bias, token_in, token_in_bias,
    token_out, token_out_bias, second_gain, second_bias, channel_in, channel_in_bias, channel_out,
    channel_out_bias,
):
    batch, patches, width = images.shape
    tokens = token_in.shape[1]
    own = channel_in.shape[1]
    rows = -(-patches // 16) * 16
    units = own // 2
    half = units // 2
    pairs = batch // 2
    core = lax.axis_index("dp") & 1
    shape = jax.ShapeDtypeStruct
    packed = (batch, rows, width)
    block = patches * width
    anywhere = pl.BlockSpec(memory_space=pl.ANY)
    vmem = pl.BlockSpec(memory_space=pltpu.VMEM)
    smem = pl.BlockSpec(memory_space=pltpu.SMEM)
    dma = pltpu.SemaphoreType.DMA
    images_t, cotangent_t = jnp.transpose(images, (1, 0, 2)), jnp.transpose(cotangent, (1, 0, 2))
    split = pltpu.VMEM((width // 128, patches * batch, 128), F32)

    def row(vector):
        return jnp.pad(vector, (0, width - vector.shape[0]))

    vectors = jnp.stack([
        row(v) for v in (first_gain, first_bias, second_gain, second_bias, channel_out_bias, token_in_bias, token_out_bias)
    ])
    bias_row = channel_in_bias.reshape(1, own)

    moved = (MOVE, rows, width)
    meta, most, sent_images, sent_cotangents = pl.pallas_call(
        share_kernel,
        name="share",
        out_shape=[
            shape((VALID + batch,), jnp.int32), shape((1,), jnp.int32), shape(moved, BF16), shape(moved, BF16),
        ],
        in_specs=[smem, smem, vmem, vmem],
        out_specs=[smem, smem, vmem, vmem],
        scratch_shapes=[
            split, split, pltpu.VMEM((8, 128), jnp.int32), pltpu.VMEM((size, 8, 128), jnp.int32),
            pltpu.SMEM((size, 128), jnp.int32), dma((size,)), dma((size,)), dma,
        ],
        compiler_params=pltpu.CompilerParams(
            vmem_limit_bytes=VMEM_LIMIT, collective_id=SHARE_ID, has_side_effects=True
        ),
    )(image_counts, skip_mask, images_t, cotangent_t)
    got_images, got_cotangents = swap(sent_images, 1, size), swap(sent_cotangents, 1, size)

    whole_one = lambda array: pl.BlockSpec(array.shape, lambda j, meta: (0,) * array.ndim, pipeline_mode=pl.Buffered(1))
    any_pair = pl.BlockSpec((2, rows, width), lambda j, meta: (j, 0, 0))
    last_kept = lambda j, meta: jnp.minimum(j, jnp.maximum((meta[KEPT] + 1) // 2 - 1, 0))
    kept_pair = lambda r: pl.BlockSpec((2, r, width), lambda j, meta: (last_kept(j, meta), 0, 0))
    native = shape((patches, batch, width), F32)
    smalls = [
        shape((8, width), F32), shape((rows, tokens), BF16), shape((tokens, rows), BF16), shape((rows, tokens), BF16),
        shape((tokens, rows), BF16), shape((tokens, 1), F32), shape((rows, 1), F32),
    ]
    token_out_t = token_out.T
    (
        second, out_grad, middle, source, out_bias_grad, tin, tin_t, tout_t, tout, tin_bias, tout_bias, activations, input_grad,
    ) = call(
        token_forward_kernel, "token_forward", (pairs,),
        (meta, images_t, cotangent_t, vectors, token_in, token_out_t),
        [whole_one(v) for v in (images_t, cotangent_t, vectors, token_in, token_out_t)],
        [shape(packed, BF16), shape(packed, BF16), shape((batch, patches, width), F32), shape(packed, BF16)] + smalls + [native] * 2,
        [any_pair, any_pair, kept_pair(patches), kept_pair(rows)] + [whole_one(v) for v in smalls] + [anywhere] * 2,
        [split, split, pltpu.VMEM((2, 2, 2, patches, width), F32), dma((2, 2, 2))],
        flops=4 * batch * rows * width * tokens * 4, traffic=batch * block * 12,
    )
    second, out_grad, middle, source, out_bias_grad = pl.pallas_call(
        token_received_kernel,
        name="token_received",
        out_shape=[shape(packed, BF16), shape(packed, BF16), shape((batch, patches, width), F32), shape(packed, BF16), shape((8, width), F32)],
        in_specs=[smem] + [vmem] * 8 + [anywhere] * 4,
        out_specs=[anywhere] * 4 + [vmem],
        scratch_shapes=[
            pltpu.VMEM((rows, width), BF16), pltpu.VMEM((rows, width), BF16), pltpu.VMEM((patches, width), F32), dma((4,)),
        ],
        input_output_aliases={9: 0, 10: 1, 11: 2, 12: 3},
        compiler_params=pltpu.CompilerParams(vmem_limit_bytes=VMEM_LIMIT),
    )(
        meta, got_images, got_cotangents, vectors, tin_t, tin_bias, tout_t, tout_bias, out_bias_grad,
        second, out_grad, middle, source,
    )

    operands = (second, out_grad, channel_in, bias_row, channel_out)
    general = functools.partial(channel_general, size, meta, core)
    if size == 2 * RING:
        fast = [functools.partial(channel_call, p, i + 1) for i, p in enumerate(FAST_PAIRS)]
        branch_at = sum((most[0] > 2 * p).astype(jnp.int32) for p in FAST_PAIRS[:-1])
        branch, second_grad, dw, in_bias_grad = lax.switch(branch_at, fast, *operands)
    else:
        branch, second_grad, dw, in_bias_grad = general(*operands)

    def item_specs(own_items):
        def index(place):
            def at(j, meta):
                if own_items:
                    return jnp.minimum(2 * j + place, jnp.maximum(meta[KEPT] - 1, 0)), 0, 0
                return jnp.minimum(meta[KEPT] + jnp.minimum(2 * j + place, jnp.maximum(meta[RECEIVED] - 1, 0)), batch - 1), 0, 0
            return at
        return [pl.BlockSpec((1, r, width), index(place)) for r in (rows, rows, patches, rows, rows) for place in range(2)]

    items = [a for a in (source, out_grad, middle, branch, second_grad) for _ in range(2)]
    consts = (vectors, tin, tin_t, tin_bias, tout)
    sums = [
        shape((rows, tokens), F32), shape((tokens, 128), F32), shape((rows, tokens), F32), shape((rows, 128), F32),
        shape((4, 8, width), F32),
    ]
    stage = [pltpu.VMEM((2, 2, 2, patches, width), F32), dma((2, 2, 2))]
    returned = shape((patches, MOVE, width), F32)
    back_images, back_grads, *partial = call(
        functools.partial(token_backward_kernel, False), "token_backward_received", (MOVE // 2,),
        (meta, *items, *consts),
        item_specs(False) + [whole_one(c) for c in consts],
        [returned] * 2 + sums, [anywhere] * 2 + [whole_one(v) for v in sums],
        stage, flops=10 * MOVE * rows * width * tokens, traffic=MOVE * block * 24,
    )
    back_images, back_grads = swap(back_images, 1, size), swap(back_grads, 1, size)
    in_rows, out_rows = width // pairs, own // pairs
    in_turns, out_turns = half // in_rows, half // out_rows
    first_alias = 1 + len(items) + len(consts) + len(sums) + 3
    activations, input_grad, *partial, in_grad_sum, out_grad_sum = call(
        functools.partial(token_backward_kernel, True), "token_backward", (pairs,),
        (meta, *items, *consts, *partial, dw, dw, dw, activations, input_grad),
        item_specs(True) + [whole_one(c) for c in consts] + [whole_one(v) for v in sums]
        + [
            pl.BlockSpec((1, 1, 1, in_rows, width), lambda t, meta, c=c: (c, t // in_turns, 1, t % in_turns, 0))
            for c in range(2)
        ]
        + [pl.BlockSpec(
            (1, 1, 1, out_rows, width),
            lambda t, meta: (t // (2 * out_turns), (t // out_turns) % 2, 0, t % out_turns, 0),
        )]
        + [anywhere] * 2,
        [native] * 2 + sums + [shape((width, own), F32), shape((own, width), F32)],
        [anywhere] * 2 + [whole_one(v) for v in sums]
        + [pl.BlockSpec((in_rows, own), lambda t, meta: (t, 0)), pl.BlockSpec((out_rows, width), lambda t, meta: (t, 0))],
        stage, flops=10 * batch * rows * width * tokens, traffic=batch * block * 24,
        aliases={first_alias: 0, first_alias + 1: 1},
    )
    tin_grad, tin_bias_grad, tout_grad, tout_bias_grad, gains = partial
    if size == 2 * RING:
        summed = pl.pallas_call(
            small_sum_kernel,
            name="small_sum",
            out_shape=shape((PACKED, width), F32),
            in_specs=[vmem] * 7,
            out_specs=vmem,
            scratch_shapes=[
                pltpu.VMEM((2, PACKED // 2, width), F32), pltpu.VMEM((PACKED // 2, width), F32),
                pltpu.VMEM((PACKED // 2, width), BF16), pltpu.VMEM((PACKED // 2, width), BF16),
                pltpu.VMEM((PACKED // 2, width), BF16), pltpu.VMEM((RING, PACKED // 2 // RING, width), BF16),
                dma((4,)), dma((RING,)), dma((RING,)), dma((RING,)), dma((RING,)),
            ],
            compiler_params=pltpu.CompilerParams(
                vmem_limit_bytes=VMEM_LIMIT, collective_id=SUM_ID, has_side_effects=True
            ),
        )(tin_grad, tout_grad, tin_bias_grad, tout_bias_grad, gains, in_bias_grad, out_bias_grad)
    else:
        summed = lax.psum(pack_small(
            tin_grad, tout_grad, tin_bias_grad, tout_bias_grad, gains, in_bias_grad, out_bias_grad
        ), "dp")
    lines = [tokens, patches, width, width, width, width, own, width]
    activations, input_grad, tin_sum, tout_sum, *vectors_sum = pl.pallas_call(
        place_kernel,
        name="place",
        out_shape=[native] * 2 + [shape((patches, tokens), F32)] * 2 + [shape((-(-n // 128), 128), F32) for n in lines],
        in_specs=[smem] + [anywhere] * 4 + [vmem],
        out_specs=[anywhere] * 2 + [vmem] * 10,
        scratch_shapes=[pltpu.VMEM((2, MOVE, patches, width), F32), dma((2, 2, MOVE))],
        input_output_aliases={3: 0, 4: 1},
        compiler_params=pltpu.CompilerParams(vmem_limit_bytes=VMEM_LIMIT),
    )(meta, back_images, back_grads, activations, input_grad, summed)
    activations, input_grad = jnp.transpose(activations, (1, 0, 2)), jnp.transpose(input_grad, (1, 0, 2))
    tin_b, tout_b, gain1, shift1, gain2, shift2, in_b, out_b = [v.reshape(-1)[:n] for v, n in zip(vectors_sum, lines)]
    small = (gain1, shift1, tin_sum, tin_b, tout_sum.T, tout_b, gain2, shift2, in_b, out_b)
    return (activations, input_grad, *small[:8], in_grad_sum, small[8], out_grad_sum, small[9])


def solution(mesh):
    placed = (
        P("dp", None, None), P("dp", None, None), P("dp"), P("dp"), P(), P(), P(), P(), P(), P(), P(), P(),
        P(None, "tp"), P("tp"), P("tp", None), P(),
    )
    return jax.shard_map(
        functools.partial(shards, mesh.shape["dp"]),
        mesh=mesh,
        in_specs=placed,
        out_specs=(
            P("dp", None, None), P("dp", None, None), P(), P(), P(), P(), P(), P(), P(), P(),
            P(None, "tp"), P("tp"), P("tp", None), P(),
        ),
        check_vma=False,
    )
```

```python
import functools

import jax
import jax.numpy as jnp
from jax import lax
from jax.experimental import pallas as pl
from jax.experimental.pallas import tpu as pltpu
from jax.sharding import PartitionSpec as P

EPSILON = 1e-06
ROOT_HALF = 0.7071067811865476
INV_ROOT_TAU = 0.3989422804014327
F32, BF16 = jnp.float32, jnp.bfloat16
VMEM_LIMIT = 60 * 1024 * 1024
CHANNEL_VMEM = 60 * 1024 * 1024
RING, SEG, LAST_TURN = 8, 48, 9
FAST_PAIRS = (6, 8)
SHARE_ID, SUM_ID = 9, 10
PACKED = 256

MOVE = 4
N_LIVE, KEPT, RECEIVED, N_PAIRS, CORE, GIVEN, LIST, VALID = 0, 1, 2, 3, 4, 5, 8, 24
GAIN1, SHIFT1, GAIN2, SHIFT2, OUT_BIAS, TIN_BIAS, TOUT_BIAS = range(7)


def dot(left, right, left_dim, right_dim):
    return lax.dot_general(
        left, right, (((left_dim,), (right_dim,)), ((), ())), preferred_element_type=F32
    )


def gelu_parts(values):
    half = 0.5 * (1.0 + lax.erf(values * ROOT_HALF))
    slope = half + values * (INV_ROOT_TAU * jnp.exp(-0.5 * values * values))
    return (values * half).astype(BF16), slope


def gelu_only(values):
    return (values * (0.5 * (1.0 + lax.erf(values * ROOT_HALF)))).astype(BF16)


def standardize(values):
    width = values.shape[-1]
    center = jnp.sum(values, axis=-1, keepdims=True) * (1.0 / width)
    deviation = values - center
    scale = lax.rsqrt(
        jnp.sum(deviation * deviation, axis=-1, keepdims=True) * (1.0 / width) + EPSILON
    )
    return deviation * scale, scale


def norm_back(grad_hat, hat, scale):
    width = hat.shape[-1]
    first = jnp.sum(grad_hat, axis=-1, keepdims=True) * (1.0 / width)
    second = jnp.sum(grad_hat * hat, axis=-1, keepdims=True) * (1.0 / width)
    return scale * (grad_hat - first - hat * second)


def pad_rows(values, rows):
    return jnp.concatenate(
        [values, jnp.zeros((rows - values.shape[0], values.shape[1]), values.dtype)], axis=0
    )


def row_sums(values):
    rows, width = values.shape
    return jnp.sum(values.reshape(rows // 8, 8, width), axis=0)


def lane_sums(values):
    total = values[:, :128]
    for at in range(128, values.shape[1], 128):
        total = total + values[:, at : at + 128]
    return total


def split_lanes(source, target, pieces):
    patches, images, width = source.shape
    step = patches // pieces
    for piece in range(pieces):
        rows = source[piece * step : (piece + 1) * step].astype(F32).reshape(step * images, width)
        for group in range(width // 128):
            target[group, piece * step * images : (piece + 1) * step * images, :] = rows[:, group * 128 : (group + 1) * 128]


def one_image(split, index, images):
    patches = split.shape[1] // images
    return jnp.concatenate(
        [split[group, pl.ds(index, patches, stride=images), :] for group in range(split.shape[0])], axis=1
    )


def share_kernel(
    counts, skips, images, cotangents, meta, most, sent_images, sent_cotangents,
    x_raw, c_raw, x_split, c_split, mine, gathered, gathered_smem, send_sem, recv_sem, local_sem, load_sem,
):
    slots = images.shape[1]
    rows = sent_images.shape[1]
    size = gathered.shape[0]
    me = lax.axis_index("dp")
    loads = [
        pltpu.make_async_copy(images, x_raw, load_sem.at[0]), pltpu.make_async_copy(cotangents, c_raw, load_sem.at[1]),
    ]
    for load in loads:
        load.start()
    barrier = pltpu.get_barrier_semaphore()

    def peer(step):
        return {"dp": lax.rem(me + step, size)}

    for step in range(1, size):
        pl.semaphore_signal(barrier, inc=1, device_id=peer(step), device_id_type=pl.DeviceIdType.MESH)
    one, none = jnp.int32(1), jnp.int32(0)
    valid, live, rank, total = [], [], [], none
    for slot in range(slots):
        valid.append(jnp.where(slot < counts[0], one, none))
        live.append(valid[slot] * skips[slot])
        rank.append(total)
        total = total + live[slot]
    mine[...] = jnp.zeros_like(mine) + total
    gathered[me] = mine[...]
    pl.semaphore_wait(barrier, size - 1)

    def send(step):
        return pltpu.make_async_remote_copy(
            src_ref=mine, dst_ref=gathered.at[me], send_sem=send_sem.at[step], recv_sem=recv_sem.at[step],
            device_id=peer(step), device_id_type=pl.DeviceIdType.MESH,
        )

    for step in range(1, size):
        send(step).start()
    for load, raw, split in zip(loads, (x_raw, c_raw), (x_split, c_split)):
        load.wait()
        split_lanes(raw, split, 14)
    place_of = [jnp.where(live[slot] == 1, rank[slot], total + slot - rank[slot]) for slot in range(slots)]
    for place in range(slots):
        index, ok = none, none
        for slot in range(slots):
            hit = jnp.where(place_of[slot] == place, one, none)
            index = index + hit * slot
            ok = ok + hit * valid[slot]
        meta[LIST + place] = index
        meta[VALID + place] = ok
    for place in range(MOVE):
        index = none
        for slot in range(slots):
            index = index + slot * live[slot] * jnp.where(rank[slot] == total - 1 - place, one, none)
        sent_images[place] = pad_rows(one_image(x_split, index, slots), rows).astype(BF16)
        sent_cotangents[place] = pad_rows(one_image(c_split, index, slots), rows).astype(BF16)
    for step in range(1, size):
        send(step).wait()
    local = pltpu.make_async_copy(gathered.at[:, 0, :], gathered_smem, local_sem)
    local.start()
    local.wait()

    def excess(left, right):
        return jnp.clip(lax.shift_right_arithmetic(left - right, one), 0, MOVE)

    fullest = none
    for chip in range(size // 2):
        left, right = gathered_smem[2 * chip, 0], gathered_smem[2 * chip + 1, 0]
        shift = excess(left, right) - excess(right, left)
        fullest = jnp.maximum(fullest, jnp.maximum(left - shift, right + shift))
    most[0] = fullest
    sibling = me + 1 - 2 * lax.rem(me, 2)
    there = gathered_smem[sibling, 0]
    given, received = excess(total, there), excess(there, total)
    kept = total - given
    for at, value in (
        (N_LIVE, total), (KEPT, kept), (RECEIVED, received),
        (N_PAIRS, lax.shift_right_arithmetic(kept + received + 1, one)), (CORE, lax.rem(me, 2)), (GIVEN, given),
    ):
        meta[at] = value


def column(row):
    return jnp.transpose(jnp.broadcast_to(row, (8, row.shape[1])))[:, :1]


def token_forward(sources, grads, vectors, tin_t, tin_bias, tout_t, tout_bias, rows):
    patches = sources[0].shape[0]
    normed = [
        pad_rows(standardize(x)[0] * vectors[GAIN1 : GAIN1 + 1] + vectors[SHIFT1 : SHIFT1 + 1], rows).astype(BF16)
        for x in sources
    ]
    pre = [dot(tin_t[...], n, 1, 0) + tin_bias[...] for n in normed]
    act = [gelu_only(p) for p in pre]
    branch = [dot(tout_t[...], a, 1, 0)[:patches] + tout_bias[:patches] for a in act]
    middle = [x + b for x, b in zip(sources, branch)]
    second = [
        pad_rows(standardize(m)[0] * vectors[GAIN2 : GAIN2 + 1] + vectors[SHIFT2 : SHIFT2 + 1], rows) for m in middle
    ]
    return middle, second, [pad_rows(g, rows) for g in grads]


def token_forward_kernel(
    meta, images, cotangents, vectors, tin, tout_in,
    second, out_grad, middle, source, grad_sum, tin_pad, tin_t, tout_t, tout, tin_bias, tout_bias, activations, input_grad,
    x_split, c_split, nothing, fill_sem,
):
    step = pl.program_id(0)
    steps = pl.num_programs(0)
    rows = second.shape[1]
    patches, slots, _ = images.shape

    groups = x_split.shape[0]
    x_rows, c_rows = (split.reshape(groups, patches * slots, 128) for split in (x_split, c_split))

    def fills(item, valid):
        index = meta[LIST + item]
        copies = []
        for number, (split, out) in enumerate(((x_split, activations), (c_split, input_grad))):
            for group in range(groups):
                copies.append(pltpu.make_async_copy(
                    split.at[group, :, index, :] if valid else nothing, out.at[:, index, pl.ds(group * 128, 128)],
                    fill_sem.at[item, number * groups + group],
                ))
        return copies

    @pl.when(step == 0)
    def _():
        piece = patches // 14

        @pl.loop(0, 14)
        def _(number):
            cut = pl.ds(number * piece, piece)
            for raw, split in ((images, x_split), (cotangents, c_split)):
                for group in range(groups):
                    split[group, cut] = raw[cut, :, group * 128 : (group + 1) * 128].astype(F32)

        nothing[...] = jnp.zeros_like(nothing)

        @pl.loop(meta[N_LIVE], slots)
        def _(item):
            @pl.when(meta[VALID + item] == 1)
            def _():
                for copy in fills(item, True):
                    copy.start()

            @pl.when(meta[VALID + item] == 0)
            def _():
                for copy in fills(item, False):
                    copy.start()

        grad_sum[...] = jnp.zeros_like(grad_sum)
        wide = pad_rows(tin[...].astype(F32), rows)
        tin_pad[...] = wide.astype(BF16)
        tin_t[...] = jnp.transpose(wide).astype(BF16)
        wide = pad_rows(tout_in[...].astype(F32), rows)
        tout_t[...] = wide.astype(BF16)
        tout[...] = jnp.transpose(wide).astype(BF16)
        tin_bias[...] = column(vectors[TIN_BIAS : TIN_BIAS + 1, : tin_bias.shape[0]])
        tout_bias[...] = column(vectors[TOUT_BIAS : TOUT_BIAS + 1, : tout_bias.shape[0]])

    def run(places):
        at = [meta[LIST + 2 * step + place] for place in places]
        sources = [one_image(x_rows, index, slots) for index in at]
        grads = [one_image(c_rows, index, slots) for index in at]
        mid, sec, gra = token_forward(sources, grads, vectors, tin_t, tin_bias, tout_t, tout_bias, rows)
        for place, m, s, g, x in zip(places, mid, sec, gra, sources):
            middle[place] = m
            second[place] = s.astype(BF16)
            out_grad[place] = g.astype(BF16)
            source[place] = pad_rows(x, rows).astype(BF16)
            grad_sum[...] += row_sums(g)

    @pl.when(2 * step + 1 < meta[KEPT])
    def _():
        run((0, 1))

    @pl.when(2 * step + 1 == meta[KEPT])
    def _():
        run((0,))
        second[1] = jnp.zeros_like(second[1])
        out_grad[1] = jnp.zeros_like(out_grad[1])

    @pl.when(2 * step >= meta[KEPT])
    def _():
        second[...] = jnp.zeros_like(second)
        out_grad[...] = jnp.zeros_like(out_grad)

    @pl.when(step == steps - 1)
    def _():
        @pl.loop(meta[N_LIVE], slots)
        def _(item):
            for copy in fills(item, False):
                copy.wait()


def token_received_kernel(
    meta, images, cotangents, vectors, tin_t, tin_bias, tout_t, tout_bias, grad_sum_in,
    second_in, out_grad_in, middle_in, source_in,
    second, out_grad, middle, source, grad_sum,
    second_one, grad_one, middle_one, sem,
):
    grad_sum[...] = grad_sum_in[...]
    rows = second_one.shape[1]
    patches = middle_one.shape[1]

    def copies(place):
        index = meta[KEPT] + place
        return [
            pltpu.make_async_copy(src.at[place], dst.at[index], sem.at[number, place])
            for number, (src, dst) in enumerate((
                (second_one, second), (grad_one, out_grad), (middle_one, middle), (images, source),
            ))
        ]

    @pl.loop(0, meta[RECEIVED])
    def _(place):
        x = images[place, :patches].astype(F32)
        mid, sec, gra = token_forward(
            [x], [cotangents[place, :patches].astype(F32)], vectors, tin_t, tin_bias, tout_t, tout_bias, rows
        )
        second_one[place] = sec[0].astype(BF16)
        grad_one[place] = gra[0].astype(BF16)
        middle_one[place] = mid[0]
        grad_sum[...] += row_sums(gra[0])
        for copy in copies(place):
            copy.start()

    @pl.loop(0, meta[RECEIVED])
    def _(place):
        for copy in copies(place):
            copy.wait()


def hidden_kernel(
    sub, meta, second, out_grad, win, win_bias, wout,
    act_out, pre_grad_out, sent, kept, bias_grad, wout_grad, win_grad,
):
    step, steps = pl.program_id(0), pl.num_programs(0)

    @pl.when(step == 0)
    def _():
        wout_grad[...] = jnp.zeros_like(wout_grad)
        win_grad[...] = jnp.zeros_like(win_grad)
        bias_grad[...] = jnp.zeros_like(bias_grad)

    @pl.when(step < meta[N_PAIRS])
    def _():
        pair, rows, width = second.shape
        s = second[...].reshape(pair * rows, width)
        g = out_grad[...].reshape(pair * rows, width)

        def head(at):
            cut = slice(at, at + sub)
            return dot(s, win[:, cut], 1, 0) + win_bias[:, cut], dot(g, wout[cut, :], 1, 1)

        units = win.shape[1]
        ahead = head(0)
        for at in range(0, units, sub):
            pre, act_grad = ahead
            if at + sub < units:
                ahead = head(at + sub)
            act, slope = gelu_parts(pre)
            grad = act_grad * slope
            pre_grad = grad.astype(BF16)
            cut = slice(at, at + sub)
            act_out[:, :, cut] = act.reshape(pair, rows, sub)
            pre_grad_out[:, :, cut] = pre_grad.reshape(pair, rows, sub)
            bias_grad[:, cut] += row_sums(pre_grad.astype(F32))
            wout_grad[cut, :] += dot(act, g, 0, 0)
            win_grad[:, cut] += dot(s, pre_grad, 0, 0)

    @pl.when(step == steps - 1)
    def _():
        half = kept.shape[1]
        mine = pl.ds(pl.multiple_of(meta[CORE] * half, half), half)
        other = pl.ds(pl.multiple_of((1 - meta[CORE]) * half, half), half)
        kept[0] = wout_grad[mine, :].astype(BF16)
        kept[1] = win_grad[mine, :].astype(BF16)
        sent[0] = wout_grad[other, :].astype(BF16)
        sent[1] = win_grad[other, :].astype(BF16)


def far_units(sub, s, g, win, win_bias, wout, out, grad_out):
    def head(at):
        cut = slice(at, at + sub)
        return dot(s, win[:, cut], 1, 0) + win_bias[:, cut], dot(g, wout[cut, :], 1, 1)

    units = win.shape[1]
    ahead = head(0)
    for at in range(0, units, sub):
        pre, act_grad = ahead
        if at + sub < units:
            ahead = head(at + sub)
        act, slope = gelu_parts(pre)
        pre_grad = (act_grad * slope).astype(BF16)
        cut = slice(at, at + sub)
        more, more_grad = dot(act, wout[cut, :], 1, 0), dot(pre_grad, win[:, cut], 1, 1)
        out = more if out is None else out + more
        grad_out = more_grad if grad_out is None else grad_out + more_grad
    return out, grad_out


def far_first_kernel(
    sub, meta, second, out_grad, act0, grad0, act1, grad1, win_own, wout_own, win, win_bias, wout,
    out_part, grad_part,
):
    step = pl.program_id(0)

    @pl.when(step < meta[N_PAIRS])
    def _():
        pair, rows, width = second.shape
        flat = (pair * rows, width)
        s, g = second[...].reshape(flat), out_grad[...].reshape(flat)
        units = win.shape[1]
        out, grad_out = far_units(sub, s, g, win, win_bias, wout, None, None)
        for index, (act, pre_grad) in enumerate(((act0, grad0), (act1, grad1))):
            cut = slice(index * units, (index + 1) * units)
            out = out + dot(act[...].reshape(flat), wout_own[cut, :], 1, 0)
            grad_out = grad_out + dot(pre_grad[...].reshape(flat), win_own[:, cut], 1, 1)
        out_part[...] = out.reshape(pair, rows, width)
        grad_part[...] = grad_out.reshape(pair, rows, width)


def far_last_kernel(
    sub, meta, second, out_grad, out_part, grad_part, win, win_bias, wout, branch, second_grad,
):
    step = pl.program_id(0)

    @pl.when(step < meta[N_PAIRS])
    def _():
        pair, rows, width = second.shape
        flat = (pair * rows, width)
        s, g = second[...].reshape(flat), out_grad[...].reshape(flat)
        out, grad_out = far_units(
            sub, s, g, win, win_bias, wout, out_part[...].reshape(flat), grad_part[...].reshape(flat)
        )
        branch[...] = out.reshape(pair, rows, width).astype(BF16)
        second_grad[...] = grad_out.reshape(pair, rows, width).astype(BF16)


def token_backward_kernel(
    own, meta, *refs,
):
    items = [refs[2 * number : 2 * number + 2] for number in range(5)]
    images, grads, middles, branches, second_grads = items
    vectors, tin, tin_t, tin_bias, tout = refs[10:15]
    refs = refs[15:]
    if own:
        sums_in, refs = refs[:4], refs[4:]
        dw_in0, dw_in1, dw_out = refs[:3]
        refs = refs[5:]
    activations, input_grad = refs[:2]
    sums = refs[2:6]
    refs = refs[6:]
    if own:
        win_grad, wout_grad = refs[:2]
        refs = refs[2:]
    stage, stage_sem = refs
    tin_grad, tout_grad, tout_bias_grad, gains = sums
    step, steps = pl.program_id(0), pl.num_programs(0)
    patches, rows = middles[0].shape[1], images[0].shape[1]
    count = meta[KEPT] if own else meta[RECEIVED]

    @pl.when(step == 0)
    def _():
        for number, ref in enumerate(sums):
            ref[...] = sums_in[number][...] if own else jnp.zeros_like(ref)

    if own:
        units = dw_in0.shape[-1]
        win_grad[:, :units] = dw_in0[...].reshape(win_grad.shape[0], units).astype(F32)
        win_grad[:, units:] = dw_in1[...].reshape(win_grad.shape[0], units).astype(F32)
        wout_grad[...] = dw_out[...].reshape(wout_grad.shape).astype(F32)

    def copies(at_step, place):
        slot = lax.rem(at_step, 2)
        item = 2 * at_step + place
        if own:
            index = meta[LIST + item]
            targets = (activations.at[:, index, :], input_grad.at[:, index, :])
        else:
            targets = (activations.at[:, item, :], input_grad.at[:, item, :])
        return [
            pltpu.make_async_copy(stage.at[slot, place, number], target, stage_sem.at[slot, place, number])
            for number, target in enumerate(targets)
        ]

    def vector(row):
        return vectors[row : row + 1]

    def run(places):
        slot = lax.rem(step, 2)
        hat_width = middles[0].shape[2]
        middle = [middles[p][0] for p in places]
        norm2 = [standardize(m) for m in middle]
        grad2 = [second_grads[p][0].astype(F32)[:patches] for p in places]
        middle_grad = [
            grads[p][0].astype(F32)[:patches] + norm_back(g * vector(GAIN2), hat, scale)
            for p, g, (hat, scale) in zip(places, grad2, norm2)
        ]
        branch_grad = [pad_rows(m, rows).astype(BF16) for m in middle_grad]
        norm1 = [standardize(images[p][0].astype(F32)[:patches]) for p in places]
        ones = jnp.concatenate([jnp.ones((1, hat_width), F32), jnp.zeros((rows - patches - 1, hat_width), F32)], axis=0)
        normed = [
            jnp.concatenate([hat * vector(GAIN1) + vector(SHIFT1), ones], axis=0).astype(BF16) for hat, _ in norm1
        ]
        pre = [dot(tin_t[...], n, 1, 0) + tin_bias[...] for n in normed]
        act_grad = [dot(tout[...], b, 1, 0) for b in branch_grad]
        parts = [gelu_parts(p) for p in pre]
        pre_grad = [(a * slope).astype(BF16) for a, (_, slope) in zip(act_grad, parts)]
        normed_grad = [dot(tin[...], p, 1, 0)[:patches] for p in pre_grad]
        for p, m in zip(places, middle):
            stage[slot, p, 0] = m + (branches[p][0].astype(F32)[:patches] + vector(OUT_BIAS))
        for p, m, n, (hat, scale) in zip(places, middle_grad, normed_grad, norm1):
            stage[slot, p, 1] = m + norm_back(n * vector(GAIN1), hat, scale)
        for p in places:
            for copy in copies(step, p):
                copy.start()
        tout_grad[...] += sum(dot(b, act, 1, 1) for (act, _), b in zip(parts, branch_grad))
        tin_grad[...] += sum(dot(n, p, 1, 1) for n, p in zip(normed, pre_grad))
        tout_bias_grad[...] += sum(lane_sums(b.astype(F32)) for b in branch_grad)
        gains[0] += sum(row_sums(pad_rows(g * hat, rows)) for g, (hat, _) in zip(grad2, norm2))
        gains[1] += sum(row_sums(pad_rows(g, rows)) for g in grad2)
        gains[2] += sum(row_sums(pad_rows(n * hat, rows)) for n, (hat, _) in zip(normed_grad, norm1))
        gains[3] += sum(row_sums(pad_rows(n, rows)) for n in normed_grad)

    for place in range(2):

        @pl.when((step >= 2) & (2 * (step - 2) + place < count))
        def _():
            for copy in copies(step - 2, place):
                copy.wait()

    @pl.when(2 * step + 1 < count)
    def _():
        run((0, 1))

    @pl.when(2 * step + 1 == count)
    def _():
        run((0,))

    for place in range(2):
        for back in (1, 0):

            @pl.when((step == steps - 1) & (step >= back) & (2 * (step - back) + place < count))
            def _():
                for copy in copies(step - back, place):
                    copy.wait()


def place_kernel(
    meta, images, grads, activations_in, input_grad_in, summed,
    activations, input_grad,
    tin_out, tout_out, tin_bias_out, tout_bias_out, gain1_out, shift1_out, gain2_out, shift2_out, in_bias_out, out_bias_out,
    held, sem,
):
    def loads(place):
        return [
            pltpu.make_async_copy(back.at[:, place, :], held.at[number, place], sem.at[0, number, place])
            for number, back in enumerate((images, grads))
        ]

    def stores(place):
        index = meta[LIST + meta[N_LIVE] - 1 - place]
        return [
            pltpu.make_async_copy(held.at[number, place], out.at[:, index, :], sem.at[1, number, place])
            for number, out in enumerate((activations, input_grad))
        ]

    @pl.loop(0, meta[GIVEN])
    def _(place):
        for copy in loads(place):
            copy.start()

    patches, tokens = tin_out.shape
    rows = -(-patches // 16) * 16
    width = summed.shape[1]
    unfold = lambda v: jnp.concatenate([v[:, :tokens], v[:, tokens:]], axis=0)[:patches]
    tin_out[...] = unfold(summed[: rows // 2])
    tout_out[...] = unfold(summed[rows // 2 : rows])
    split = lambda row: jnp.concatenate([row[:, at : at + 128] for at in range(0, row.shape[1], 128)], axis=0)
    below = patches - rows // 2
    tin_bias_out[...] = split(summed[below : below + 1, tokens:])

    def vector(number, length=width):
        return split(summed[rows + number : rows + number + 1, : -(-length // 128) * 128])

    gain2_out[...], shift2_out[...], gain1_out[...], shift1_out[...] = (vector(number) for number in range(4))
    in_bias_out[...] = jnp.concatenate([vector(4), vector(5)], axis=0)
    out_bias_out[...] = vector(6)
    tout_bias_out[...] = vector(7, patches)

    @pl.loop(0, meta[GIVEN])
    def _(place):
        for load, store in zip(loads(place), stores(place)):
            load.wait()
            store.start()

    @pl.loop(0, meta[GIVEN])
    def _(place):
        for copy in stores(place):
            copy.wait()


def pack_small(tin_grad, tout_grad, tout_bias_grad, gains, in_bias_grad, out_bias_grad):
    rows, width = tin_grad.shape[0], out_bias_grad.shape[1]
    line = lambda v: jnp.sum(v, axis=0, keepdims=True)
    flat = lambda v: jnp.concatenate([v, jnp.zeros((1, width - v.shape[1]), F32)], axis=1)
    fold = lambda v: jnp.concatenate([v[: rows // 2], v[rows // 2 :]], axis=1)
    vectors = [line(gains[number]) for number in range(4)]
    in_bias = line(in_bias_grad)
    vectors += [in_bias[:, :width], in_bias[:, width:], line(out_bias_grad)]
    vectors += [flat(line(jnp.transpose(tout_bias_grad)))]
    return jnp.concatenate(
        [fold(tin_grad), fold(tout_grad)] + vectors + [jnp.zeros((PACKED - rows - len(vectors), width), F32)], axis=0
    )


def small_sum_kernel(
    tin_grad, tout_grad, tout_bias_grad, gains, in_bias_grad, out_bias_grad,
    summed,
    packed, landed, reduced, gathered, other, pieces, core_sem, sum_send, sum_recv, gather_send, gather_recv,
):
    width = packed.shape[-1]
    rows = tin_grad.shape[0]
    me = lax.axis_index("dp")
    core, chip = lax.rem(me, 2), lax.div(me, 2)
    sibling = me + 1 - 2 * core

    def chip_at(step):
        return lax.rem(chip + step, RING)

    def peer(step):
        return {"dp": 2 * chip_at(step) + core}

    barrier = pltpu.get_barrier_semaphore()
    for near in [{"dp": sibling}] + [peer(step) for step in range(1, RING)]:
        pl.semaphore_signal(barrier, inc=1, device_id=near, device_id_type=pl.DeviceIdType.MESH)

    def remote(src, dst, send, recv, device):
        return pltpu.make_async_remote_copy(
            src_ref=src, dst_ref=dst, send_sem=send, recv_sem=recv, device_id=device,
            device_id_type=pl.DeviceIdType.MESH,
        )

    everything = pack_small(
        tin_grad[...], tout_grad[...], tout_bias_grad[...], gains[...], in_bias_grad[...], out_bias_grad[...]
    )
    packed[0] = everything[: PACKED // 2]
    packed[1] = everything[PACKED // 2 :]
    pl.semaphore_wait(barrier, RING)

    swap_copy = remote(packed.at[1 - core], landed, core_sem.at[0], core_sem.at[1], {"dp": sibling})
    swap_copy.start()
    swap_copy.wait()
    packed[core] = packed[core] + landed[...]
    reduced[...] = packed[core].astype(BF16)
    piece = PACKED // 2 // RING

    def segment(ref, index):
        return ref.at[pl.ds(pl.multiple_of(index * piece, piece), piece)]

    def sum_copy(step):
        return remote(segment(reduced, chip_at(step)), pieces.at[step], sum_send.at[step], sum_recv.at[step], peer(step))

    for step in range(1, RING):
        sum_copy(step).start()
    total = segment(packed.at[core], chip)[...]
    for step in range(1, RING):
        sum_copy(step).wait()
        total = total + pieces[step].astype(F32)
    pieces[0] = total.astype(BF16)

    def gather_copy(step):
        return remote(
            pieces.at[0], segment(gathered, chip), gather_send.at[step], gather_recv.at[step], peer(step)
        )

    for step in range(1, RING):
        gather_copy(step).start()
    segment(gathered, chip)[...] = pieces[0]
    for step in range(1, RING):
        gather_copy(step).wait()
    back_copy = remote(gathered, other, core_sem.at[2], core_sem.at[3], {"dp": sibling})
    back_copy.start()
    back_copy.wait()
    summed[: PACKED // 2] = jnp.where(core == 0, gathered[...], other[...]).astype(F32)
    summed[PACKED // 2 :] = jnp.where(core == 0, other[...], gathered[...]).astype(F32)


def last_pair(step, meta):
    return jnp.minimum(step, jnp.maximum(meta[N_PAIRS] - 1, 0))


def pair_spec(rows, width):
    return pl.BlockSpec((2, rows, width), lambda j, meta: (last_pair(j, meta), 0, 0))


def whole_spec(array):
    zeros = (0,) * array.ndim
    return pl.BlockSpec(array.shape, lambda j, meta: zeros)


def call(body, name, grid, args, in_specs, outs, out_specs, scratch=(), flops=0, traffic=0, aliases={}):
    return pl.pallas_call(
        body,
        name=name,
        out_shape=outs,
        grid_spec=pltpu.PrefetchScalarGridSpec(
            num_scalar_prefetch=1,
            grid=grid,
            in_specs=in_specs,
            out_specs=out_specs,
            scratch_shapes=scratch,
        ),
        input_output_aliases=aliases,
        cost_estimate=pl.CostEstimate(flops=flops, bytes_accessed=traffic, transcendentals=0),
        compiler_params=pltpu.CompilerParams(
            vmem_limit_bytes=VMEM_LIMIT, dimension_semantics=("arbitrary",)
        ),
    )(*args)


def swap(value, bit, size):
    return lax.ppermute(value, "dp", [(i, i ^ bit) for i in range(size)])


def sum_over_dp(kept, sent, size):
    me = lax.axis_index("dp")
    core, bit1, rest = me & 1, (me >> 1) & 1, me >> 2
    groups = size // 4
    total = kept.astype(F32) + swap(sent, 1, size).astype(F32)
    mine = jnp.where(bit1 == 0, total[0], total[1])
    other = jnp.where(bit1 == 0, total[1], total[0]).astype(BF16)
    total = mine + swap(other, 2, size).astype(F32)
    rows, width = total.shape
    pieces = total.astype(BF16).reshape(groups, rows // groups, width)
    if groups <= 4:
        arrived = [
            swap(lax.dynamic_index_in_dim(pieces, rest ^ k, keepdims=False), 4 * k, size)
            for k in range(1, groups)
        ]
        piece = lax.dynamic_index_in_dim(
            total.reshape(groups, rows // groups, width), rest, keepdims=False
        )
        for other in arrived:
            piece = piece + other.astype(F32)
        piece = piece.astype(BF16)
        whole = jnp.zeros((groups, rows // groups, width), BF16)
        whole = lax.dynamic_update_index_in_dim(whole, piece, rest, 0)
        for k in range(1, groups):
            whole = lax.dynamic_update_index_in_dim(whole, swap(piece, 4 * k, size), rest ^ k, 0)
    else:
        teams = [[4 * r + low for r in range(groups)] for low in range(4)]
        arrived = lax.all_to_all(pieces, "dp", 0, 0, axis_index_groups=teams)
        piece = jnp.sum(arrived.astype(F32), axis=0).astype(BF16)
        whole = lax.all_gather(piece, "dp", axis_index_groups=teams)
    part = whole.reshape(rows, width)
    far = swap(part, 2, size)
    both = jnp.where(bit1 == 0, jnp.stack([part, far]), jnp.stack([far, part]))
    far = swap(both, 1, size)
    return jnp.where(core == 0, jnp.stack([both, far]), jnp.stack([far, both]))


def channel_kernel(
    sub, second_hbm, grad_hbm, win_hbm, wout_hbm, bias,
    branch_hbm, second_grad_hbm, dw_hbm, bias_grad,
    s_all, g_all, acts, grads, w_own, w_far, bias_far, dw, traded, starts, hops,
    load_sem, out_sem, bias_sem, far_sem, core_sem, result_sem, ring_send, ring_recv, free_sem,
):
    pairs, _, rows, width = s_all.shape
    units = width
    half = units // 2
    flat = (2 * rows, width)
    packed = (2, rows, width)
    me = lax.axis_index("dp")
    core, y, z = lax.rem(me, 2), lax.rem(lax.div(me, 2), 2), lax.div(me, 4)
    tp = lax.axis_index("tp")
    at = y * 4 + z + y * (3 - 2 * z)

    def device_at(place):
        place = lax.rem(place + RING, RING)
        row = lax.div(place, 4)
        col = lax.rem(place, 4)
        return (col + row * (3 - 2 * col)) * 4 + row * 2 + core

    sibling = me + 1 - 2 * core
    ahead_device, behind_device = device_at(at + 1), device_at(at - 1)

    barrier = pltpu.get_barrier_semaphore()
    for near in ({"dp": sibling}, {"dp": ahead_device}, {"dp": behind_device}, {"tp": 1 - tp}):
        pl.semaphore_signal(barrier, inc=1, device_id=near, device_id_type=pl.DeviceIdType.MESH)

    def remote(src, dst, send, recv, device):
        return pltpu.make_async_remote_copy(
            src_ref=src, dst_ref=dst, send_sem=send, recv_sem=recv, device_id=device,
            device_id_type=pl.DeviceIdType.MESH,
        )

    def weight_loads(chunk):
        cut = pl.ds(chunk * units, units)
        return (
            pltpu.make_async_copy(wout_hbm.at[cut, :], w_own.at[0, chunk], load_sem.at[chunk, 0]),
            pltpu.make_async_copy(win_hbm.at[:, cut], w_own.at[1, chunk], load_sem.at[chunk, 1]),
        )

    row_loads = (
        pltpu.make_async_copy(second_hbm.at[pl.ds(0, pairs)], s_all, load_sem.at[2, 0]),
        pltpu.make_async_copy(grad_hbm.at[pl.ds(0, pairs)], g_all, load_sem.at[2, 1]),
    )
    for load in (*weight_loads(0), *row_loads, *weight_loads(1)):
        load.start()
    bias_grad[...] = jnp.zeros_like(bias_grad)
    pl.semaphore_wait(barrier, 4)

    def far_copy(chunk):
        return remote(
            w_own.at[core, chunk], w_far.at[core, chunk], far_sem.at[0, chunk], far_sem.at[1, chunk], {"tp": 1 - tp}
        )

    def pass_copy(chunk):
        return remote(
            w_far.at[core, chunk], w_far.at[core, chunk], far_sem.at[2, chunk], far_sem.at[3, chunk], {"dp": sibling}
        )

    bias_copy = remote(bias, bias_far, bias_sem.at[0], bias_sem.at[1], {"tp": 1 - tp})
    bias_copy.start()
    for load in weight_loads(0):
        load.wait()
    far_copy(0).start()
    for load in row_loads:
        load.wait()

    def reach(matrix, way):
        return 3 + jnp.where(matrix == way, 1, 0)

    def segment(chunk, matrix, index):
        index = lax.rem(index + 2 * RING, RING)
        return dw.at[chunk, core, pl.ds(pl.multiple_of(matrix * half + index * SEG, SEG), SEG)]

    def sign(way):
        return 1 - 2 * way

    def toward(way):
        return {"dp": jnp.where(way == 0, ahead_device, behind_device)}

    def part_of(ref, chunk, matrix, which):
        return ref.at[chunk, which, pl.ds(pl.multiple_of(matrix * half, half), half)]

    def landing(chunk, matrix):
        return traded.at[chunk, pl.ds(pl.multiple_of(matrix * half, half), half)]

    def core_copy(chunk, matrix):
        return remote(
            part_of(dw, chunk, matrix, 1 - core), landing(chunk, matrix),
            core_sem.at[0, chunk, matrix], core_sem.at[1, chunk, matrix], {"dp": sibling},
        )

    def back_copy(chunk, matrix):
        return remote(
            part_of(dw, chunk, matrix, core), landing(chunk, matrix),
            core_sem.at[2, chunk, matrix], core_sem.at[3, chunk, matrix], {"dp": sibling},
        )

    def result_copies(chunk, matrix):
        return (
            pltpu.make_async_copy(
                part_of(dw, chunk, matrix, core), part_of(dw_hbm, chunk, matrix, core), result_sem.at[0, chunk, matrix]
            ),
            pltpu.make_async_copy(
                landing(chunk, matrix), part_of(dw_hbm, chunk, matrix, 1 - core), result_sem.at[1, chunk, matrix]
            ),
        )

    def hop_copy(chunk, matrix, way, hop, src):
        slot = way * 4 + hop - 1
        return remote(
            src, hops.at[chunk, matrix, slot], ring_send.at[chunk, matrix, slot], ring_recv.at[chunk, matrix, slot], toward(way)
        )

    def hop_arrived(chunk, matrix, way, hop):
        slot = hops.at[chunk, matrix, way * 4 + hop - 1]
        hop_copy(chunk, matrix, way, hop, slot).wait_recv()
        return slot

    def spread_copy(chunk, matrix, way, hop, index):
        slot = 8 + way * 4 + hop - 1
        place = segment(chunk, matrix, index)
        return remote(
            place, place, ring_send.at[chunk, matrix, slot], ring_recv.at[chunk, matrix, slot], toward(way)
        )

    def service(chunk, matrix, turn):
        @pl.when(turn == 0)
        def _():
            core_copy(chunk, matrix).wait()

            @pl.loop(0, RING)
            def _(index):
                mine = segment(chunk, matrix, index)
                theirs = traded.at[chunk, pl.ds(pl.multiple_of(matrix * half + index * SEG, SEG), SEG)]
                mine[...] = (mine[...].astype(F32) + theirs[...].astype(F32)).astype(BF16)

            pl.semaphore_signal(
                free_sem.at[chunk, matrix], inc=1, device_id={"dp": sibling}, device_id_type=pl.DeviceIdType.MESH
            )

            @pl.loop(0, 2)
            def _(way):
                begin = starts.at[chunk, matrix, way]
                begin[...] = segment(chunk, matrix, at + sign(way) * reach(matrix, way))[...]
                hop_copy(chunk, matrix, way, 1, begin).start()

        @pl.when((turn >= 1) & (turn <= 3))
        def _():
            hop = turn + 1

            @pl.loop(0, 2)
            def _(way):
                @pl.when(hop <= reach(matrix, way))
                def _():
                    slot = hop_arrived(chunk, matrix, way, hop - 1)
                    own = segment(chunk, matrix, at + sign(way) * (reach(matrix, way) - hop + 1))
                    slot[...] = (slot[...].astype(F32) + own[...].astype(F32)).astype(BF16)
                    hop_copy(chunk, matrix, way, hop, slot).start()

        @pl.when(turn == 4)
        def _():
            own = segment(chunk, matrix, at)
            total = own[...].astype(F32)
            for way in range(2):
                total = total + hop_arrived(chunk, matrix, way, reach(matrix, way))[...].astype(F32)
            own[...] = total.astype(BF16)
            for way in range(2):
                spread_copy(chunk, matrix, way, 1, at).start()

        @pl.when((turn >= 5) & (turn <= 7))
        def _():
            hop = turn - 3

            @pl.loop(0, 2)
            def _(way):
                @pl.when(hop <= reach(matrix, way))
                def _():
                    index = at - sign(way) * (hop - 1)
                    spread_copy(chunk, matrix, way, hop - 1, index).wait_recv()
                    spread_copy(chunk, matrix, way, hop, index).start()

        @pl.when(turn == 8)
        def _():
            for way in range(2):
                last = reach(matrix, way)
                spread_copy(chunk, matrix, way, last, at - sign(way) * last).wait_recv()
            pl.semaphore_wait(free_sem.at[chunk, matrix], 1)
            back_copy(chunk, matrix).start()

        @pl.when(turn == LAST_TURN)
        def _():
            back_copy(chunk, matrix).wait_recv()
            for result in result_copies(chunk, matrix):
                result.start()

    def serve(*turns):
        @pl.loop(0, 4)
        def _(block):
            turn = sum(jnp.where(block == number, value, 0) for number, value in enumerate(turns))

            @pl.when((turn >= 0) & (turn <= LAST_TURN))
            def _():
                service(lax.div(block, 2), lax.rem(block, 2), turn)

    def rows_of(ref, pair):
        return ref[pair].reshape(flat)

    depth = pairs * 2 * rows
    odd_turns, even_turns = pairs // 2, (pairs - 1) // 2

    @pl.loop(0, 2)
    def _(chunk):
        @pl.when(chunk == 1)
        def _():
            for load in weight_loads(1):
                load.wait()

        @pl.loop(0, pairs)
        def _(pair):
            s, g = rows_of(s_all, pair), rows_of(g_all, pair)

            def head(start):
                cut = slice(start, start + sub)
                place = pl.ds(pl.multiple_of(chunk * units + start, 128), sub)
                return (
                    dot(s, w_own[1, chunk, :, cut], 1, 0) + bias[:, place],
                    dot(g, w_own[0, chunk, cut, :], 1, 1),
                )

            ahead = head(0)
            for start in range(0, units, sub):
                pre, act_grad = ahead
                if start + sub < units:
                    ahead = head(start + sub)
                act, slope = gelu_parts(pre)
                pre_grad = (act_grad * slope).astype(BF16)
                cut = slice(start, start + sub)
                place = pl.ds(pl.multiple_of(chunk * units + start, 128), sub)
                acts[chunk, pair, :, :, cut] = act.reshape(2, rows, sub)
                grads[chunk, pair, :, :, cut] = pre_grad.reshape(2, rows, sub)
                bias_grad[:, place] += row_sums(pre_grad.astype(F32))

            @pl.when((chunk == 1) & (pair > 0))
            def _():
                odd = lax.rem(pair, 2) == 1
                serve(jnp.where(odd, lax.div(pair + 1, 2), -1), jnp.where(odd, -1, lax.div(pair, 2) - 1), -1, -1)

        for matrix in range(2):

            @pl.loop(0, 2)
            def _(part):
                cut = pl.ds(pl.multiple_of(part * half, half), half)
                if matrix == 0:
                    left, right = acts[chunk, :, :, :, cut], g_all[...]
                else:
                    left, right = s_all[:, :, :, cut], grads[chunk]
                grad = dot(left.reshape(depth, half), right.reshape(depth, width), 0, 0)
                dw[chunk, part, matrix * half : (matrix + 1) * half] = grad.astype(BF16)

                @pl.when(chunk == 1)
                def _():
                    serve(
                        jnp.where(part == 1, odd_turns + 1 + matrix, -1), jnp.where(part == 0, even_turns + matrix, -1), -1, -1
                    )

            core_copy(chunk, matrix).start()
            if matrix == 0:

                @pl.when(chunk == 1)
                def _():
                    far_copy(0).wait_recv()
                    pass_copy(0).start()
                    far_copy(1).start()

        serve(jnp.where(chunk == 0, 0, -1), -1, jnp.where(chunk == 0, -1, 0), -1)

    bias_copy.wait()

    def out_copies(pair):
        return (
            pltpu.make_async_copy(acts.at[0, pair], branch_hbm.at[pair], out_sem.at[0, pair]),
            pltpu.make_async_copy(grads.at[0, pair], second_grad_hbm.at[pair], out_sem.at[1, pair]),
        )

    @pl.loop(0, 2)
    def _(chunk):
        pass_copy(chunk).wait_recv()

        @pl.loop(0, pairs)
        def _(pair):
            done = chunk * pairs + pair

            @pl.when(chunk == 0)
            def _():
                out = sum(dot(rows_of(acts.at[own], pair), w_own[0, own], 1, 0) for own in range(2))
                grad_out = sum(dot(rows_of(grads.at[own], pair), w_own[1, own], 1, 1) for own in range(2))
                acts[0, pair] = out.reshape(packed).astype(BF16)
                grads[0, pair] = grad_out.reshape(packed).astype(BF16)

                @pl.when(pair == pairs - 1)
                def _():
                    far_copy(1).wait_recv()
                    pass_copy(1).start()

            serve(odd_turns + 3 + done, -1, 1 + done, -1)
            out, grad_out = far_units(
                sub, rows_of(s_all, pair), rows_of(g_all, pair), w_far.at[1, chunk],
                bias_far.at[:, pl.ds(pl.multiple_of(chunk * units, units), units)], w_far.at[0, chunk],
                rows_of(acts.at[0], pair).astype(F32), rows_of(grads.at[0], pair).astype(F32),
            )
            acts[0, pair] = out.reshape(packed).astype(BF16)
            grads[0, pair] = grad_out.reshape(packed).astype(BF16)

            @pl.when(chunk == 1)
            def _():
                for copy in out_copies(pair):
                    copy.start()

            serve(-1, even_turns + 2 + done, -1, done)

    @pl.loop(0, 2)
    def _(chunk):
        far_copy(chunk).wait_send()
        pass_copy(chunk).wait_send()

        @pl.loop(0, 2)
        def _(matrix):
            back_copy(chunk, matrix).wait_send()
            for result in result_copies(chunk, matrix):
                result.wait()

            @pl.loop(0, 2)
            def _(way):
                @pl.loop(1, reach(matrix, way) + 1)
                def _(hop):
                    hop_copy(chunk, matrix, way, hop, hops.at[chunk, matrix, way * 4 + hop - 1]).wait_send()
                    spread_copy(chunk, matrix, way, hop, at).wait_send()

    @pl.loop(0, pairs)
    def _(pair):
        for copy in out_copies(pair):
            copy.wait()


def channel_call(pairs, collective_id, second, out_grad, channel_in, bias_row, channel_out):
    batch, rows, width = second.shape
    own = channel_in.shape[1]
    units = own // 2
    half = units // 2
    shape = jax.ShapeDtypeStruct
    slots = (batch // 2, 2, rows, width)
    anywhere = pl.BlockSpec(memory_space=pl.ANY)
    vmem = pl.BlockSpec(memory_space=pltpu.VMEM)
    dma = pltpu.SemaphoreType.DMA
    held = (pairs, 2, rows, width)
    branch, second_grad, dw, bias_grad = pl.pallas_call(
        functools.partial(channel_kernel, 256),
        name=f"channel_{pairs}",
        out_shape=[
            shape(slots, BF16), shape(slots, BF16), shape((2, 2, 2 * half, width), BF16), shape((8, own), F32),
        ],
        in_specs=[anywhere] * 4 + [vmem],
        out_specs=[anywhere] * 3 + [vmem],
        scratch_shapes=[
            pltpu.VMEM(held, BF16), pltpu.VMEM(held, BF16),
            pltpu.VMEM((2,) + held, BF16), pltpu.VMEM((2,) + held, BF16),
            pltpu.VMEM((2, 2, units, width), BF16), pltpu.VMEM((2, 2, units, width), BF16),
            pltpu.VMEM((1, own), F32),
            pltpu.VMEM((2, 2, 2 * half, width), BF16), pltpu.VMEM((2, 2 * half, width), BF16),
            pltpu.VMEM((2, 2, 2, SEG, width), BF16), pltpu.VMEM((2, 2, 8, SEG, width), BF16),
            dma((3, 2)), dma((2, pairs)), dma((2,)), dma((4, 2)), dma((4, 2, 2)),
            dma((2, 2, 2)), dma((2, 2, 16)), dma((2, 2, 16)), pltpu.SemaphoreType.REGULAR((2, 2)),
        ],
        cost_estimate=pl.CostEstimate(
            flops=40 * pairs * rows * width * units, bytes_accessed=40 << 20, transcendentals=0
        ),
        compiler_params=pltpu.CompilerParams(
            vmem_limit_bytes=CHANNEL_VMEM, collective_id=collective_id, has_side_effects=True
        ),
    )(second.reshape(slots), out_grad.reshape(slots), channel_in, channel_out, bias_row)
    packed = (batch, rows, width)
    return branch.reshape(packed), second_grad.reshape(packed), dw.reshape(2, 2, 2, half, width), bias_grad


def channel_general(size, meta, core, second, out_grad, channel_in, bias_row, channel_out):
    batch, rows, width = second.shape
    own = channel_in.shape[1]
    units = own // 2
    pairs = batch // 2
    packed = (batch, rows, width)
    shape = jax.ShapeDtypeStruct
    pair = pair_spec(rows, width)

    tp_swap = [(0, 1), (1, 0)]
    far_bias = lax.ppermute(bias_row, "tp", tp_swap)
    far = []
    for index in range(2):
        cut = slice(index * units, (index + 1) * units)
        out_cut, in_cut = channel_out[cut, :], channel_in[:, cut]
        got = lax.ppermute(jnp.where(core == 0, out_cut, in_cut), "tp", tp_swap)
        traded = swap(got, 1, size)
        far.append((jnp.where(core == 0, traded, got), jnp.where(core == 0, got, traded)))

    hidden = []
    for index in range(2):
        hidden.append(call(
            functools.partial(hidden_kernel, 256), "hidden_own", (pairs,),
            (meta, second, out_grad, channel_in, bias_row, channel_out),
            [
                pair, pair,
                pl.BlockSpec((width, units), lambda j, meta, index=index: (0, index)),
                pl.BlockSpec((1, units), lambda j, meta, index=index: (0, index)),
                pl.BlockSpec((units, width), lambda j, meta, index=index: (index, 0)),
            ],
            [shape((batch, rows, units), BF16)] * 2 + [shape((2, width // 2, width), BF16)] * 2 + [shape((8, units), F32)],
            [pair_spec(rows, units)] * 2
            + [pl.BlockSpec((2, width // 2, width), lambda j, meta: (0, 0, 0))] * 2
            + [pl.BlockSpec((8, units), lambda j, meta: (0, 0))],
            [pltpu.VMEM((units, width), F32), pltpu.VMEM((width, units), F32)],
            flops=8 * batch * rows * width * units, traffic=8 * batch * rows * width,
        ))
    dw = jnp.stack([sum_over_dp(h[3], h[2], size) for h in hidden])
    mats = (channel_in, channel_out, far[0][0], far_bias[:, :units], far[0][1])
    parts = call(
        functools.partial(far_first_kernel, 256), "far_first", (pairs,),
        (meta, second, out_grad, hidden[0][0], hidden[0][1], hidden[1][0], hidden[1][1], *mats),
        [pair] * 2 + [pair_spec(rows, units)] * 4 + [whole_spec(m) for m in mats],
        [shape(packed, F32)] * 2, [pair] * 2,
        flops=16 * batch * rows * width * units, traffic=20 * batch * rows * width,
    )
    mats = (far[1][0], far_bias[:, units:], far[1][1])
    branch, second_grad = call(
        functools.partial(far_last_kernel, 256), "far_last", (pairs,),
        (meta, second, out_grad, *parts, *mats),
        [pair] * 4 + [whole_spec(m) for m in mats],
        [shape(packed, BF16)] * 2, [pair] * 2,
        flops=8 * batch * rows * width * units, traffic=20 * batch * rows * width,
    )
    return branch, second_grad, dw, jnp.concatenate([h[4] for h in hidden], axis=1)


def shards(
    size,
    images, cotangent, image_counts, skip_mask, first_gain, first_bias, token_in, token_in_bias,
    token_out, token_out_bias, second_gain, second_bias, channel_in, channel_in_bias, channel_out,
    channel_out_bias,
):
    batch, patches, width = images.shape
    tokens = token_in.shape[1]
    own = channel_in.shape[1]
    rows = -(-patches // 16) * 16
    units = own // 2
    half = units // 2
    pairs = batch // 2
    core = lax.axis_index("dp") & 1
    shape = jax.ShapeDtypeStruct
    packed = (batch, rows, width)
    block = patches * width
    anywhere = pl.BlockSpec(memory_space=pl.ANY)
    vmem = pl.BlockSpec(memory_space=pltpu.VMEM)
    smem = pl.BlockSpec(memory_space=pltpu.SMEM)
    dma = pltpu.SemaphoreType.DMA
    images_t, cotangent_t = jnp.transpose(images, (1, 0, 2)), jnp.transpose(cotangent, (1, 0, 2))
    split = pltpu.VMEM((width // 128, patches * batch, 128), F32)

    def row(vector):
        return jnp.pad(vector, (0, width - vector.shape[0]))

    vectors = jnp.stack([
        row(v) for v in (first_gain, first_bias, second_gain, second_bias, channel_out_bias, token_in_bias, token_out_bias)
    ])
    bias_row = channel_in_bias.reshape(1, own)

    moved = (MOVE, rows, width)
    meta, most, sent_images, sent_cotangents = pl.pallas_call(
        share_kernel,
        name="share",
        out_shape=[
            shape((VALID + batch,), jnp.int32), shape((1,), jnp.int32), shape(moved, BF16), shape(moved, BF16),
        ],
        in_specs=[smem, smem, anywhere, anywhere],
        out_specs=[smem, smem, vmem, vmem],
        scratch_shapes=[
            pltpu.VMEM((patches, batch, width), BF16), pltpu.VMEM((patches, batch, width), BF16), split, split,
            pltpu.VMEM((8, 128), jnp.int32), pltpu.VMEM((size, 8, 128), jnp.int32),
            pltpu.SMEM((size, 128), jnp.int32), dma((size,)), dma((size,)), dma, dma((2,)),
        ],
        compiler_params=pltpu.CompilerParams(
            vmem_limit_bytes=VMEM_LIMIT, collective_id=SHARE_ID, has_side_effects=True
        ),
    )(image_counts, skip_mask, images_t, cotangent_t)
    got_images, got_cotangents = swap(sent_images, 1, size), swap(sent_cotangents, 1, size)

    whole_one = lambda array: pl.BlockSpec(array.shape, lambda j, meta: (0,) * array.ndim, pipeline_mode=pl.Buffered(1))
    any_pair = pl.BlockSpec((2, rows, width), lambda j, meta: (j, 0, 0))
    last_kept = lambda j, meta: jnp.minimum(j, jnp.maximum((meta[KEPT] + 1) // 2 - 1, 0))
    kept_pair = lambda r: pl.BlockSpec((2, r, width), lambda j, meta: (last_kept(j, meta), 0, 0))
    native = shape((patches, batch, width), F32)
    smalls = [
        shape((8, width), F32), shape((rows, tokens), BF16), shape((tokens, rows), BF16), shape((rows, tokens), BF16),
        shape((tokens, rows), BF16), shape((tokens, 1), F32), shape((rows, 1), F32),
    ]
    token_out_t = token_out.T
    (
        second, out_grad, middle, source, out_bias_grad, tin, tin_t, tout_t, tout, tin_bias, tout_bias, activations, input_grad,
    ) = call(
        token_forward_kernel, "token_forward", (pairs,),
        (meta, images_t, cotangent_t, vectors, token_in, token_out_t),
        [whole_one(v) for v in (images_t, cotangent_t, vectors, token_in, token_out_t)],
        [shape(packed, BF16), shape(packed, BF16), shape((batch, patches, width), F32), shape(packed, BF16)] + smalls + [native] * 2,
        [any_pair, any_pair, kept_pair(patches), kept_pair(rows)] + [whole_one(v) for v in smalls] + [anywhere] * 2,
        [
            pltpu.VMEM((width // 128, patches, batch, 128), F32), pltpu.VMEM((width // 128, patches, batch, 128), F32),
            pltpu.VMEM((patches, 128), F32), dma((batch, 2 * (width // 128))),
        ],
        flops=4 * batch * rows * width * tokens * 4, traffic=batch * block * 12,
    )
    second, out_grad, middle, source, out_bias_grad = pl.pallas_call(
        token_received_kernel,
        name="token_received",
        out_shape=[shape(packed, BF16), shape(packed, BF16), shape((batch, patches, width), F32), shape(packed, BF16), shape((8, width), F32)],
        in_specs=[smem] + [vmem] * 8 + [anywhere] * 4,
        out_specs=[anywhere] * 4 + [vmem],
        scratch_shapes=[
            pltpu.VMEM(moved, BF16), pltpu.VMEM(moved, BF16), pltpu.VMEM((MOVE, patches, width), F32), dma((4, MOVE)),
        ],
        input_output_aliases={9: 0, 10: 1, 11: 2, 12: 3},
        compiler_params=pltpu.CompilerParams(vmem_limit_bytes=VMEM_LIMIT),
    )(
        meta, got_images, got_cotangents, vectors, tin_t, tin_bias, tout_t, tout_bias, out_bias_grad,
        second, out_grad, middle, source,
    )

    operands = (second, out_grad, channel_in, bias_row, channel_out)
    general = functools.partial(channel_general, size, meta, core)
    if size == 2 * RING:
        fast = [functools.partial(channel_call, p, i + 1) for i, p in enumerate(FAST_PAIRS)]
        branch_at = sum((most[0] > 2 * p).astype(jnp.int32) for p in FAST_PAIRS[:-1])
        branch, second_grad, dw, in_bias_grad = lax.switch(branch_at, fast, *operands)
    else:
        branch, second_grad, dw, in_bias_grad = general(*operands)

    def item_specs(own_items):
        def index(place):
            def at(j, meta):
                if own_items:
                    return jnp.minimum(2 * j + place, jnp.maximum(meta[KEPT] - 1, 0)), 0, 0
                return jnp.minimum(meta[KEPT] + jnp.minimum(2 * j + place, jnp.maximum(meta[RECEIVED] - 1, 0)), batch - 1), 0, 0
            return at
        return [pl.BlockSpec((1, r, width), index(place)) for r in (rows, rows, patches, rows, rows) for place in range(2)]

    items = [a for a in (source, out_grad, middle, branch, second_grad) for _ in range(2)]
    consts = (vectors, tin, tin_t, tin_bias, tout)
    sums = [
        shape((rows, tokens), F32), shape((rows, tokens), F32), shape((rows, 128), F32),
        shape((4, 8, width), F32),
    ]
    stage = [pltpu.VMEM((2, 2, 2, patches, width), F32), dma((2, 2, 2))]
    returned = shape((patches, MOVE, width), F32)
    back_images, back_grads, *partial = call(
        functools.partial(token_backward_kernel, False), "token_backward_received", (MOVE // 2,),
        (meta, *items, *consts),
        item_specs(False) + [whole_one(c) for c in consts],
        [returned] * 2 + sums, [anywhere] * 2 + [whole_one(v) for v in sums],
        stage, flops=10 * MOVE * rows * width * tokens, traffic=MOVE * block * 24,
    )
    back_images, back_grads = swap(back_images, 1, size), swap(back_grads, 1, size)
    in_rows, out_rows = width // pairs, own // pairs
    in_turns, out_turns = half // in_rows, half // out_rows
    first_alias = 1 + len(items) + len(consts) + len(sums) + 3
    activations, input_grad, *partial, in_grad_sum, out_grad_sum = call(
        functools.partial(token_backward_kernel, True), "token_backward", (pairs,),
        (meta, *items, *consts, *partial, dw, dw, dw, activations, input_grad),
        item_specs(True) + [whole_one(c) for c in consts] + [whole_one(v) for v in sums]
        + [
            pl.BlockSpec((1, 1, 1, in_rows, width), lambda t, meta, c=c: (c, t // in_turns, 1, t % in_turns, 0))
            for c in range(2)
        ]
        + [pl.BlockSpec(
            (1, 1, 1, out_rows, width),
            lambda t, meta: (t // (2 * out_turns), (t // out_turns) % 2, 0, t % out_turns, 0),
        )]
        + [anywhere] * 2,
        [native] * 2 + sums + [shape((width, own), F32), shape((own, width), F32)],
        [anywhere] * 2 + [whole_one(v) for v in sums]
        + [pl.BlockSpec((in_rows, own), lambda t, meta: (t, 0)), pl.BlockSpec((out_rows, width), lambda t, meta: (t, 0))],
        stage, flops=10 * batch * rows * width * tokens, traffic=batch * block * 24,
        aliases={first_alias: 0, first_alias + 1: 1},
    )
    tin_grad, tout_grad, tout_bias_grad, gains = partial
    if size == 2 * RING:
        summed = pl.pallas_call(
            small_sum_kernel,
            name="small_sum",
            out_shape=shape((PACKED, width), F32),
            in_specs=[vmem] * 6,
            out_specs=vmem,
            scratch_shapes=[
                pltpu.VMEM((2, PACKED // 2, width), F32), pltpu.VMEM((PACKED // 2, width), F32),
                pltpu.VMEM((PACKED // 2, width), BF16), pltpu.VMEM((PACKED // 2, width), BF16),
                pltpu.VMEM((PACKED // 2, width), BF16), pltpu.VMEM((RING, PACKED // 2 // RING, width), BF16),
                dma((4,)), dma((RING,)), dma((RING,)), dma((RING,)), dma((RING,)),
            ],
            compiler_params=pltpu.CompilerParams(
                vmem_limit_bytes=VMEM_LIMIT, collective_id=SUM_ID, has_side_effects=True
            ),
        )(tin_grad, tout_grad, tout_bias_grad, gains, in_bias_grad, out_bias_grad)
    else:
        summed = lax.psum(pack_small(
            tin_grad, tout_grad, tout_bias_grad, gains, in_bias_grad, out_bias_grad
        ), "dp")
    lines = [tokens, patches, width, width, width, width, own, width]
    activations, input_grad, tin_sum, tout_sum, *vectors_sum = pl.pallas_call(
        place_kernel,
        name="place",
        out_shape=[native] * 2 + [shape((patches, tokens), F32)] * 2 + [shape((-(-n // 128), 128), F32) for n in lines],
        in_specs=[smem] + [anywhere] * 4 + [vmem],
        out_specs=[anywhere] * 2 + [vmem] * 10,
        scratch_shapes=[pltpu.VMEM((2, MOVE, patches, width), F32), dma((2, 2, MOVE))],
        input_output_aliases={3: 0, 4: 1},
        compiler_params=pltpu.CompilerParams(vmem_limit_bytes=VMEM_LIMIT),
    )(meta, back_images, back_grads, activations, input_grad, summed)
    activations, input_grad = jnp.transpose(activations, (1, 0, 2)), jnp.transpose(input_grad, (1, 0, 2))
    tin_b, tout_b, gain1, shift1, gain2, shift2, in_b, out_b = [v.reshape(-1)[:n] for v, n in zip(vectors_sum, lines)]
    small = (gain1, shift1, tin_sum, tin_b, tout_sum.T, tout_b, gain2, shift2, in_b, out_b)
    return (activations, input_grad, *small[:8], in_grad_sum, small[8], out_grad_sum, small[9])


def solution(mesh):
    placed = (
        P("dp", None, None), P("dp", None, None), P("dp"), P("dp"), P(), P(), P(), P(), P(), P(), P(), P(),
        P(None, "tp"), P("tp"), P("tp", None), P(),
    )
    return jax.shard_map(
        functools.partial(shards, mesh.shape["dp"]),
        mesh=mesh,
        in_specs=placed,
        out_specs=(
            P("dp", None, None), P("dp", None, None), P(), P(), P(), P(), P(), P(), P(), P(),
            P(None, "tp"), P("tp"), P("tp", None), P(),
        ),
        check_vma=False,
    )
```

```python
import functools

import jax
import jax.numpy as jnp
from jax import lax
from jax.experimental import pallas as pl
from jax.experimental.pallas import tpu as pltpu
from jax.sharding import PartitionSpec as P

EPSILON = 1e-06
ROOT_HALF = 0.7071067811865476
INV_ROOT_TAU = 0.3989422804014327
F32, BF16 = jnp.float32, jnp.bfloat16
VMEM_LIMIT = 60 * 1024 * 1024
CHANNEL_VMEM = 60 * 1024 * 1024
RING, SEG, LAST_TURN = 8, 48, 9
PIECES = (256, 512)
FAST_PAIRS = (6, 8)
SHARE_ID, SUM_ID = 9, 10
PACKED = 256

MOVE = 4
N_LIVE, KEPT, RECEIVED, N_PAIRS, CORE, GIVEN, LIST, VALID = 0, 1, 2, 3, 4, 5, 8, 24
GAIN1, SHIFT1, GAIN2, SHIFT2, OUT_BIAS, TIN_BIAS, TOUT_BIAS = range(7)


def dot(left, right, left_dim, right_dim):
    return lax.dot_general(
        left, right, (((left_dim,), (right_dim,)), ((), ())), preferred_element_type=F32
    )


def gelu_parts(values):
    half = 0.5 * (1.0 + lax.erf(values * ROOT_HALF))
    slope = half + values * (INV_ROOT_TAU * jnp.exp(-0.5 * values * values))
    return (values * half).astype(BF16), slope


def gelu_only(values):
    return (values * (0.5 * (1.0 + lax.erf(values * ROOT_HALF)))).astype(BF16)


def standardize(values):
    width = values.shape[-1]
    center = jnp.sum(values, axis=-1, keepdims=True) * (1.0 / width)
    deviation = values - center
    scale = lax.rsqrt(
        jnp.sum(deviation * deviation, axis=-1, keepdims=True) * (1.0 / width) + EPSILON
    )
    return deviation * scale, scale


def norm_back(grad_hat, hat, scale):
    width = hat.shape[-1]
    first = jnp.sum(grad_hat, axis=-1, keepdims=True) * (1.0 / width)
    second = jnp.sum(grad_hat * hat, axis=-1, keepdims=True) * (1.0 / width)
    return scale * (grad_hat - first - hat * second)


def pad_rows(values, rows):
    return jnp.concatenate(
        [values, jnp.zeros((rows - values.shape[0], values.shape[1]), values.dtype)], axis=0
    )


def row_sums(values):
    rows, width = values.shape
    return jnp.sum(values.reshape(rows // 8, 8, width), axis=0)


def lane_sums(values):
    total = values[:, :128]
    for at in range(128, values.shape[1], 128):
        total = total + values[:, at : at + 128]
    return total


def split_lanes(source, target, pieces):
    patches, images, width = source.shape
    step = patches // pieces
    for piece in range(pieces):
        rows = source[piece * step : (piece + 1) * step].astype(F32).reshape(step * images, width)
        for group in range(width // 128):
            target[group, piece * step * images : (piece + 1) * step * images, :] = rows[:, group * 128 : (group + 1) * 128]


def one_image(split, index, images):
    patches = split.shape[1] // images
    return jnp.concatenate(
        [split[group, pl.ds(index, patches, stride=images), :] for group in range(split.shape[0])], axis=1
    )


def share_kernel(
    counts, skips, images, cotangents, meta, most, sent_images, sent_cotangents,
    x_raw, c_raw, x_split, c_split, mine, gathered, gathered_smem, send_sem, recv_sem, local_sem, load_sem,
):
    slots = images.shape[1]
    rows = sent_images.shape[1]
    size = gathered.shape[0]
    me = lax.axis_index("dp")
    loads = [
        pltpu.make_async_copy(images, x_raw, load_sem.at[0]), pltpu.make_async_copy(cotangents, c_raw, load_sem.at[1]),
    ]
    for load in loads:
        load.start()
    barrier = pltpu.get_barrier_semaphore()

    def peer(step):
        return {"dp": lax.rem(me + step, size)}

    for step in range(1, size):
        pl.semaphore_signal(barrier, inc=1, device_id=peer(step), device_id_type=pl.DeviceIdType.MESH)
    one, none = jnp.int32(1), jnp.int32(0)
    valid, live, rank, total = [], [], [], none
    for slot in range(slots):
        valid.append(jnp.where(slot < counts[0], one, none))
        live.append(valid[slot] * skips[slot])
        rank.append(total)
        total = total + live[slot]
    mine[...] = jnp.zeros_like(mine) + total
    gathered[me] = mine[...]
    pl.semaphore_wait(barrier, size - 1)

    def send(step):
        return pltpu.make_async_remote_copy(
            src_ref=mine, dst_ref=gathered.at[me], send_sem=send_sem.at[step], recv_sem=recv_sem.at[step],
            device_id=peer(step), device_id_type=pl.DeviceIdType.MESH,
        )

    for step in range(1, size):
        send(step).start()
    for load, raw, split in zip(loads, (x_raw, c_raw), (x_split, c_split)):
        load.wait()
        split_lanes(raw, split, 14)
    place_of = [jnp.where(live[slot] == 1, rank[slot], total + slot - rank[slot]) for slot in range(slots)]
    for place in range(slots):
        index, ok = none, none
        for slot in range(slots):
            hit = jnp.where(place_of[slot] == place, one, none)
            index = index + hit * slot
            ok = ok + hit * valid[slot]
        meta[LIST + place] = index
        meta[VALID + place] = ok
    for place in range(MOVE):
        index = none
        for slot in range(slots):
            index = index + slot * live[slot] * jnp.where(rank[slot] == total - 1 - place, one, none)
        sent_images[place] = pad_rows(one_image(x_split, index, slots), rows).astype(BF16)
        sent_cotangents[place] = pad_rows(one_image(c_split, index, slots), rows).astype(BF16)
    for step in range(1, size):
        send(step).wait()
    local = pltpu.make_async_copy(gathered.at[:, 0, :], gathered_smem, local_sem)
    local.start()
    local.wait()

    def excess(left, right):
        return jnp.clip(lax.shift_right_arithmetic(left - right, one), 0, MOVE)

    fullest = none
    for chip in range(size // 2):
        left, right = gathered_smem[2 * chip, 0], gathered_smem[2 * chip + 1, 0]
        shift = excess(left, right) - excess(right, left)
        fullest = jnp.maximum(fullest, jnp.maximum(left - shift, right + shift))
    most[0] = fullest
    sibling = me + 1 - 2 * lax.rem(me, 2)
    there = gathered_smem[sibling, 0]
    given, received = excess(total, there), excess(there, total)
    kept = total - given
    for at, value in (
        (N_LIVE, total), (KEPT, kept), (RECEIVED, received),
        (N_PAIRS, lax.shift_right_arithmetic(kept + received + 1, one)), (CORE, lax.rem(me, 2)), (GIVEN, given),
    ):
        meta[at] = value


def column(row):
    return jnp.transpose(jnp.broadcast_to(row, (8, row.shape[1])))[:, :1]


def token_forward(sources, grads, vectors, tin_t, tin_bias, tout_t, tout_bias, rows):
    patches = sources[0].shape[0]
    normed = [
        pad_rows(standardize(x)[0] * vectors[GAIN1 : GAIN1 + 1] + vectors[SHIFT1 : SHIFT1 + 1], rows).astype(BF16)
        for x in sources
    ]
    pre = [dot(tin_t[...], n, 1, 0) + tin_bias[...] for n in normed]
    act = [gelu_only(p) for p in pre]
    branch = [dot(tout_t[...], a, 1, 0)[:patches] + tout_bias[:patches] for a in act]
    middle = [x + b for x, b in zip(sources, branch)]
    second = [
        pad_rows(standardize(m)[0] * vectors[GAIN2 : GAIN2 + 1] + vectors[SHIFT2 : SHIFT2 + 1], rows) for m in middle
    ]
    return middle, second, [pad_rows(g, rows) for g in grads]


def token_forward_kernel(
    meta, images, cotangents, vectors, tin, tout_in,
    second, out_grad, middle, source, grad_sum, tin_pad, tin_t, tout_t, tout, tin_bias, tout_bias, activations, input_grad,
    x_split, c_split, nothing, fill_sem,
):
    step = pl.program_id(0)
    steps = pl.num_programs(0)
    rows = second.shape[1]
    patches, slots, _ = images.shape

    groups = x_split.shape[0]
    x_rows, c_rows = (split.reshape(groups, patches * slots, 128) for split in (x_split, c_split))

    def fills(item, valid):
        index = meta[LIST + item]
        copies = []
        for number, (split, out) in enumerate(((x_split, activations), (c_split, input_grad))):
            for group in range(groups):
                copies.append(pltpu.make_async_copy(
                    split.at[group, :, index, :] if valid else nothing, out.at[:, index, pl.ds(group * 128, 128)],
                    fill_sem.at[item, number * groups + group],
                ))
        return copies

    @pl.when(step == 0)
    def _():
        piece = patches // 14

        @pl.loop(0, 14)
        def _(number):
            cut = pl.ds(number * piece, piece)
            for raw, split in ((images, x_split), (cotangents, c_split)):
                for group in range(groups):
                    split[group, cut] = raw[cut, :, group * 128 : (group + 1) * 128].astype(F32)

        nothing[...] = jnp.zeros_like(nothing)

        @pl.loop(meta[N_LIVE], slots)
        def _(item):
            @pl.when(meta[VALID + item] == 1)
            def _():
                for copy in fills(item, True):
                    copy.start()

            @pl.when(meta[VALID + item] == 0)
            def _():
                for copy in fills(item, False):
                    copy.start()

        grad_sum[...] = jnp.zeros_like(grad_sum)
        wide = pad_rows(tin[...].astype(F32), rows)
        tin_pad[...] = wide.astype(BF16)
        tin_t[...] = jnp.transpose(wide).astype(BF16)
        wide = pad_rows(tout_in[...].astype(F32), rows)
        tout_t[...] = wide.astype(BF16)
        tout[...] = jnp.transpose(wide).astype(BF16)
        tin_bias[...] = column(vectors[TIN_BIAS : TIN_BIAS + 1, : tin_bias.shape[0]])
        tout_bias[...] = column(vectors[TOUT_BIAS : TOUT_BIAS + 1, : tout_bias.shape[0]])

    def run(places):
        at = [meta[LIST + 2 * step + place] for place in places]
        sources = [one_image(x_rows, index, slots) for index in at]
        grads = [one_image(c_rows, index, slots) for index in at]
        mid, sec, gra = token_forward(sources, grads, vectors, tin_t, tin_bias, tout_t, tout_bias, rows)
        for place, m, s, g, x in zip(places, mid, sec, gra, sources):
            middle[place] = m
            second[place] = s.astype(BF16)
            out_grad[place] = g.astype(BF16)
            source[place] = pad_rows(x, rows).astype(BF16)
            grad_sum[...] += row_sums(g)

    @pl.when(2 * step + 1 < meta[KEPT])
    def _():
        run((0, 1))

    @pl.when(2 * step + 1 == meta[KEPT])
    def _():
        run((0,))
        second[1] = jnp.zeros_like(second[1])
        out_grad[1] = jnp.zeros_like(out_grad[1])

    @pl.when(2 * step >= meta[KEPT])
    def _():
        second[...] = jnp.zeros_like(second)
        out_grad[...] = jnp.zeros_like(out_grad)

    @pl.when(step == steps - 1)
    def _():
        @pl.loop(meta[N_LIVE], slots)
        def _(item):
            for copy in fills(item, False):
                copy.wait()


def token_received_kernel(
    meta, images, cotangents, vectors, tin_t, tin_bias, tout_t, tout_bias, grad_sum_in,
    second_in, out_grad_in, middle_in, source_in,
    second, out_grad, middle, source, grad_sum,
    second_one, grad_one, middle_one, sem,
):
    grad_sum[...] = grad_sum_in[...]
    rows = second_one.shape[1]
    patches = middle_one.shape[1]

    def copies(place):
        index = meta[KEPT] + place
        return [
            pltpu.make_async_copy(src.at[place], dst.at[index], sem.at[number, place])
            for number, (src, dst) in enumerate((
                (second_one, second), (grad_one, out_grad), (middle_one, middle), (images, source),
            ))
        ]

    @pl.loop(0, meta[RECEIVED])
    def _(place):
        x = images[place, :patches].astype(F32)
        mid, sec, gra = token_forward(
            [x], [cotangents[place, :patches].astype(F32)], vectors, tin_t, tin_bias, tout_t, tout_bias, rows
        )
        second_one[place] = sec[0].astype(BF16)
        grad_one[place] = gra[0].astype(BF16)
        middle_one[place] = mid[0]
        grad_sum[...] += row_sums(gra[0])
        for copy in copies(place):
            copy.start()

    @pl.loop(0, meta[RECEIVED])
    def _(place):
        for copy in copies(place):
            copy.wait()


def hidden_kernel(
    sub, meta, second, out_grad, win, win_bias, wout,
    act_out, pre_grad_out, sent, kept, bias_grad, wout_grad, win_grad,
):
    step, steps = pl.program_id(0), pl.num_programs(0)

    @pl.when(step == 0)
    def _():
        wout_grad[...] = jnp.zeros_like(wout_grad)
        win_grad[...] = jnp.zeros_like(win_grad)
        bias_grad[...] = jnp.zeros_like(bias_grad)

    @pl.when(step < meta[N_PAIRS])
    def _():
        pair, rows, width = second.shape
        s = second[...].reshape(pair * rows, width)
        g = out_grad[...].reshape(pair * rows, width)

        def head(at):
            cut = slice(at, at + sub)
            return dot(s, win[:, cut], 1, 0) + win_bias[:, cut], dot(g, wout[cut, :], 1, 1)

        units = win.shape[1]
        ahead = head(0)
        for at in range(0, units, sub):
            pre, act_grad = ahead
            if at + sub < units:
                ahead = head(at + sub)
            act, slope = gelu_parts(pre)
            grad = act_grad * slope
            pre_grad = grad.astype(BF16)
            cut = slice(at, at + sub)
            act_out[:, :, cut] = act.reshape(pair, rows, sub)
            pre_grad_out[:, :, cut] = pre_grad.reshape(pair, rows, sub)
            bias_grad[:, cut] += row_sums(pre_grad.astype(F32))
            wout_grad[cut, :] += dot(act, g, 0, 0)
            win_grad[:, cut] += dot(s, pre_grad, 0, 0)

    @pl.when(step == steps - 1)
    def _():
        half = kept.shape[1]
        mine = pl.ds(pl.multiple_of(meta[CORE] * half, half), half)
        other = pl.ds(pl.multiple_of((1 - meta[CORE]) * half, half), half)
        kept[0] = wout_grad[mine, :].astype(BF16)
        kept[1] = win_grad[mine, :].astype(BF16)
        sent[0] = wout_grad[other, :].astype(BF16)
        sent[1] = win_grad[other, :].astype(BF16)


def far_units(sub, s, g, win, win_bias, wout, out, grad_out):
    def head(cut):
        return dot(s, win[:, cut], 1, 0) + win_bias[:, cut], dot(g, wout[cut, :], 1, 1)

    cuts = groups_of(win.shape[1])
    ahead = head(cuts[0])
    for number, cut in enumerate(cuts):
        pre, act_grad = ahead
        if number + 1 < len(cuts):
            ahead = head(cuts[number + 1])
        act, slope = gelu_parts(pre)
        pre_grad = (act_grad * slope).astype(BF16)
        more, more_grad = dot(act, wout[cut, :], 1, 0), dot(pre_grad, win[:, cut], 1, 1)
        out = more if out is None else out + more
        grad_out = more_grad if grad_out is None else grad_out + more_grad
    return out, grad_out


def groups_of(units):
    sizes, cuts = PIECES, []
    start = 0
    while start < units:
        for size in sizes:
            cuts.append(slice(start, start + size))
            start += size
    return cuts


def far_first_kernel(
    sub, meta, second, out_grad, act0, grad0, act1, grad1, win_own, wout_own, win, win_bias, wout,
    out_part, grad_part,
):
    step = pl.program_id(0)

    @pl.when(step < meta[N_PAIRS])
    def _():
        pair, rows, width = second.shape
        flat = (pair * rows, width)
        s, g = second[...].reshape(flat), out_grad[...].reshape(flat)
        units = win.shape[1]
        out, grad_out = far_units(sub, s, g, win, win_bias, wout, None, None)
        for index, (act, pre_grad) in enumerate(((act0, grad0), (act1, grad1))):
            cut = slice(index * units, (index + 1) * units)
            out = out + dot(act[...].reshape(flat), wout_own[cut, :], 1, 0)
            grad_out = grad_out + dot(pre_grad[...].reshape(flat), win_own[:, cut], 1, 1)
        out_part[...] = out.reshape(pair, rows, width)
        grad_part[...] = grad_out.reshape(pair, rows, width)


def far_last_kernel(
    sub, meta, second, out_grad, out_part, grad_part, win, win_bias, wout, branch, second_grad,
):
    step = pl.program_id(0)

    @pl.when(step < meta[N_PAIRS])
    def _():
        pair, rows, width = second.shape
        flat = (pair * rows, width)
        s, g = second[...].reshape(flat), out_grad[...].reshape(flat)
        out, grad_out = far_units(
            sub, s, g, win, win_bias, wout, out_part[...].reshape(flat), grad_part[...].reshape(flat)
        )
        branch[...] = out.reshape(pair, rows, width).astype(BF16)
        second_grad[...] = grad_out.reshape(pair, rows, width).astype(BF16)


def token_backward_kernel(
    own, meta, *refs,
):
    items = [refs[2 * number : 2 * number + 2] for number in range(5)]
    images, grads, middles, branches, second_grads = items
    vectors, tin, tin_t, tin_bias, tout = refs[10:15]
    refs = refs[15:]
    if own:
        sums_in, refs = refs[:4], refs[4:]
        dw_in0, dw_in1, dw_out = refs[:3]
        refs = refs[5:]
    activations, input_grad = refs[:2]
    sums = refs[2:6]
    refs = refs[6:]
    if own:
        win_grad, wout_grad = refs[:2]
        refs = refs[2:]
    stage, stage_sem = refs
    tin_grad, tout_grad, tout_bias_grad, gains = sums
    step, steps = pl.program_id(0), pl.num_programs(0)
    patches, rows = middles[0].shape[1], images[0].shape[1]
    count = meta[KEPT] if own else meta[RECEIVED]

    @pl.when(step == 0)
    def _():
        for number, ref in enumerate(sums):
            ref[...] = sums_in[number][...] if own else jnp.zeros_like(ref)

    if own:
        units = dw_in0.shape[-1]
        win_grad[:, :units] = dw_in0[...].reshape(win_grad.shape[0], units).astype(F32)
        win_grad[:, units:] = dw_in1[...].reshape(win_grad.shape[0], units).astype(F32)
        wout_grad[...] = dw_out[...].reshape(wout_grad.shape).astype(F32)

    def copies(at_step, place):
        slot = lax.rem(at_step, 2)
        item = 2 * at_step + place
        if own:
            index = meta[LIST + item]
            targets = (activations.at[:, index, :], input_grad.at[:, index, :])
        else:
            targets = (activations.at[:, item, :], input_grad.at[:, item, :])
        return [
            pltpu.make_async_copy(stage.at[slot, place, number], target, stage_sem.at[slot, place, number])
            for number, target in enumerate(targets)
        ]

    def vector(row):
        return vectors[row : row + 1]

    def run(places):
        slot = lax.rem(step, 2)
        hat_width = middles[0].shape[2]
        middle = [middles[p][0] for p in places]
        norm2 = [standardize(m) for m in middle]
        grad2 = [second_grads[p][0].astype(F32)[:patches] for p in places]
        middle_grad = [
            grads[p][0].astype(F32)[:patches] + norm_back(g * vector(GAIN2), hat, scale)
            for p, g, (hat, scale) in zip(places, grad2, norm2)
        ]
        branch_grad = [pad_rows(m, rows).astype(BF16) for m in middle_grad]
        norm1 = [standardize(images[p][0].astype(F32)[:patches]) for p in places]
        ones = jnp.concatenate([jnp.ones((1, hat_width), F32), jnp.zeros((rows - patches - 1, hat_width), F32)], axis=0)
        normed = [
            jnp.concatenate([hat * vector(GAIN1) + vector(SHIFT1), ones], axis=0).astype(BF16) for hat, _ in norm1
        ]
        pre = [dot(tin_t[...], n, 1, 0) + tin_bias[...] for n in normed]
        act_grad = [dot(tout[...], b, 1, 0) for b in branch_grad]
        parts = [gelu_parts(p) for p in pre]
        pre_grad = [(a * slope).astype(BF16) for a, (_, slope) in zip(act_grad, parts)]
        normed_grad = [dot(tin[...], p, 1, 0)[:patches] for p in pre_grad]
        for p, m in zip(places, middle):
            stage[slot, p, 0] = m + (branches[p][0].astype(F32)[:patches] + vector(OUT_BIAS))
        for p, m, n, (hat, scale) in zip(places, middle_grad, normed_grad, norm1):
            stage[slot, p, 1] = m + norm_back(n * vector(GAIN1), hat, scale)
        for p in places:
            for copy in copies(step, p):
                copy.start()
        tout_grad[...] += sum(dot(b, act, 1, 1) for (act, _), b in zip(parts, branch_grad))
        tin_grad[...] += sum(dot(n, p, 1, 1) for n, p in zip(normed, pre_grad))
        tout_bias_grad[...] += sum(lane_sums(b.astype(F32)) for b in branch_grad)
        gains[0] += sum(row_sums(pad_rows(g * hat, rows)) for g, (hat, _) in zip(grad2, norm2))
        gains[1] += sum(row_sums(pad_rows(g, rows)) for g in grad2)
        gains[2] += sum(row_sums(pad_rows(n * hat, rows)) for n, (hat, _) in zip(normed_grad, norm1))
        gains[3] += sum(row_sums(pad_rows(n, rows)) for n in normed_grad)

    for place in range(2):

        @pl.when((step >= 2) & (2 * (step - 2) + place < count))
        def _():
            for copy in copies(step - 2, place):
                copy.wait()

    @pl.when(2 * step + 1 < count)
    def _():
        run((0, 1))

    @pl.when(2 * step + 1 == count)
    def _():
        run((0,))

    for place in range(2):
        for back in (1, 0):

            @pl.when((step == steps - 1) & (step >= back) & (2 * (step - back) + place < count))
            def _():
                for copy in copies(step - back, place):
                    copy.wait()


def place_kernel(
    meta, images, grads, activations_in, input_grad_in, summed,
    activations, input_grad,
    tin_out, tout_out, tin_bias_out, tout_bias_out, gain1_out, shift1_out, gain2_out, shift2_out, in_bias_out, out_bias_out,
    held, sem,
):
    def loads(place):
        return [
            pltpu.make_async_copy(back.at[:, place, :], held.at[number, place], sem.at[0, number, place])
            for number, back in enumerate((images, grads))
        ]

    def stores(place):
        index = meta[LIST + meta[N_LIVE] - 1 - place]
        return [
            pltpu.make_async_copy(held.at[number, place], out.at[:, index, :], sem.at[1, number, place])
            for number, out in enumerate((activations, input_grad))
        ]

    @pl.loop(0, meta[GIVEN])
    def _(place):
        for copy in loads(place):
            copy.start()

    patches, tokens = tin_out.shape
    rows = -(-patches // 16) * 16
    width = summed.shape[1]
    unfold = lambda v: jnp.concatenate([v[:, :tokens], v[:, tokens:]], axis=0)[:patches]
    tin_out[...] = unfold(summed[: rows // 2])
    tout_out[...] = unfold(summed[rows // 2 : rows])
    split = lambda row: jnp.concatenate([row[:, at : at + 128] for at in range(0, row.shape[1], 128)], axis=0)
    below = patches - rows // 2
    tin_bias_out[...] = split(summed[below : below + 1, tokens:])

    def vector(number, length=width):
        return split(summed[rows + number : rows + number + 1, : -(-length // 128) * 128])

    gain2_out[...], shift2_out[...], gain1_out[...], shift1_out[...] = (vector(number) for number in range(4))
    in_bias_out[...] = jnp.concatenate([vector(4), vector(5)], axis=0)
    out_bias_out[...] = vector(6)
    tout_bias_out[...] = vector(7, patches)

    @pl.loop(0, meta[GIVEN])
    def _(place):
        for load, store in zip(loads(place), stores(place)):
            load.wait()
            store.start()

    @pl.loop(0, meta[GIVEN])
    def _(place):
        for copy in stores(place):
            copy.wait()


def pack_small(tin_grad, tout_grad, tout_bias_grad, gains, in_bias_grad, out_bias_grad):
    rows, width = tin_grad.shape[0], out_bias_grad.shape[1]
    line = lambda v: jnp.sum(v, axis=0, keepdims=True)
    flat = lambda v: jnp.concatenate([v, jnp.zeros((1, width - v.shape[1]), F32)], axis=1)
    fold = lambda v: jnp.concatenate([v[: rows // 2], v[rows // 2 :]], axis=1)
    vectors = [line(gains[number]) for number in range(4)]
    in_bias = line(in_bias_grad)
    vectors += [in_bias[:, :width], in_bias[:, width:], line(out_bias_grad)]
    vectors += [flat(line(jnp.transpose(tout_bias_grad)))]
    return jnp.concatenate(
        [fold(tin_grad), fold(tout_grad)] + vectors + [jnp.zeros((PACKED - rows - len(vectors), width), F32)], axis=0
    )


def small_sum_kernel(
    tin_grad, tout_grad, tout_bias_grad, gains, in_bias_grad, out_bias_grad,
    summed,
    packed, landed, reduced, gathered, other, pieces, core_sem, sum_send, sum_recv, gather_send, gather_recv,
):
    width = packed.shape[-1]
    rows = tin_grad.shape[0]
    me = lax.axis_index("dp")
    core, chip = lax.rem(me, 2), lax.div(me, 2)
    sibling = me + 1 - 2 * core

    def chip_at(step):
        return lax.rem(chip + step, RING)

    def peer(step):
        return {"dp": 2 * chip_at(step) + core}

    barrier = pltpu.get_barrier_semaphore()
    for near in [{"dp": sibling}] + [peer(step) for step in range(1, RING)]:
        pl.semaphore_signal(barrier, inc=1, device_id=near, device_id_type=pl.DeviceIdType.MESH)

    def remote(src, dst, send, recv, device):
        return pltpu.make_async_remote_copy(
            src_ref=src, dst_ref=dst, send_sem=send, recv_sem=recv, device_id=device,
            device_id_type=pl.DeviceIdType.MESH,
        )

    everything = pack_small(
        tin_grad[...], tout_grad[...], tout_bias_grad[...], gains[...], in_bias_grad[...], out_bias_grad[...]
    )
    packed[0] = everything[: PACKED // 2]
    packed[1] = everything[PACKED // 2 :]
    pl.semaphore_wait(barrier, RING)

    swap_copy = remote(packed.at[1 - core], landed, core_sem.at[0], core_sem.at[1], {"dp": sibling})
    swap_copy.start()
    swap_copy.wait()
    packed[core] = packed[core] + landed[...]
    reduced[...] = packed[core].astype(BF16)
    piece = PACKED // 2 // RING

    def segment(ref, index):
        return ref.at[pl.ds(pl.multiple_of(index * piece, piece), piece)]

    def sum_copy(step):
        return remote(segment(reduced, chip_at(step)), pieces.at[step], sum_send.at[step], sum_recv.at[step], peer(step))

    for step in range(1, RING):
        sum_copy(step).start()
    total = segment(packed.at[core], chip)[...]
    for step in range(1, RING):
        sum_copy(step).wait()
        total = total + pieces[step].astype(F32)
    pieces[0] = total.astype(BF16)

    def gather_copy(step):
        return remote(
            pieces.at[0], segment(gathered, chip), gather_send.at[step], gather_recv.at[step], peer(step)
        )

    for step in range(1, RING):
        gather_copy(step).start()
    segment(gathered, chip)[...] = pieces[0]
    for step in range(1, RING):
        gather_copy(step).wait()
    back_copy = remote(gathered, other, core_sem.at[2], core_sem.at[3], {"dp": sibling})
    back_copy.start()
    back_copy.wait()
    summed[: PACKED // 2] = jnp.where(core == 0, gathered[...], other[...]).astype(F32)
    summed[PACKED // 2 :] = jnp.where(core == 0, other[...], gathered[...]).astype(F32)


def last_pair(step, meta):
    return jnp.minimum(step, jnp.maximum(meta[N_PAIRS] - 1, 0))


def pair_spec(rows, width):
    return pl.BlockSpec((2, rows, width), lambda j, meta: (last_pair(j, meta), 0, 0))


def whole_spec(array):
    zeros = (0,) * array.ndim
    return pl.BlockSpec(array.shape, lambda j, meta: zeros)


def call(body, name, grid, args, in_specs, outs, out_specs, scratch=(), flops=0, traffic=0, aliases={}):
    return pl.pallas_call(
        body,
        name=name,
        out_shape=outs,
        grid_spec=pltpu.PrefetchScalarGridSpec(
            num_scalar_prefetch=1,
            grid=grid,
            in_specs=in_specs,
            out_specs=out_specs,
            scratch_shapes=scratch,
        ),
        input_output_aliases=aliases,
        cost_estimate=pl.CostEstimate(flops=flops, bytes_accessed=traffic, transcendentals=0),
        compiler_params=pltpu.CompilerParams(
            vmem_limit_bytes=VMEM_LIMIT, dimension_semantics=("arbitrary",)
        ),
    )(*args)


def swap(value, bit, size):
    return lax.ppermute(value, "dp", [(i, i ^ bit) for i in range(size)])


def sum_over_dp(kept, sent, size):
    me = lax.axis_index("dp")
    core, bit1, rest = me & 1, (me >> 1) & 1, me >> 2
    groups = size // 4
    total = kept.astype(F32) + swap(sent, 1, size).astype(F32)
    mine = jnp.where(bit1 == 0, total[0], total[1])
    other = jnp.where(bit1 == 0, total[1], total[0]).astype(BF16)
    total = mine + swap(other, 2, size).astype(F32)
    rows, width = total.shape
    pieces = total.astype(BF16).reshape(groups, rows // groups, width)
    if groups <= 4:
        arrived = [
            swap(lax.dynamic_index_in_dim(pieces, rest ^ k, keepdims=False), 4 * k, size)
            for k in range(1, groups)
        ]
        piece = lax.dynamic_index_in_dim(
            total.reshape(groups, rows // groups, width), rest, keepdims=False
        )
        for other in arrived:
            piece = piece + other.astype(F32)
        piece = piece.astype(BF16)
        whole = jnp.zeros((groups, rows // groups, width), BF16)
        whole = lax.dynamic_update_index_in_dim(whole, piece, rest, 0)
        for k in range(1, groups):
            whole = lax.dynamic_update_index_in_dim(whole, swap(piece, 4 * k, size), rest ^ k, 0)
    else:
        teams = [[4 * r + low for r in range(groups)] for low in range(4)]
        arrived = lax.all_to_all(pieces, "dp", 0, 0, axis_index_groups=teams)
        piece = jnp.sum(arrived.astype(F32), axis=0).astype(BF16)
        whole = lax.all_gather(piece, "dp", axis_index_groups=teams)
    part = whole.reshape(rows, width)
    far = swap(part, 2, size)
    both = jnp.where(bit1 == 0, jnp.stack([part, far]), jnp.stack([far, part]))
    far = swap(both, 1, size)
    return jnp.where(core == 0, jnp.stack([both, far]), jnp.stack([far, both]))


def channel_kernel(
    sub, second_hbm, grad_hbm, win_hbm, wout_hbm, bias,
    branch_hbm, second_grad_hbm, dw_hbm, bias_grad,
    s_all, g_all, acts, grads, w_own, w_far, bias_far, dw, traded, starts, hops,
    load_sem, out_sem, bias_sem, far_sem, core_sem, result_sem, ring_send, ring_recv, free_sem,
):
    pairs, _, rows, width = s_all.shape
    units = width
    half = units // 2
    flat = (2 * rows, width)
    packed = (2, rows, width)
    me = lax.axis_index("dp")
    core, y, z = lax.rem(me, 2), lax.rem(lax.div(me, 2), 2), lax.div(me, 4)
    tp = lax.axis_index("tp")
    at = y * 4 + z + y * (3 - 2 * z)

    def device_at(place):
        place = lax.rem(place + RING, RING)
        row = lax.div(place, 4)
        col = lax.rem(place, 4)
        return (col + row * (3 - 2 * col)) * 4 + row * 2 + core

    sibling = me + 1 - 2 * core
    ahead_device, behind_device = device_at(at + 1), device_at(at - 1)

    barrier = pltpu.get_barrier_semaphore()
    for near in ({"dp": sibling}, {"dp": ahead_device}, {"dp": behind_device}, {"tp": 1 - tp}):
        pl.semaphore_signal(barrier, inc=1, device_id=near, device_id_type=pl.DeviceIdType.MESH)

    def remote(src, dst, send, recv, device):
        return pltpu.make_async_remote_copy(
            src_ref=src, dst_ref=dst, send_sem=send, recv_sem=recv, device_id=device,
            device_id_type=pl.DeviceIdType.MESH,
        )

    def weight_loads(chunk):
        cut = pl.ds(chunk * units, units)
        return (
            pltpu.make_async_copy(wout_hbm.at[cut, :], w_own.at[0, chunk], load_sem.at[chunk, 0]),
            pltpu.make_async_copy(win_hbm.at[:, cut], w_own.at[1, chunk], load_sem.at[chunk, 1]),
        )

    row_loads = (
        pltpu.make_async_copy(second_hbm.at[pl.ds(0, pairs)], s_all, load_sem.at[2, 0]),
        pltpu.make_async_copy(grad_hbm.at[pl.ds(0, pairs)], g_all, load_sem.at[2, 1]),
    )
    for load in (*weight_loads(0), *row_loads, *weight_loads(1)):
        load.start()
    bias_grad[...] = jnp.zeros_like(bias_grad)
    pl.semaphore_wait(barrier, 4)

    def far_copy(chunk):
        return remote(
            w_own.at[core, chunk], w_far.at[core, chunk], far_sem.at[0, chunk], far_sem.at[1, chunk], {"tp": 1 - tp}
        )

    def pass_copy(chunk):
        return remote(
            w_far.at[core, chunk], w_far.at[core, chunk], far_sem.at[2, chunk], far_sem.at[3, chunk], {"dp": sibling}
        )

    bias_copy = remote(bias, bias_far, bias_sem.at[0], bias_sem.at[1], {"tp": 1 - tp})
    bias_copy.start()
    for load in weight_loads(0):
        load.wait()
    far_copy(0).start()
    for load in row_loads:
        load.wait()

    def reach(matrix, way):
        return 3 + jnp.where(matrix == way, 1, 0)

    def segment(chunk, matrix, index):
        index = lax.rem(index + 2 * RING, RING)
        return dw.at[chunk, core, pl.ds(pl.multiple_of(matrix * half + index * SEG, SEG), SEG)]

    def sign(way):
        return 1 - 2 * way

    def toward(way):
        return {"dp": jnp.where(way == 0, ahead_device, behind_device)}

    def part_of(ref, chunk, matrix, which):
        return ref.at[chunk, which, pl.ds(pl.multiple_of(matrix * half, half), half)]

    def landing(chunk, matrix):
        return traded.at[chunk, pl.ds(pl.multiple_of(matrix * half, half), half)]

    def core_copy(chunk, matrix):
        return remote(
            part_of(dw, chunk, matrix, 1 - core), landing(chunk, matrix),
            core_sem.at[0, chunk, matrix], core_sem.at[1, chunk, matrix], {"dp": sibling},
        )

    def back_copy(chunk, matrix):
        return remote(
            part_of(dw, chunk, matrix, core), landing(chunk, matrix),
            core_sem.at[2, chunk, matrix], core_sem.at[3, chunk, matrix], {"dp": sibling},
        )

    def result_copies(chunk, matrix):
        return (
            pltpu.make_async_copy(
                part_of(dw, chunk, matrix, core), part_of(dw_hbm, chunk, matrix, core), result_sem.at[0, chunk, matrix]
            ),
            pltpu.make_async_copy(
                landing(chunk, matrix), part_of(dw_hbm, chunk, matrix, 1 - core), result_sem.at[1, chunk, matrix]
            ),
        )

    def hop_copy(chunk, matrix, way, hop, src):
        slot = way * 4 + hop - 1
        return remote(
            src, hops.at[chunk, matrix, slot], ring_send.at[chunk, matrix, slot], ring_recv.at[chunk, matrix, slot], toward(way)
        )

    def hop_arrived(chunk, matrix, way, hop):
        slot = hops.at[chunk, matrix, way * 4 + hop - 1]
        hop_copy(chunk, matrix, way, hop, slot).wait_recv()
        return slot

    def spread_copy(chunk, matrix, way, hop, index):
        slot = 8 + way * 4 + hop - 1
        place = segment(chunk, matrix, index)
        return remote(
            place, place, ring_send.at[chunk, matrix, slot], ring_recv.at[chunk, matrix, slot], toward(way)
        )

    def service(chunk, matrix, turn):
        @pl.when(turn == 0)
        def _():
            core_copy(chunk, matrix).wait()

            @pl.loop(0, RING)
            def _(index):
                mine = segment(chunk, matrix, index)
                theirs = traded.at[chunk, pl.ds(pl.multiple_of(matrix * half + index * SEG, SEG), SEG)]
                mine[...] = (mine[...].astype(F32) + theirs[...].astype(F32)).astype(BF16)

            pl.semaphore_signal(
                free_sem.at[chunk, matrix], inc=1, device_id={"dp": sibling}, device_id_type=pl.DeviceIdType.MESH
            )

            @pl.loop(0, 2)
            def _(way):
                begin = starts.at[chunk, matrix, way]
                begin[...] = segment(chunk, matrix, at + sign(way) * reach(matrix, way))[...]
                hop_copy(chunk, matrix, way, 1, begin).start()

        @pl.when((turn >= 1) & (turn <= 3))
        def _():
            hop = turn + 1

            @pl.loop(0, 2)
            def _(way):
                @pl.when(hop <= reach(matrix, way))
                def _():
                    slot = hop_arrived(chunk, matrix, way, hop - 1)
                    own = segment(chunk, matrix, at + sign(way) * (reach(matrix, way) - hop + 1))
                    slot[...] = (slot[...].astype(F32) + own[...].astype(F32)).astype(BF16)
                    hop_copy(chunk, matrix, way, hop, slot).start()

        @pl.when(turn == 4)
        def _():
            own = segment(chunk, matrix, at)
            total = own[...].astype(F32)
            for way in range(2):
                total = total + hop_arrived(chunk, matrix, way, reach(matrix, way))[...].astype(F32)
            own[...] = total.astype(BF16)
            for way in range(2):
                spread_copy(chunk, matrix, way, 1, at).start()

        @pl.when((turn >= 5) & (turn <= 7))
        def _():
            hop = turn - 3

            @pl.loop(0, 2)
            def _(way):
                @pl.when(hop <= reach(matrix, way))
                def _():
                    index = at - sign(way) * (hop - 1)
                    spread_copy(chunk, matrix, way, hop - 1, index).wait_recv()
                    spread_copy(chunk, matrix, way, hop, index).start()

        @pl.when(turn == 8)
        def _():
            for way in range(2):
                last = reach(matrix, way)
                spread_copy(chunk, matrix, way, last, at - sign(way) * last).wait_recv()
            pl.semaphore_wait(free_sem.at[chunk, matrix], 1)
            back_copy(chunk, matrix).start()

        @pl.when(turn == LAST_TURN)
        def _():
            back_copy(chunk, matrix).wait_recv()
            for result in result_copies(chunk, matrix):
                result.start()

    def serve(*turns):
        @pl.loop(0, 4)
        def _(block):
            turn = sum(jnp.where(block == number, value, 0) for number, value in enumerate(turns))

            @pl.when((turn >= 0) & (turn <= LAST_TURN))
            def _():
                service(lax.div(block, 2), lax.rem(block, 2), turn)

    def rows_of(ref, pair):
        return ref[pair].reshape(flat)

    depth = pairs * 2 * rows
    odd_turns, even_turns = pairs // 2, (pairs - 1) // 2

    @pl.loop(0, 2)
    def _(chunk):
        @pl.when(chunk == 1)
        def _():
            for load in weight_loads(1):
                load.wait()

        @pl.loop(0, pairs)
        def _(pair):
            s, g = rows_of(s_all, pair), rows_of(g_all, pair)

            cuts = groups_of(units)

            def place(cut):
                return pl.ds(pl.multiple_of(chunk * units + cut.start, 128), cut.stop - cut.start)

            def head(cut):
                return (
                    dot(s, w_own[1, chunk, :, cut], 1, 0) + bias[:, place(cut)],
                    dot(g, w_own[0, chunk, cut, :], 1, 1),
                )

            ahead = head(cuts[0])
            for number, cut in enumerate(cuts):
                pre, act_grad = ahead
                if number + 1 < len(cuts):
                    ahead = head(cuts[number + 1])
                act, slope = gelu_parts(pre)
                pre_grad = (act_grad * slope).astype(BF16)
                acts[chunk, pair, :, :, cut] = act.reshape(2, rows, cut.stop - cut.start)
                grads[chunk, pair, :, :, cut] = pre_grad.reshape(2, rows, cut.stop - cut.start)
                bias_grad[:, place(cut)] += row_sums(pre_grad.astype(F32))

            @pl.when((chunk == 1) & (pair > 0))
            def _():
                odd = lax.rem(pair, 2) == 1
                serve(jnp.where(odd, lax.div(pair + 1, 2), -1), jnp.where(odd, -1, lax.div(pair, 2) - 1), -1, -1)

        for matrix in range(2):

            @pl.loop(0, 2)
            def _(part):
                cut = pl.ds(pl.multiple_of(part * half, half), half)
                if matrix == 0:
                    left, right = acts[chunk, :, :, :, cut], g_all[...]
                else:
                    left, right = s_all[:, :, :, cut], grads[chunk]
                grad = dot(left.reshape(depth, half), right.reshape(depth, width), 0, 0)
                dw[chunk, part, matrix * half : (matrix + 1) * half] = grad.astype(BF16)

                @pl.when(chunk == 1)
                def _():
                    serve(
                        jnp.where(part == 1, odd_turns + 1 + matrix, -1), jnp.where(part == 0, even_turns + matrix, -1), -1, -1
                    )

            core_copy(chunk, matrix).start()
            if matrix == 0:

                @pl.when(chunk == 1)
                def _():
                    far_copy(0).wait_recv()
                    pass_copy(0).start()
                    far_copy(1).start()

        serve(jnp.where(chunk == 0, 0, -1), -1, jnp.where(chunk == 0, -1, 0), -1)

    bias_copy.wait()

    def out_copies(pair):
        return (
            pltpu.make_async_copy(acts.at[0, pair], branch_hbm.at[pair], out_sem.at[0, pair]),
            pltpu.make_async_copy(grads.at[0, pair], second_grad_hbm.at[pair], out_sem.at[1, pair]),
        )

    @pl.loop(0, 2)
    def _(chunk):
        pass_copy(chunk).wait_recv()

        @pl.loop(0, pairs)
        def _(pair):
            done = chunk * pairs + pair

            @pl.when(chunk == 0)
            def _():
                out = sum(dot(rows_of(acts.at[own], pair), w_own[0, own], 1, 0) for own in range(2))
                grad_out = sum(dot(rows_of(grads.at[own], pair), w_own[1, own], 1, 1) for own in range(2))
                acts[0, pair] = out.reshape(packed).astype(BF16)
                grads[0, pair] = grad_out.reshape(packed).astype(BF16)

                @pl.when(pair == pairs - 1)
                def _():
                    far_copy(1).wait_recv()
                    pass_copy(1).start()

            serve(odd_turns + 3 + done, -1, 1 + done, -1)
            out, grad_out = far_units(
                sub, rows_of(s_all, pair), rows_of(g_all, pair), w_far.at[1, chunk],
                bias_far.at[:, pl.ds(pl.multiple_of(chunk * units, units), units)], w_far.at[0, chunk],
                rows_of(acts.at[0], pair).astype(F32), rows_of(grads.at[0], pair).astype(F32),
            )
            acts[0, pair] = out.reshape(packed).astype(BF16)
            grads[0, pair] = grad_out.reshape(packed).astype(BF16)

            @pl.when(chunk == 1)
            def _():
                for copy in out_copies(pair):
                    copy.start()

            serve(-1, even_turns + 2 + done, -1, done)

    @pl.loop(0, 2)
    def _(chunk):
        far_copy(chunk).wait_send()
        pass_copy(chunk).wait_send()

        @pl.loop(0, 2)
        def _(matrix):
            back_copy(chunk, matrix).wait_send()
            for result in result_copies(chunk, matrix):
                result.wait()

            @pl.loop(0, 2)
            def _(way):
                @pl.loop(1, reach(matrix, way) + 1)
                def _(hop):
                    hop_copy(chunk, matrix, way, hop, hops.at[chunk, matrix, way * 4 + hop - 1]).wait_send()
                    spread_copy(chunk, matrix, way, hop, at).wait_send()

    @pl.loop(0, pairs)
    def _(pair):
        for copy in out_copies(pair):
            copy.wait()


def channel_call(pairs, collective_id, second, out_grad, channel_in, bias_row, channel_out):
    batch, rows, width = second.shape
    own = channel_in.shape[1]
    units = own // 2
    half = units // 2
    shape = jax.ShapeDtypeStruct
    slots = (batch // 2, 2, rows, width)
    anywhere = pl.BlockSpec(memory_space=pl.ANY)
    vmem = pl.BlockSpec(memory_space=pltpu.VMEM)
    dma = pltpu.SemaphoreType.DMA
    held = (pairs, 2, rows, width)
    branch, second_grad, dw, bias_grad = pl.pallas_call(
        functools.partial(channel_kernel, 256),
        name=f"channel_{pairs}",
        out_shape=[
            shape(slots, BF16), shape(slots, BF16), shape((2, 2, 2 * half, width), BF16), shape((8, own), F32),
        ],
        in_specs=[anywhere] * 4 + [vmem],
        out_specs=[anywhere] * 3 + [vmem],
        scratch_shapes=[
            pltpu.VMEM(held, BF16), pltpu.VMEM(held, BF16),
            pltpu.VMEM((2,) + held, BF16), pltpu.VMEM((2,) + held, BF16),
            pltpu.VMEM((2, 2, units, width), BF16), pltpu.VMEM((2, 2, units, width), BF16),
            pltpu.VMEM((1, own), F32),
            pltpu.VMEM((2, 2, 2 * half, width), BF16), pltpu.VMEM((2, 2 * half, width), BF16),
            pltpu.VMEM((2, 2, 2, SEG, width), BF16), pltpu.VMEM((2, 2, 8, SEG, width), BF16),
            dma((3, 2)), dma((2, pairs)), dma((2,)), dma((4, 2)), dma((4, 2, 2)),
            dma((2, 2, 2)), dma((2, 2, 16)), dma((2, 2, 16)), pltpu.SemaphoreType.REGULAR((2, 2)),
        ],
        cost_estimate=pl.CostEstimate(
            flops=40 * pairs * rows * width * units, bytes_accessed=40 << 20, transcendentals=0
        ),
        compiler_params=pltpu.CompilerParams(
            vmem_limit_bytes=CHANNEL_VMEM, collective_id=collective_id, has_side_effects=True
        ),
    )(second.reshape(slots), out_grad.reshape(slots), channel_in, channel_out, bias_row)
    packed = (batch, rows, width)
    return branch.reshape(packed), second_grad.reshape(packed), dw.reshape(2, 2, 2, half, width), bias_grad


def channel_general(size, meta, core, second, out_grad, channel_in, bias_row, channel_out):
    batch, rows, width = second.shape
    own = channel_in.shape[1]
    units = own // 2
    pairs = batch // 2
    packed = (batch, rows, width)
    shape = jax.ShapeDtypeStruct
    pair = pair_spec(rows, width)

    tp_swap = [(0, 1), (1, 0)]
    far_bias = lax.ppermute(bias_row, "tp", tp_swap)
    far = []
    for index in range(2):
        cut = slice(index * units, (index + 1) * units)
        out_cut, in_cut = channel_out[cut, :], channel_in[:, cut]
        got = lax.ppermute(jnp.where(core == 0, out_cut, in_cut), "tp", tp_swap)
        traded = swap(got, 1, size)
        far.append((jnp.where(core == 0, traded, got), jnp.where(core == 0, got, traded)))

    hidden = []
    for index in range(2):
        hidden.append(call(
            functools.partial(hidden_kernel, 256), "hidden_own", (pairs,),
            (meta, second, out_grad, channel_in, bias_row, channel_out),
            [
                pair, pair,
                pl.BlockSpec((width, units), lambda j, meta, index=index: (0, index)),
                pl.BlockSpec((1, units), lambda j, meta, index=index: (0, index)),
                pl.BlockSpec((units, width), lambda j, meta, index=index: (index, 0)),
            ],
            [shape((batch, rows, units), BF16)] * 2 + [shape((2, width // 2, width), BF16)] * 2 + [shape((8, units), F32)],
            [pair_spec(rows, units)] * 2
            + [pl.BlockSpec((2, width // 2, width), lambda j, meta: (0, 0, 0))] * 2
            + [pl.BlockSpec((8, units), lambda j, meta: (0, 0))],
            [pltpu.VMEM((units, width), F32), pltpu.VMEM((width, units), F32)],
            flops=8 * batch * rows * width * units, traffic=8 * batch * rows * width,
        ))
    dw = jnp.stack([sum_over_dp(h[3], h[2], size) for h in hidden])
    mats = (channel_in, channel_out, far[0][0], far_bias[:, :units], far[0][1])
    parts = call(
        functools.partial(far_first_kernel, 256), "far_first", (pairs,),
        (meta, second, out_grad, hidden[0][0], hidden[0][1], hidden[1][0], hidden[1][1], *mats),
        [pair] * 2 + [pair_spec(rows, units)] * 4 + [whole_spec(m) for m in mats],
        [shape(packed, F32)] * 2, [pair] * 2,
        flops=16 * batch * rows * width * units, traffic=20 * batch * rows * width,
    )
    mats = (far[1][0], far_bias[:, units:], far[1][1])
    branch, second_grad = call(
        functools.partial(far_last_kernel, 256), "far_last", (pairs,),
        (meta, second, out_grad, *parts, *mats),
        [pair] * 4 + [whole_spec(m) for m in mats],
        [shape(packed, BF16)] * 2, [pair] * 2,
        flops=8 * batch * rows * width * units, traffic=20 * batch * rows * width,
    )
    return branch, second_grad, dw, jnp.concatenate([h[4] for h in hidden], axis=1)


def shards(
    size,
    images, cotangent, image_counts, skip_mask, first_gain, first_bias, token_in, token_in_bias,
    token_out, token_out_bias, second_gain, second_bias, channel_in, channel_in_bias, channel_out,
    channel_out_bias,
):
    batch, patches, width = images.shape
    tokens = token_in.shape[1]
    own = channel_in.shape[1]
    rows = -(-patches // 16) * 16
    units = own // 2
    half = units // 2
    pairs = batch // 2
    core = lax.axis_index("dp") & 1
    shape = jax.ShapeDtypeStruct
    packed = (batch, rows, width)
    block = patches * width
    anywhere = pl.BlockSpec(memory_space=pl.ANY)
    vmem = pl.BlockSpec(memory_space=pltpu.VMEM)
    smem = pl.BlockSpec(memory_space=pltpu.SMEM)
    dma = pltpu.SemaphoreType.DMA
    images_t, cotangent_t = jnp.transpose(images, (1, 0, 2)), jnp.transpose(cotangent, (1, 0, 2))
    split = pltpu.VMEM((width // 128, patches * batch, 128), F32)

    def row(vector):
        return jnp.pad(vector, (0, width - vector.shape[0]))

    vectors = jnp.stack([
        row(v) for v in (first_gain, first_bias, second_gain, second_bias, channel_out_bias, token_in_bias, token_out_bias)
    ])
    bias_row = channel_in_bias.reshape(1, own)

    moved = (MOVE, rows, width)
    meta, most, sent_images, sent_cotangents = pl.pallas_call(
        share_kernel,
        name="share",
        out_shape=[
            shape((VALID + batch,), jnp.int32), shape((1,), jnp.int32), shape(moved, BF16), shape(moved, BF16),
        ],
        in_specs=[smem, smem, anywhere, anywhere],
        out_specs=[smem, smem, vmem, vmem],
        scratch_shapes=[
            pltpu.VMEM((patches, batch, width), BF16), pltpu.VMEM((patches, batch, width), BF16), split, split,
            pltpu.VMEM((8, 128), jnp.int32), pltpu.VMEM((size, 8, 128), jnp.int32),
            pltpu.SMEM((size, 128), jnp.int32), dma((size,)), dma((size,)), dma, dma((2,)),
        ],
        compiler_params=pltpu.CompilerParams(
            vmem_limit_bytes=VMEM_LIMIT, collective_id=SHARE_ID, has_side_effects=True
        ),
    )(image_counts, skip_mask, images_t, cotangent_t)
    got_images, got_cotangents = swap(sent_images, 1, size), swap(sent_cotangents, 1, size)

    whole_one = lambda array: pl.BlockSpec(array.shape, lambda j, meta: (0,) * array.ndim, pipeline_mode=pl.Buffered(1))
    any_pair = pl.BlockSpec((2, rows, width), lambda j, meta: (j, 0, 0))
    last_kept = lambda j, meta: jnp.minimum(j, jnp.maximum((meta[KEPT] + 1) // 2 - 1, 0))
    kept_pair = lambda r: pl.BlockSpec((2, r, width), lambda j, meta: (last_kept(j, meta), 0, 0))
    native = shape((patches, batch, width), F32)
    smalls = [
        shape((8, width), F32), shape((rows, tokens), BF16), shape((tokens, rows), BF16), shape((rows, tokens), BF16),
        shape((tokens, rows), BF16), shape((tokens, 1), F32), shape((rows, 1), F32),
    ]
    token_out_t = token_out.T
    (
        second, out_grad, middle, source, out_bias_grad, tin, tin_t, tout_t, tout, tin_bias, tout_bias, activations, input_grad,
    ) = call(
        token_forward_kernel, "token_forward", (pairs,),
        (meta, images_t, cotangent_t, vectors, token_in, token_out_t),
        [whole_one(v) for v in (images_t, cotangent_t, vectors, token_in, token_out_t)],
        [shape(packed, BF16), shape(packed, BF16), shape((batch, patches, width), F32), shape(packed, BF16)] + smalls + [native] * 2,
        [any_pair, any_pair, kept_pair(patches), kept_pair(rows)] + [whole_one(v) for v in smalls] + [anywhere] * 2,
        [
            pltpu.VMEM((width // 128, patches, batch, 128), F32), pltpu.VMEM((width // 128, patches, batch, 128), F32),
            pltpu.VMEM((patches, 128), F32), dma((batch, 2 * (width // 128))),
        ],
        flops=4 * batch * rows * width * tokens * 4, traffic=batch * block * 12,
    )
    second, out_grad, middle, source, out_bias_grad = pl.pallas_call(
        token_received_kernel,
        name="token_received",
        out_shape=[shape(packed, BF16), shape(packed, BF16), shape((batch, patches, width), F32), shape(packed, BF16), shape((8, width), F32)],
        in_specs=[smem] + [vmem] * 8 + [anywhere] * 4,
        out_specs=[anywhere] * 4 + [vmem],
        scratch_shapes=[
            pltpu.VMEM(moved, BF16), pltpu.VMEM(moved, BF16), pltpu.VMEM((MOVE, patches, width), F32), dma((4, MOVE)),
        ],
        input_output_aliases={9: 0, 10: 1, 11: 2, 12: 3},
        compiler_params=pltpu.CompilerParams(vmem_limit_bytes=VMEM_LIMIT),
    )(
        meta, got_images, got_cotangents, vectors, tin_t, tin_bias, tout_t, tout_bias, out_bias_grad,
        second, out_grad, middle, source,
    )

    operands = (second, out_grad, channel_in, bias_row, channel_out)
    general = functools.partial(channel_general, size, meta, core)
    if size == 2 * RING:
        fast = [functools.partial(channel_call, p, i + 1) for i, p in enumerate(FAST_PAIRS)]
        branch_at = sum((most[0] > 2 * p).astype(jnp.int32) for p in FAST_PAIRS[:-1])
        branch, second_grad, dw, in_bias_grad = lax.switch(branch_at, fast, *operands)
    else:
        branch, second_grad, dw, in_bias_grad = general(*operands)

    def item_specs(own_items):
        def index(place):
            def at(j, meta):
                if own_items:
                    return jnp.minimum(2 * j + place, jnp.maximum(meta[KEPT] - 1, 0)), 0, 0
                return jnp.minimum(meta[KEPT] + jnp.minimum(2 * j + place, jnp.maximum(meta[RECEIVED] - 1, 0)), batch - 1), 0, 0
            return at
        return [pl.BlockSpec((1, r, width), index(place)) for r in (rows, rows, patches, rows, rows) for place in range(2)]

    items = [a for a in (source, out_grad, middle, branch, second_grad) for _ in range(2)]
    consts = (vectors, tin, tin_t, tin_bias, tout)
    sums = [
        shape((rows, tokens), F32), shape((rows, tokens), F32), shape((rows, 128), F32),
        shape((4, 8, width), F32),
    ]
    stage = [pltpu.VMEM((2, 2, 2, patches, width), F32), dma((2, 2, 2))]
    returned = shape((patches, MOVE, width), F32)
    back_images, back_grads, *partial = call(
        functools.partial(token_backward_kernel, False), "token_backward_received", (MOVE // 2,),
        (meta, *items, *consts),
        item_specs(False) + [whole_one(c) for c in consts],
        [returned] * 2 + sums, [anywhere] * 2 + [whole_one(v) for v in sums],
        stage, flops=10 * MOVE * rows * width * tokens, traffic=MOVE * block * 24,
    )
    back_images, back_grads = swap(back_images, 1, size), swap(back_grads, 1, size)
    in_rows, out_rows = width // pairs, own // pairs
    in_turns, out_turns = half // in_rows, half // out_rows
    first_alias = 1 + len(items) + len(consts) + len(sums) + 3
    activations, input_grad, *partial, in_grad_sum, out_grad_sum = call(
        functools.partial(token_backward_kernel, True), "token_backward", (pairs,),
        (meta, *items, *consts, *partial, dw, dw, dw, activations, input_grad),
        item_specs(True) + [whole_one(c) for c in consts] + [whole_one(v) for v in sums]
        + [
            pl.BlockSpec((1, 1, 1, in_rows, width), lambda t, meta, c=c: (c, t // in_turns, 1, t % in_turns, 0))
            for c in range(2)
        ]
        + [pl.BlockSpec(
            (1, 1, 1, out_rows, width),
            lambda t, meta: (t // (2 * out_turns), (t // out_turns) % 2, 0, t % out_turns, 0),
        )]
        + [anywhere] * 2,
        [native] * 2 + sums + [shape((width, own), F32), shape((own, width), F32)],
        [anywhere] * 2 + [whole_one(v) for v in sums]
        + [pl.BlockSpec((in_rows, own), lambda t, meta: (t, 0)), pl.BlockSpec((out_rows, width), lambda t, meta: (t, 0))],
        stage, flops=10 * batch * rows * width * tokens, traffic=batch * block * 24,
        aliases={first_alias: 0, first_alias + 1: 1},
    )
    tin_grad, tout_grad, tout_bias_grad, gains = partial
    if size == 2 * RING:
        summed = pl.pallas_call(
            small_sum_kernel,
            name="small_sum",
            out_shape=shape((PACKED, width), F32),
            in_specs=[vmem] * 6,
            out_specs=vmem,
            scratch_shapes=[
                pltpu.VMEM((2, PACKED // 2, width), F32), pltpu.VMEM((PACKED // 2, width), F32),
                pltpu.VMEM((PACKED // 2, width), BF16), pltpu.VMEM((PACKED // 2, width), BF16),
                pltpu.VMEM((PACKED // 2, width), BF16), pltpu.VMEM((RING, PACKED // 2 // RING, width), BF16),
                dma((4,)), dma((RING,)), dma((RING,)), dma((RING,)), dma((RING,)),
            ],
            compiler_params=pltpu.CompilerParams(
                vmem_limit_bytes=VMEM_LIMIT, collective_id=SUM_ID, has_side_effects=True
            ),
        )(tin_grad, tout_grad, tout_bias_grad, gains, in_bias_grad, out_bias_grad)
    else:
        summed = lax.psum(pack_small(
            tin_grad, tout_grad, tout_bias_grad, gains, in_bias_grad, out_bias_grad
        ), "dp")
    lines = [tokens, patches, width, width, width, width, own, width]
    activations, input_grad, tin_sum, tout_sum, *vectors_sum = pl.pallas_call(
        place_kernel,
        name="place",
        out_shape=[native] * 2 + [shape((patches, tokens), F32)] * 2 + [shape((-(-n // 128), 128), F32) for n in lines],
        in_specs=[smem] + [anywhere] * 4 + [vmem],
        out_specs=[anywhere] * 2 + [vmem] * 10,
        scratch_shapes=[pltpu.VMEM((2, MOVE, patches, width), F32), dma((2, 2, MOVE))],
        input_output_aliases={3: 0, 4: 1},
        compiler_params=pltpu.CompilerParams(vmem_limit_bytes=VMEM_LIMIT),
    )(meta, back_images, back_grads, activations, input_grad, summed)
    activations, input_grad = jnp.transpose(activations, (1, 0, 2)), jnp.transpose(input_grad, (1, 0, 2))
    tin_b, tout_b, gain1, shift1, gain2, shift2, in_b, out_b = [v.reshape(-1)[:n] for v, n in zip(vectors_sum, lines)]
    small = (gain1, shift1, tin_sum, tin_b, tout_sum.T, tout_b, gain2, shift2, in_b, out_b)
    return (activations, input_grad, *small[:8], in_grad_sum, small[8], out_grad_sum, small[9])


def solution(mesh):
    placed = (
        P("dp", None, None), P("dp", None, None), P("dp"), P("dp"), P(), P(), P(), P(), P(), P(), P(), P(),
        P(None, "tp"), P("tp"), P("tp", None), P(),
    )
    return jax.shard_map(
        functools.partial(shards, mesh.shape["dp"]),
        mesh=mesh,
        in_specs=placed,
        out_specs=(
            P("dp", None, None), P("dp", None, None), P(), P(), P(), P(), P(), P(), P(), P(),
            P(None, "tp"), P("tp"), P("tp", None), P(),
        ),
        check_vma=False,
    )
```
